32 devices in a mesh: grp: 4 (over x, core), dev: 8 (over z, y).
Axes of the slice: x: 2, y: 2, z: 4, core: 2. Of those that a mesh axis runs over, the one named last changes fastest.
Arguments:
- features: bfloat16 [4, 64, 32, 128], P('grp', None, 'dev'), may hold values from -6 to 6
- coarse_flow: bfloat16 [4, 4, 32, 128], P('grp', None, 'dev'), may hold values from -6 to 6
- target: bfloat16 [4, 2, 32, 128], P('grp', None, 'dev'), may hold values from -9 to 9
- valid_mask: int32 [4, 32, 128], P('grp', 'dev'), may hold values from 0 to 1, as said below
- weights: float32 [2306048], P('dev'), may hold values from -1 to 1, as said below
- momentum: float32 [2306048], P('dev'), may hold values from -39 to 39, as said below
- average: float32 [2306048], P('dev'), may hold values from -1 to 1, as said below
Outputs:
- flow: float32 [4, 2, 32, 128], P('grp', None, None, 'dev')
- feature_grad: float32 [4, 64, 32, 128], P('grp', None, 'dev')
- coarse_grad: float32 [4, 4, 32, 128], P('grp', None, 'dev')
- new_weights: float32 [2306048], P('dev')
- new_momentum: float32 [2306048], P('dev')
- new_average: float32 [2306048], P('dev')
- weights_bf16: bfloat16 [2306048], P('dev')
The draws below stay inside these ranges and needn't reach their ends.
Inputs may be any that keep to these rules, and one draw needn't show every extreme that they name: `valid_mask`: 1 marks a pixel whose ground truth counts in the loss. `weights`: entries after 2304830 are zero. `momentum`: entries after 2304830 are zero. `average`: entries after 2304830 are zero.
All inputs are finite; a program needn't handle non-finite values.
Results may differ from the reference program's by a relative error of at most 0.013.
Values may be sent and summed in bfloat16 or wider, within the bound.
No kernel may reach another device: no remote copies, remote signals or barrier semaphores. Data moves between devices by JAX's collectives and lax.ppermute only.
A program may use at most 320 MiB of HBM per device.

```python
import jax
import jax.numpy as jnp
import numpy as np
from jax import lax

FC = 32
SR = 4
D1 = 128
D2 = 128
D3 = 96
D4 = 64
D5 = 32
X1 = 128
X2 = 128
X3 = 128
X4 = 96
X5 = 64
X6 = 32
P_PAD = 2306048
MARGIN = 8
TH = 32
TW = 16
PAIRS = 4
WIDTH = 128
PIXELS = 16384
N_DEV = 8


DILATIONS = (1, 2, 4, 8, 16, 1, 1)


def layer_table_drawn():
    layers = []
    channels = (2 * SR + 1) ** 2 + FC + 4
    for outgoing in (D1, D2, D3, D4, D5):
        layers.append((channels, outgoing, 1))
        channels = channels + outgoing
    layers.append((channels, 2, 1))
    for outgoing, dilation in zip((X1, X2, X3, X4, X5, X6, 2), DILATIONS):
        layers.append((channels, outgoing, dilation))
        channels = outgoing
    return layers


def entry_scales(kernel_scale, bias_scale, exponent):
    pieces = []
    for incoming, outgoing, dilation in layer_table_drawn():
        pieces.append(np.full(incoming * outgoing * 9, kernel_scale * (9.0 * incoming) ** (0.0 - exponent), np.float32))
        pieces.append(np.full(outgoing, bias_scale, np.float32))
    filled = np.concatenate(pieces)
    return jnp.asarray(np.concatenate([filled, np.zeros(P_PAD - filled.shape[0], np.float32)]))


def draw_weights(key, part):
    key = jax.random.fold_in(key, 1)
    standard = jnp.clip(jax.random.normal(key, (P_PAD,), jnp.float32), -5.0, 5.0)
    return standard * entry_scales(1.5, 0.2, 0.5)


def draw_momentum(key, part):
    key = jax.random.fold_in(key, 2)
    grad_size = 0.02 * PIXELS ** 0.5
    standard = jnp.clip(jax.random.normal(key, (P_PAD,), jnp.float32), -5.0, 5.0)
    return standard * entry_scales(grad_size, 3.0 * grad_size, 0.0)


def draw_average(key, part):
    key = jax.random.fold_in(key, 3)
    standard = jnp.clip(jax.random.normal(key, (P_PAD,), jnp.float32), -5.0, 5.0)
    return standard * entry_scales(1.5, 0.2, 0.5)


def draw_valid_mask(key, part):
    key = jax.random.fold_in(key, 4)
    levels = jax.random.randint(key, (PAIRS, TH, WIDTH), 0, 1000, dtype=jnp.int32)
    pair_at = jnp.arange(PAIRS, dtype=jnp.int32)[:, None, None]
    row_at = jnp.arange(TH, dtype=jnp.int32)[None, :, None]
    bound_at = 200 + 150 * pair_at // (PAIRS - 1) + 150 * row_at // (TH - 1)
    return (levels < bound_at).astype(jnp.int32)


def block_levels(own_key, extent, cuts, smallest, high):
    def one(axis_at, blocks):
        draws = jax.random.uniform(jax.random.fold_in(jax.random.fold_in(own_key, 6), axis_at), (blocks,), jnp.float32, smallest / len(cuts), high / len(cuts))
        return jnp.repeat(jnp.exp(draws), extent[axis_at] // blocks).reshape((-1,) + (1,) * (len(extent) - axis_at - 1))

    level = one(*cuts[0])
    for cut in cuts[1:]:
        level = level * one(*cut)
    return level


def centred(stream_key, dims, spread, bound, cuts=(), kind=jnp.bfloat16):
    gain = block_levels(stream_key, dims, cuts, -0.22, 0.18) if cuts else 1.0
    entries = jax.random.normal(stream_key, dims, jnp.float32) * spread * gain
    return jnp.minimum(jnp.maximum(entries, -bound), bound).astype(kind)


def setup_inputs(seed: int = 0) -> dict:
    keys = jax.random.split(jax.random.key(seed), 8)
    features = centred(keys[0], (PAIRS, 2 * FC, TH, WIDTH), 1.0, 6.0, ((0, 4), (2, 8)))
    coarse_flow = centred(keys[1], (PAIRS, 4, TH, WIDTH), 1.0, 6.0, ((0, 4), (2, 8)))
    target = centred(keys[2], (PAIRS, 2, TH, WIDTH), 1.5, 9.0, ((0, 4), (2, 8)))
    valid_mask = draw_valid_mask(jax.random.fold_in(keys[7], 71), 0)
    weights = draw_weights(jax.random.fold_in(keys[7], 71), 0)
    momentum = draw_momentum(jax.random.fold_in(keys[7], 71), 0)
    average = draw_average(jax.random.fold_in(keys[7], 71), 0)
    return {"features": features, "coarse_flow": coarse_flow, "target": target, "valid_mask": valid_mask, "weights": weights, "momentum": momentum, "average": average}


@jax.custom_vjp
def low(v):
    return lax.optimization_barrier(v.astype(jnp.bfloat16)).astype(jnp.float32)

@jax.custom_vjp
def low_back(v):
    return v

def low_keep(v):
    return (low(v), None)

def low_pass(kept, grad):
    return (grad,)

def back_keep(v):
    return (v, None)

def back_low(kept, grad):
    return (low(grad),)
low.defvjp(low_keep, low_pass)
low_back.defvjp(back_keep, back_low)
SLOPE = 0.1
EPE_EPS = 0.01
MOMENTUM_RATE = 0.5
AVERAGE_DECAY = 0.5
LEARN_RATE = 0.001
DECAY_RATE = 0.0001
DILATIONS = (1, 2, 4, 8, 16, 1, 1)

def layer_table():
    layers = []
    channels = (2 * SR + 1) ** 2 + FC + 4
    for outgoing in (D1, D2, D3, D4, D5):
        layers.append((channels, outgoing, 1))
        channels = channels + outgoing
    layers.append((channels, 2, 1))
    for outgoing, dilation in zip((X1, X2, X3, X4, X5, X6, 2), DILATIONS):
        layers.append((channels, outgoing, dilation))
        channels = outgoing
    return layers

def unpack(flat_values):
    pieces = []
    offset = 0
    for incoming, outgoing, dilation in layer_table():
        kernel_count = incoming * outgoing * 9
        kernel = flat_values[offset:offset + kernel_count].reshape(outgoing, incoming, 3, 3)
        offset = offset + kernel_count
        biases = flat_values[offset:offset + outgoing]
        offset = offset + outgoing
        pieces.append((kernel, biases, dilation))
    return pieces

def leaky(values):
    return SLOPE * values + (1.0 - SLOPE) * jax.nn.silu(values)

def convolve(activations, kernel, biases, dilation):
    result = lax.conv_general_dilated(activations, kernel, (1, 1), ((dilation, dilation), (dilation, dilation)), rhs_dilation=(dilation, dilation), dimension_numbers=('NCHW', 'OIHW', 'NCHW'), precision=lax.Precision.HIGHEST)
    return result + biases[None, :, None, None]

def correlate(first_map, second_map):
    padded = jnp.pad(second_map, ((0, 0), (0, 0), (SR, SR), (SR, SR)))
    height = first_map.shape[2]
    breadth = first_map.shape[3]
    volume = []
    for row_shift in range(2 * SR + 1):
        for col_shift in range(2 * SR + 1):
            window = padded[:, :, row_shift:row_shift + height, col_shift:col_shift + breadth]
            volume.append(lax.optimization_barrier(jnp.mean(first_map * window, axis=1)))
    return jnp.stack(volume, axis=1)

def network(patches, layers):
    first_map = patches[:, :FC]
    second_map = patches[:, FC:2 * FC]
    coarse_map = patches[:, 2 * FC:]
    volume = low(leaky(correlate(first_map, second_map)))
    stacked = jnp.concatenate([volume, first_map, coarse_map], axis=1)
    for kernel, biases, dilation in layers[:5]:
        fresh_out = low(leaky(low_back(convolve(stacked, kernel, biases, dilation))))
        stacked = jnp.concatenate([fresh_out, stacked], axis=1)
    kernel, biases, dilation = layers[5]
    estimate = low_back(convolve(stacked, kernel, biases, dilation))
    current = stacked
    for kernel, biases, dilation in layers[6:12]:
        current = low(leaky(low_back(convolve(current, kernel, biases, dilation))))
    kernel, biases, dilation = layers[12]
    return estimate + low_back(convolve(current, kernel, biases, dilation))

def pair_loss(feature_values, coarse_values, target_values, valid_values, layers, weighting):
    picture = jnp.concatenate([feature_values, coarse_values], axis=0)
    padded = jnp.pad(picture, ((0, 0), (MARGIN, MARGIN), (MARGIN, MARGIN)))
    columns = jnp.arange(N_DEV, dtype=jnp.int32)[:, None] * TW + jnp.arange(TW + 2 * MARGIN, dtype=jnp.int32)[None, :]
    patches = jnp.transpose(padded[:, :, columns], (2, 0, 1, 3))
    motion = network(patches, layers)
    interior = motion[:, :, MARGIN:MARGIN + TH, MARGIN:MARGIN + TW]
    placed = jnp.transpose(interior, (1, 2, 0, 3)).reshape(2, TH, N_DEV * TW)
    mismatch = placed - target_values
    length = jnp.sqrt(lax.optimization_barrier(jnp.sum(mismatch * mismatch, axis=0)) + EPE_EPS)
    return (weighting * jnp.sum(valid_values * length), placed)

def update(weights, momentum, average, gradient):
    gradient = gradient + DECAY_RATE * weights
    renewed = MOMENTUM_RATE * momentum + gradient
    stepped = weights - LEARN_RATE * (gradient + MOMENTUM_RATE * renewed)
    return (stepped, renewed, AVERAGE_DECAY * average + (1.0 - AVERAGE_DECAY) * stepped)

def reference(features, coarse_flow, target, valid_mask, weights, momentum, average):
    counted = jnp.sum(valid_mask.astype(jnp.float32))
    weighting = valid_mask.shape[0] * valid_mask.shape[1] * valid_mask.shape[2] / counted
    target_values = target.astype(jnp.float32)
    valid_values = valid_mask.astype(jnp.float32)

    def objective(feature_values, coarse_values, weight_values):
        layers = unpack(low(weight_values))

        def per_pair(members):
            return pair_loss(members[0], members[1], members[2], members[3], layers, weighting)
        losses, motions = lax.map(jax.checkpoint(per_pair), (feature_values, coarse_values, target_values, valid_values))
        return (jnp.sum(losses), motions)
    loss_sum, pullback, motions = jax.vjp(objective, features.astype(jnp.float32), coarse_flow.astype(jnp.float32), weights, has_aux=True)
    feature_grad, coarse_grad, weight_grad = pullback(jnp.ones_like(loss_sum))
    new_weights, new_momentum, new_average = update(weights, momentum, average, weight_grad)
    return (motions, feature_grad, coarse_grad, new_weights, new_momentum, new_average, new_weights.astype(jnp.bfloat16))
```

```python
import jax
import jax.numpy as jnp
from jax import lax
from jax.experimental import pallas as pl
from jax.experimental.pallas import tpu as pltpu
from jax.sharding import PartitionSpec as P

FC = 32
SR = 4
EXT = 2 * SR + 1
NCOST = EXT * EXT
NS0 = NCOST + FC + 4
DENSE = (128, 128, 96, 64, 32)
CONTEXT = (128, 128, 128, 96, 64, 32, 2)
DILATIONS = (1, 2, 4, 8, 16, 1, 1)
MARGIN = 8

SLOPE = 0.1
EPE_EPS = 0.01
MOMENTUM_RATE = 0.5
AVERAGE_DECAY = 0.5
LEARN_RATE = 0.001
DECAY_RATE = 0.0001

LANES = 128
PH = 48
PW = 32
PX = PH * PW
RIM = 16 * PW
STRIP = 128
MT = 512
PITCH = 40
F32 = jnp.float32
BF16 = jnp.bfloat16
NT = (((1,), (1,)), ((), ()))
TN = (((0,), (0,)), ((), ()))


def layer_table():
    places = [(NS0, 0, 0), (128, 1, 0), (128, 2, 0), (96, 3, 0), (64, 4, 0), (32, 3, 96)]
    layers = []
    offset = 0

    def add(pieces, outgoing, dilation, shift):
        nonlocal offset
        incoming = sum(n for n, _, _ in pieces)
        row = 9 * incoming
        segments = []
        at = 0
        for n, block, lane in pieces:
            segments.append((n, block, lane, offset + 9 * at))
            at += n
        layers.append(
            dict(
                out=outgoing,
                row=row,
                dil=dilation,
                shift=shift,
                segments=segments,
                blocks=1 + max(b for _, b, _ in pieces),
                bias=offset + row * outgoing,
                rows=LANES if outgoing == 2 else 9 * LANES,
            )
        )
        offset += row * outgoing + outgoing

    for i, outgoing in enumerate(DENSE):
        add(places[i::-1], outgoing, 1, 96 if i == 4 else 0)
    add(places[::-1], 2, 1, 0)
    add(places[::-1], CONTEXT[0], DILATIONS[0], 0)
    for i in range(1, 7):
        add([(CONTEXT[i - 1], 0, 0)], CONTEXT[i], DILATIONS[i], 0)
    return layers, offset


LAYERS, COUNT = layer_table()


def group_rows():
    at = 0
    groups = []
    for index, layer in enumerate(LAYERS):
        own = []
        for segment in layer["segments"]:
            own.append((at, segment))
            at += -(-layer["out"] // 16) * 16
        groups.append(own)
    return groups, -(-at // 64) * 64


GROUPS, GROUP_ROWS = group_rows()
TILES = 4


def iota(shape, dim):
    return lax.broadcasted_iota(jnp.int32, shape, dim)


def rows_at(start, size, step=8):
    return pl.ds(pl.multiple_of(start, step), size)


def sigmoid(v):
    return 0.5 * jnp.tanh(0.5 * v) + 0.5


def leaky(v):
    return SLOPE * v + (1.0 - SLOPE) * v * sigmoid(v)


def leaky_slope(v):
    s = sigmoid(v)
    return SLOPE + (1.0 - SLOPE) * (s + v * s * (1.0 - s))


def loop(count, body):
    def step(i, carry):
        body(i)
        return carry

    lax.fori_loop(0, count, step, 0)


def fill_order(order):
    for k in range(9):
        for m in range(9):
            row = iota((LANES, LANES), 0) + m * LANES
            col = iota((LANES, LANES), 1)
            order[m * LANES : (m + 1) * LANES, k * LANES : (k + 1) * LANES] = jnp.where(
                row == 9 * col + k, 1.0, 0.0
            ).astype(BF16)


def unpack_kernel(*refs):
    flat = refs[0]
    outs = refs[1:14]
    bias_out = refs[14]
    whole, slabs, aligned, result, order, heads = refs[15:]
    count = flat.shape[0]
    fill_order(order)

    def widen(i):
        whole[rows_at(i * 32, 32), :] = flat[rows_at(i * 32, 32, 32), :].astype(F32)

    loop(count // 32, widen)
    whole[count : count + 32, :] = jnp.zeros((32, LANES), F32)
    lane = iota((16, LANES), 1)

    def fetch(start, size):
        row = start >> 7
        off = start & 127
        turn = (128 - off) & 127
        here = pltpu.roll(whole[pl.ds(row, size), :], turn, 1)
        after = pltpu.roll(whole[pl.ds(row + 1, size), :], turn, 1)
        return jnp.where(lane[:size] < 128 - off, here, after)

    for index, layer in enumerate(LAYERS):
        outgoing = layer["out"]
        unroll = min(8, outgoing)
        for at, (n, block, place, start) in GROUPS[index]:
            first = start - 9 * place

            def take(i, first=first, unroll=unroll, row=layer["row"]):
                for u in range(unroll):
                    o = i * unroll + u
                    slabs[rows_at(o * 16, 16, 16), :] = fetch(first + o * row, 16)

            loop(outgoing // unroll, take)
            kept = -(-outgoing // 16) * 16
            for r in range(9):
                aligned[at : at + kept, r * LANES : (r + 1) * LANES] = slabs[
                    pl.ds(r, kept, stride=16), :
                ].astype(BF16)
        shift = layer["shift"]
        line = fetch(jnp.int32(layer["bias"] - shift), 8)[:1]
        spot = iota((1, LANES), 1)
        bias_out[index : index + 1, :] = jnp.where(
            (spot >= shift) & (spot < shift + outgoing), line, 0.0
        )
    bias_out[13:16, :] = jnp.zeros((3, LANES), F32)

    size = GROUP_ROWS // TILES

    def multiply(i):
        result[rows_at(i * size, size, 16), :] = jnp.dot(
            aligned[rows_at(i * size, size, 16), :], order[...], preferred_element_type=F32
        )

    loop(TILES, multiply)

    for index, layer in enumerate(LAYERS):
        outgoing = layer["out"]
        shift = layer["shift"]
        out = outs[index]
        if outgoing == 2:
            heads[...] = jnp.zeros_like(heads)
        elif outgoing < LANES:
            out[...] = jnp.zeros_like(out)
        for block in range(layer["blocks"]):
            for k in range(9):
                total = None
                for at, (n, own, place, _) in GROUPS[index]:
                    if own != block:
                        continue
                    tile = result[at : at + outgoing, k * LANES : (k + 1) * LANES]
                    spot = iota((outgoing, LANES), 1)
                    tile = jnp.where((spot >= place) & (spot < place + n), tile, 0.0)
                    total = tile if total is None else total + tile
                columns = slice(block * LANES, (block + 1) * LANES)
                if outgoing == 2:
                    heads[2 * k : 2 * k + 2, columns] = total
                else:
                    out[k * LANES + shift : k * LANES + shift + outgoing, columns] = total.astype(
                        BF16
                    )
        if outgoing == 2:
            out[...] = heads[:, : layer["blocks"] * LANES].astype(BF16)


def unpack(flat):
    count = flat.shape[0]
    shapes = [
        jax.ShapeDtypeStruct((layer["rows"], layer["blocks"] * LANES), BF16) for layer in LAYERS
    ] + [jax.ShapeDtypeStruct((16, LANES), F32)]
    return pl.pallas_call(
        unpack_kernel,
        out_shape=shapes,
        scratch_shapes=[
            pltpu.VMEM((count + 32, LANES), F32),
            pltpu.VMEM((16 * LANES, LANES), F32),
            pltpu.VMEM((GROUP_ROWS, 9 * LANES), BF16),
            pltpu.VMEM((GROUP_ROWS, 9 * LANES), F32),
            pltpu.VMEM((9 * LANES, 9 * LANES), BF16),
            pltpu.VMEM((LANES, 5 * LANES), F32),
        ],
        compiler_params=pltpu.CompilerParams(vmem_limit_bytes=58 * 2**20),
        name="unpack_weights",
    )(flat)


def pack_kernel(*refs):
    grads = refs[:13]
    bias_in = refs[13]
    flat = refs[14]
    whole, slabs, gathered, result, order, heads = refs[15:]
    count = flat.shape[0]
    fill_order(order)
    for index, layer in enumerate(LAYERS):
        outgoing = layer["out"]
        shift = layer["shift"]
        grad = grads[index]
        if outgoing == 2:
            heads[:LANES, : layer["blocks"] * LANES] = grad[...].astype(F32)
            heads[LANES:, :] = jnp.zeros((16, heads.shape[1]), F32)
        for at, (n, block, place, _) in GROUPS[index]:
            columns = slice(block * LANES, (block + 1) * LANES)
            for k in range(9):
                if outgoing == 2:
                    tile = heads[2 * k : 2 * k + 16, columns]
                    if place:
                        tile = pltpu.roll(tile, LANES - place, 1)
                    tile = tile.astype(BF16)
                else:
                    tile = grad[k * LANES + shift : k * LANES + shift + outgoing, columns]
                    if place:
                        tile = pltpu.roll(tile.astype(F32), LANES - place, 1).astype(BF16)
                gathered[at : at + tile.shape[0], k * LANES : (k + 1) * LANES] = tile

    size = GROUP_ROWS // TILES

    def multiply(i):
        result[rows_at(i * size, size, 16), :] = lax.dot_general(
            gathered[rows_at(i * size, size, 16), :], order[...], NT, preferred_element_type=F32
        )

    loop(TILES, multiply)

    lane = iota((8, LANES), 1)
    sub = iota((8, LANES), 0)

    def put(start, here, before, masked):
        row = start >> 7
        off = start & 127
        tile = jnp.where(lane >= off, pltpu.roll(here, off, 1), pltpu.roll(before, off, 1))
        if masked:
            pltpu.store(whole.at[pl.ds(row, 8), :], tile, mask=(sub > 0) | (lane >= off))
        else:
            whole[pl.ds(row + 8, 8), :] = tile

    for index, layer in enumerate(LAYERS):
        outgoing = layer["out"]
        region = outgoing * 16
        for s, (at, (n, _, _, _)) in enumerate(GROUPS[index]):
            for r in range(-(-9 * n // LANES)):
                slabs[pl.ds(s * region + 1 + r, outgoing, stride=16), :] = result[
                    at : at + outgoing, r * LANES : (r + 1) * LANES
                ]
        unroll = 2

        def place_rows(i, layer=layer, region=region, own=GROUPS[index], unroll=unroll):
            for u in range(unroll):
                o = i * unroll + u
                for s, (_, (n, _, _, start)) in enumerate(own):
                    base = s * region + o * 16
                    begin = start + o * layer["row"]
                    put(begin, slabs[pl.ds(base + 1, 8), :], slabs[pl.ds(base, 8), :], True)
                    if 9 * n > 7 * LANES:
                        put(begin, slabs[pl.ds(base + 9, 8), :], slabs[pl.ds(base + 8, 8), :], False)

        loop(outgoing // unroll, place_rows)
        line = bias_in[index : index + 1, :]
        if layer["shift"]:
            line = pltpu.roll(line, LANES - layer["shift"], 1)
        here = jnp.where(sub == 0, line, 0.0)
        before = jnp.where(sub == 1, line, 0.0)
        put(jnp.int32(layer["bias"]), here, before, True)
    end, off = COUNT // LANES, COUNT % LANES
    pltpu.store(
        whole.at[pl.ds(end, 8), :], jnp.zeros((8, LANES), F32), mask=(sub > 0) | (lane >= off)
    )
    left = count - end
    if left > 8:
        whole[end + 8 : count, :] = jnp.zeros((left - 8, LANES), F32)

    def narrow(i):
        flat[rows_at(i * 32, 32, 32), :] = whole[rows_at(i * 32, 32), :].astype(BF16)

    loop(count // 32, narrow)


def pack(grads, bias, count):
    return pl.pallas_call(
        pack_kernel,
        out_shape=jax.ShapeDtypeStruct((count, LANES), BF16),
        scratch_shapes=[
            pltpu.VMEM((count + 32, LANES), F32),
            pltpu.VMEM((6 * 16 * LANES + 16, LANES), F32),
            pltpu.VMEM((GROUP_ROWS, 9 * LANES), BF16),
            pltpu.VMEM((GROUP_ROWS, 9 * LANES), F32),
            pltpu.VMEM((9 * LANES, 9 * LANES), BF16),
            pltpu.VMEM((LANES + 16, 5 * LANES), F32),
        ],
        compiler_params=pltpu.CompilerParams(vmem_limit_bytes=62 * 2**20),
        name="pack_gradients",
    )(*grads, bias)


ROWS4 = 4 * PW
SEC_ROWS = (PH + 2 * SR) * PITCH + LANES


def load_second(joined, second):
    second[...] = jnp.zeros_like(second)
    keep = iota((PW, LANES), 1) < FC
    for y in range(MARGIN, PH - MARGIN):
        row = joined[y * PW : (y + 1) * PW, :].astype(F32)
        row = jnp.where(keep, pltpu.roll(row, LANES - FC, 1), 0.0)
        at = (y + SR) * PITCH + 8
        second[at : at + PW, :] = row


def band_shift(dy, third):
    return EXT * dy - PITCH * third - (8 - SR)


def correlate_kernel(received, stack0, cost, joined, second):
    joined[...] = jnp.zeros_like(joined)
    blocks = received.shape[0]
    for s in range(blocks):
        tile = received[s].astype(F32).T
        joined[RIM // 2 + s * ROWS4 : RIM // 2 + (s + 1) * ROWS4, :] = tile.astype(BF16)
    load_second(joined, second)
    row = iota((ROWS4, ROWS4), 0)
    col = iota((ROWS4, ROWS4), 1)
    flip = jnp.where((row // PW == col // PW) & (row % PW + col % PW == PW - 1), 1.0, 0.0).astype(
        BF16
    )
    lane = iota((ROWS4, LANES), 1)
    narrow = iota((PW, LANES), 1)

    def body(i):
        own = joined[rows_at(i * ROWS4, ROWS4, ROWS4), :]
        first = jnp.where(lane < FC, own.astype(F32), 0.0).astype(BF16)
        first = jnp.dot(flip, first, preferred_element_type=F32).astype(BF16)
        bands = []
        for g in range(4):
            window = second[rows_at((4 * i + 3 * g) * PITCH, LANES), :].astype(BF16)
            bands.append(lax.dot_general(first, window, NT, preferred_element_type=F32))
        pieces = []
        for yy in range(4):
            total = jnp.zeros((PW, LANES), F32)
            turned = [
                pltpu.roll(band[yy * PW : (yy + 1) * PW, :], 0, 1, stride=1, stride_axis=0)
                for band in bands
            ]
            for dy in range(EXT):
                t = yy + dy
                shift = (band_shift(dy, t % 3) - (PW - 1)) % LANES
                band = pltpu.roll(turned[t // 3], shift, 1)
                total = jnp.where((narrow >= EXT * dy) & (narrow < EXT * (dy + 1)), band, total)
            pieces.append(total * (1.0 / FC))
        total = jnp.concatenate(pieces, axis=0)
        high = total.astype(BF16)
        low = (total - high.astype(F32)).astype(BF16)
        total = jnp.dot(flip, high, preferred_element_type=F32) + jnp.dot(
            flip, low, preferred_element_type=F32
        )
        cost[rows_at(i * ROWS4, ROWS4, ROWS4), :] = total
        wide = own.astype(F32)
        filled = jnp.where(lane < NCOST, leaky(total), pltpu.roll(wide, NCOST, 1))
        coarse = pltpu.roll(wide, NCOST + FC - 2 * FC, 1)
        filled = jnp.where(lane >= NCOST + FC, coarse, filled)
        filled = jnp.where(lane < NS0, filled, 0.0)
        stack0[rows_at(i * ROWS4, ROWS4, ROWS4), :] = filled.astype(BF16)

    loop(PH // 4, body)


def correlate(received):
    return pl.pallas_call(
        correlate_kernel,
        out_shape=[
            jax.ShapeDtypeStruct((PX, LANES), BF16),
            jax.ShapeDtypeStruct((PX, LANES), F32),
            jax.ShapeDtypeStruct((PX, LANES), BF16),
        ],
        scratch_shapes=[pltpu.VMEM((SEC_ROWS, LANES), F32)],
        compiler_params=pltpu.CompilerParams(vmem_limit_bytes=32 * 2**20),
        name="correlate",
    )(received)


def correlate_back(joined, cost, dstack, second, dsecond, out):
    load_second(joined, second)
    dsecond[...] = jnp.zeros_like(dsecond)
    lane = iota((ROWS4, LANES), 1)
    narrow = iota((PW, LANES), 1)

    def body(i):
        rows = rows_at(i * ROWS4, ROWS4, ROWS4)
        own = joined[rows, :]
        first = jnp.where(lane < FC, own.astype(F32), 0.0).astype(BF16)
        grad = dstack[rows, :LANES]
        volume = grad * leaky_slope(cost[rows, :]) * (1.0 / FC)
        dfirst = jnp.zeros((ROWS4, LANES), F32)
        for g in range(4):
            pieces = []
            for yy in range(4):
                piece = jnp.zeros((PW, LANES), F32)
                own_rows = volume[yy * PW : (yy + 1) * PW, :]
                for t in range(3 * g, 3 * g + 3):
                    dy = t - yy
                    if dy < 0 or dy >= EXT:
                        continue
                    part = jnp.where(
                        (narrow >= EXT * dy) & (narrow < EXT * (dy + 1)), own_rows, 0.0
                    )
                    shift = (-band_shift(dy, t % 3)) % LANES
                    piece = piece + pltpu.roll(part, shift, 1)
                pieces.append(pltpu.roll(piece, 0, 1, stride=1, stride_axis=0))
            band = jnp.concatenate(pieces, axis=0).astype(BF16)
            at = rows_at((4 * i + 3 * g) * PITCH, LANES)
            dfirst = dfirst + jnp.dot(
                band, second[at, :].astype(BF16), preferred_element_type=F32
            )
            dsecond[at, :] += lax.dot_general(band, first, TN, preferred_element_type=F32)
        direct = pltpu.roll(grad, LANES - NCOST, 1)
        coarse = pltpu.roll(grad, LANES + 2 * FC - NCOST - FC, 1)
        filled = jnp.where(lane < FC, dfirst + direct, 0.0)
        filled = jnp.where((lane >= 2 * FC) & (lane < 2 * FC + 4), coarse, filled)
        dstack[rows, LANES : 2 * LANES] = filled

    loop(PH // 4, body)
    middle = iota((ROWS4, LANES), 1)
    for s in range((PH - 2 * MARGIN) // 4):
        pieces = []
        for yy in range(4):
            at = (MARGIN + 4 * s + yy + SR) * PITCH + 8
            pieces.append(dsecond[at : at + PW, :])
        other = pltpu.roll(jnp.concatenate(pieces, axis=0), FC, 1)
        start = (MARGIN + 4 * s) * PW
        tile = dstack[start : start + ROWS4, LANES : 2 * LANES]
        tile = jnp.where((middle >= FC) & (middle < 2 * FC), other, tile)
        out[s] = tile.T[: out.shape[1]].astype(BF16)


def network_kernel(*refs):
    stack0, cost, joined, weighting = refs[:4]
    kernels = refs[4:17]
    biases = refs[17]
    motion_out = refs[18]
    picture_out = refs[19]
    grads = refs[20:33]
    bias_out = refs[33]
    stack, ctx, pre, taps, moved, dstack, dcur, ghead, partial, second, dsecond = refs[34:]

    taps[:, :RIM, :] = jnp.zeros((9, RIM, LANES), F32)
    taps[:, RIM + PX :, :] = jnp.zeros((9, RIM, LANES), F32)
    moved[:, :RIM, :] = jnp.zeros((3, RIM, LANES), BF16)
    moved[:, RIM + PX :, :] = jnp.zeros((3, RIM, LANES), BF16)
    column = iota((STRIP, LANES), 0) % PW
    lane = iota((STRIP, LANES), 1)

    def strips(body):
        loop(PX // STRIP, lambda i: body(rows_at(i * STRIP, STRIP, STRIP), i * STRIP))

    def inside(tile, shift):
        if shift == 0:
            return tile
        valid = (column + shift >= 0) & (column + shift < PW)
        return jnp.where(valid, pltpu.roll(tile, (-shift) % STRIP, 0), 0.0)

    def multiply(load, kernel):
        def body(i):
            product = lax.dot_general(
                load(rows_at(i * MT, MT, MT)), kernel[...], NT, preferred_element_type=F32
            )
            for k in range(9):
                taps[k, rows_at(RIM + i * MT, MT, MT), :] = product[:, k * LANES : (k + 1) * LANES]

        loop(PX // MT, body)

    def collect(at, dilation):
        total = None
        for kx in range(3):
            part = None
            for ky in range(3):
                tile = taps[
                    ky * 3 + kx, rows_at(RIM + at + (ky - 1) * dilation * PW, STRIP, PW), :
                ]
                part = tile if part is None else part + tile
            part = inside(part, (kx - 1) * dilation)
            total = part if total is None else total + part
        return total

    stack[:, :LANES] = stack0[...]
    for index in range(5):
        layer = LAYERS[index]
        width = layer["blocks"] * LANES
        multiply(lambda rows, width=width: stack[rows, :width], kernels[index])

        def finish(rows, at, index=index, layer=layer):
            value = collect(at, 1) + biases[index : index + 1, :]
            pre[index, rows, :] = value
            fresh = leaky(value).astype(BF16)
            if index == 4:
                stack[rows, 3 * LANES : 4 * LANES] = stack[rows, 3 * LANES : 4 * LANES] + fresh
            else:
                stack[rows, (index + 1) * LANES : (index + 2) * LANES] = fresh

        strips(finish)
    for index in range(6, 12):
        layer = LAYERS[index]
        if index == 6:
            multiply(lambda rows: stack[rows, :], kernels[index])
        else:
            multiply(lambda rows, index=index: ctx[index - 7, rows, :], kernels[index])

        def finish(rows, at, index=index, layer=layer):
            value = collect(at, layer["dil"]) + biases[index : index + 1, :]
            pre[index - 1, rows, :] = value
            ctx[index - 6, rows, :] = leaky(value).astype(BF16)

        strips(finish)

    def head(i):
        rows = rows_at(i * MT, MT, MT)
        product = lax.dot_general(stack[rows, :], kernels[5][...], NT, preferred_element_type=F32)
        product = product + lax.dot_general(
            ctx[5, rows, :], kernels[12][...], NT, preferred_element_type=F32
        )
        taps[0, rows_at(RIM + i * MT, MT, MT), :] = product

    loop(PX // MT, head)

    row = iota((LANES, LANES), 0)
    col = iota((LANES, LANES), 1)
    used = (col < 18) & (row % 2 == col % 2)
    fold = jnp.where(used & (row < 18), 1.0, 0.0)
    spread = jnp.where(used & (row < 2), 1.0, 0.0).astype(BF16)
    pick = jnp.where(used & (row >= 2 * FC + 4) & (row < 2 * FC + 6), 1.0, 0.0).astype(BF16)
    marked = jnp.where(row == 2 * FC + 6, 1.0, 0.0).astype(BF16)
    both = (biases[5:6, :], biases[12:13, :])
    shared = sum(
        jnp.dot(jnp.broadcast_to(b, (8, LANES)).astype(BF16), spread, preferred_element_type=F32)
        for b in both
    )[:1]
    partial[...] = jnp.zeros_like(partial)

    def spread_grad(rows, at, grad, dilation):
        for kx in range(3):
            moved[kx, rows_at(RIM + at, STRIP, STRIP), :] = inside(
                grad, -(kx - 1) * dilation
            ).astype(BF16)

    def settle(rows, at):
        total = None
        for kx in range(3):
            part = None
            for ky in range(3):
                tile = taps[0, rows_at(RIM + at + (ky - 1) * PW, STRIP, PW), :]
                tile = jnp.where(lane // 2 == ky * 3 + kx, tile, 0.0)
                part = tile if part is None else part + tile
            part = inside(part, kx - 1)
            total = part if total is None else total + part
        motion = (
            jnp.dot(total, fold, preferred_element_type=F32, precision=lax.Precision.HIGHEST)
            + shared
        )
        motion_out[:, rows] = motion.T[: motion_out.shape[0]]
        own = joined[rows, :]
        aim = jnp.dot(own, pick, preferred_element_type=F32)
        mask = jnp.dot(own, marked, preferred_element_type=F32)
        mismatch = motion - aim
        square = mismatch * mismatch
        other = jnp.where(
            lane % 2 == 0, pltpu.roll(square, LANES - 1, 1), pltpu.roll(square, 1, 1)
        )
        length = jnp.sqrt(square + other + EPE_EPS)
        height = (iota((STRIP, LANES), 0) + at) // PW
        interior = (
            (height >= MARGIN)
            & (height < PH - MARGIN)
            & (column >= MARGIN)
            & (column < PW - MARGIN)
            & (lane < 18)
        )
        grad = jnp.where(interior, weighting[...] * mask * mismatch / length, 0.0)
        grad = grad.astype(BF16).astype(F32)
        partial[5] += grad.reshape(STRIP // 8, 8, LANES).sum(0)
        spread_grad(rows, at, grad, 1)

    strips(settle)
    partial[12] = partial[5]

    def choose(rows, at):
        total = None
        for kx in range(3):
            for ky in range(3):
                tile = moved[kx, rows_at(RIM + at - (ky - 1) * PW, STRIP, PW), :].astype(F32)
                tile = jnp.where(lane // 2 == ky * 3 + kx, tile, 0.0)
                total = tile if total is None else total + tile
        ghead[rows, :] = total.astype(BF16)

    strips(choose)
    grads[5][...] = lax.dot_general(
        ghead[...], stack[...], TN, preferred_element_type=F32
    ).astype(BF16)
    grads[12][...] = lax.dot_general(
        ghead[...], ctx[5], TN, preferred_element_type=F32
    ).astype(BF16)

    def head_back(i):
        rows = rows_at(i * MT, MT, MT)
        dstack[rows, :] = jnp.dot(ghead[rows, :], kernels[5][...], preferred_element_type=F32)
        dcur[rows, :] = jnp.dot(ghead[rows, :], kernels[12][...], preferred_element_type=F32)

    loop(PX // MT, head_back)

    def back(index, pre_at, load_grad, load_input, store):
        layer = LAYERS[index]
        dilation = layer["dil"]

        def through(rows, at):
            grad = load_grad(rows) * leaky_slope(pre[pre_at, rows, :])
            grad = grad.astype(BF16).astype(F32)
            partial[index] += grad.reshape(STRIP // 8, 8, LANES).sum(0)
            spread_grad(rows, at, grad, dilation)

        strips(through)

        def kernel_grad(ky):
            for kx in range(3):
                out_rows = rows_at((ky * 3 + kx) * LANES, LANES, LANES)
                tile = moved[kx, rows_at(RIM - (ky - 1) * dilation * PW, PX, PW), :]
                grads[index][out_rows, :] = lax.dot_general(
                    tile, load_input(), TN, preferred_element_type=F32
                ).astype(BF16)

        loop(3, kernel_grad)

        def input_grad(i):
            tiles = [
                moved[kx, rows_at(RIM + i * MT - (ky - 1) * dilation * PW, MT, PW), :]
                for ky in range(3)
                for kx in range(3)
            ]
            store(
                rows_at(i * MT, MT, MT),
                jnp.dot(
                    jnp.concatenate(tiles, axis=1), kernels[index][...], preferred_element_type=F32
                ),
            )

        loop(PX // MT, input_grad)

    def store_current(rows, value):
        dcur[rows, :] = value

    for index in range(11, 6, -1):
        back(
            index,
            index - 1,
            lambda rows: dcur[rows, :],
            lambda index=index: ctx[index - 7],
            store_current,
        )

    def store_stack(rows, value):
        dstack[rows, : value.shape[1]] += value

    back(6, 5, lambda rows: dcur[rows, :], lambda: stack[...], store_stack)
    for index in range(4, -1, -1):
        block = 3 if index == 4 else index + 1
        width = LAYERS[index]["blocks"] * LANES
        back(
            index,
            index,
            lambda rows, block=block: dstack[rows, block * LANES : (block + 1) * LANES],
            lambda width=width: stack[:, :width],
            store_stack,
        )
    bias_out[...] = partial[...].sum(1)
    correlate_back(joined, cost, dstack, second, dsecond, picture_out)


def network(stack0, cost, joined, weighting, kernels, biases, blocks, channels):
    grads = [jax.ShapeDtypeStruct(k.shape, BF16) for k in kernels]
    outs = pl.pallas_call(
        network_kernel,
        out_shape=[
            jax.ShapeDtypeStruct((8, PX), F32),
            jax.ShapeDtypeStruct((blocks, channels, LANES), BF16),
            *grads,
            jax.ShapeDtypeStruct((16, LANES), F32),
        ],
        scratch_shapes=[
            pltpu.VMEM((PX, 5 * LANES), BF16),
            pltpu.VMEM((6, PX, LANES), BF16),
            pltpu.VMEM((11, PX, LANES), F32),
            pltpu.VMEM((9, PX + 2 * RIM, LANES), F32),
            pltpu.VMEM((3, PX + 2 * RIM, LANES), BF16),
            pltpu.VMEM((PX, 5 * LANES), F32),
            pltpu.VMEM((PX, LANES), F32),
            pltpu.VMEM((PX, LANES), BF16),
            pltpu.VMEM((16, 8, LANES), F32),
            pltpu.VMEM((SEC_ROWS, LANES), F32),
            pltpu.VMEM((SEC_ROWS, LANES), F32),
        ],
        compiler_params=pltpu.CompilerParams(vmem_limit_bytes=62 * 2**20),
        name="network",
    )(stack0, cost, joined, weighting, *kernels, biases)
    return outs[0], outs[1], outs[2:15], outs[15]


def update(weights, momentum, average, gradient):
    gradient = gradient + DECAY_RATE * weights
    renewed = MOMENTUM_RATE * momentum + gradient
    stepped = weights - LEARN_RATE * (gradient + MOMENTUM_RATE * renewed)
    return (stepped, renewed, AVERAGE_DECAY * average + (1.0 - AVERAGE_DECAY) * stepped)


CHANNELS = 72


def shards(features, coarse_flow, target, valid_mask, weights, momentum, average):
    groups = lax.axis_size("grp")
    devices = lax.axis_size("dev")
    own_rows = features.shape[2]
    width = features.shape[3]
    breadth = width // devices
    height = own_rows * devices
    assert breadth + 2 * MARGIN == PW and height + 2 * MARGIN == PH
    gathered = lax.all_gather(weights.astype(BF16), "dev", axis=0, tiled=True)
    counted = lax.psum(jnp.sum(valid_mask.astype(F32)), ("grp", "dev"))
    weighting = groups * height * width / counted

    marked = valid_mask.astype(BF16)[:, None]
    spare = jnp.zeros((1, CHANNELS - 71, own_rows, width), BF16)
    picture = jnp.concatenate([features, coarse_flow, target, marked, spare], axis=1)[0]
    picture = jnp.pad(picture, ((0, 0), (0, 0), (MARGIN, MARGIN)))
    windows = jnp.stack([picture[:, :, t * breadth : t * breadth + PW] for t in range(devices)])
    received = lax.all_to_all(windows, "dev", split_axis=0, concat_axis=0, tiled=True)
    per = 4 // own_rows
    blocks = devices // per
    received = received.reshape(blocks, per, CHANNELS, own_rows * PW)
    received = jnp.swapaxes(received, 1, 2).reshape(blocks, CHANNELS, LANES)
    received = jnp.pad(received, ((0, 0), (0, LANES - CHANNELS), (0, 0)))

    stack0, cost, joined = correlate(received)
    unpacked = unpack(gathered.reshape(-1, LANES))
    kernels, biases = unpacked[:13], unpacked[13]
    motion, tiles, grads, bias_grads = network(
        stack0,
        cost,
        joined,
        jnp.full((1, LANES), weighting, F32),
        kernels,
        biases,
        blocks,
        CHANNELS,
    )
    flow = motion[:2].reshape(1, 2, PH, PW)[
        :, :, MARGIN : MARGIN + height, MARGIN : MARGIN + breadth
    ]
    flat_grad = pack(grads, bias_grads, gathered.shape[0] // LANES)

    tiles = tiles.reshape(blocks, CHANNELS, per, own_rows, PW)
    tiles = jnp.swapaxes(tiles, 1, 2).reshape(devices, CHANNELS, own_rows, PW)
    returned = lax.all_to_all(tiles, "dev", split_axis=0, concat_axis=0, tiled=True)
    returned = returned.astype(F32)
    wide = jnp.transpose(returned, (1, 2, 0, 3))
    centre = wide[..., MARGIN : MARGIN + breadth]
    left = wide[:, :, 1:, :MARGIN]
    right = wide[:, :, :-1, MARGIN + breadth :]
    none = ((0, 0), (0, 0))
    centre = centre + jnp.pad(left, (*none, (0, 1), (breadth - MARGIN, 0)))
    centre = centre + jnp.pad(right, (*none, (1, 0), (0, breadth - MARGIN)))
    row_grad = centre.reshape(1, CHANNELS, own_rows, width)
    feature_grad = row_grad[:, : 2 * FC]
    coarse_grad = row_grad[:, 2 * FC : 2 * FC + 4]

    shard_grad = lax.psum_scatter(
        flat_grad.reshape(-1), "dev", scatter_dimension=0, tiled=True
    )
    total_grad = lax.psum(shard_grad, "grp").astype(F32)
    new_weights, new_momentum, new_average = update(weights, momentum, average, total_grad)
    return (
        flow,
        feature_grad,
        coarse_grad,
        new_weights,
        new_momentum,
        new_average,
        new_weights.astype(BF16),
    )


def solution(mesh):
    in_specs = (
        P("grp", None, "dev", None),
        P("grp", None, "dev", None),
        P("grp", None, "dev", None),
        P("grp", "dev", None),
        P("dev"),
        P("dev"),
        P("dev"),
    )
    out_specs = (
        P("grp", None, None, "dev"),
        P("grp", None, "dev", None),
        P("grp", None, "dev", None),
        P("dev"),
        P("dev"),
        P("dev"),
        P("dev"),
    )
    return jax.shard_map(shards, mesh=mesh, in_specs=in_specs, out_specs=out_specs, check_vma=False)
```

```python
import functools

import jax
import jax.numpy as jnp
from jax import lax
from jax.experimental import pallas as pl
from jax.experimental.pallas import tpu as pltpu
from jax.sharding import PartitionSpec as P

FC = 32
SR = 4
EXT = 2 * SR + 1
NCOST = EXT * EXT
NS0 = NCOST + FC + 4
DENSE = (128, 128, 96, 64, 32)
CONTEXT = (128, 128, 128, 96, 64, 32, 2)
DILATIONS = (1, 2, 4, 8, 16, 1, 1)
MARGIN = 8

SLOPE = 0.1
EPE_EPS = 0.01
MOMENTUM_RATE = 0.5
AVERAGE_DECAY = 0.5
LEARN_RATE = 0.001
DECAY_RATE = 0.0001

LANES = 128
PH = 48
PW = 32
PX = PH * PW
RIM = 16 * PW
STRIP = 128
MT = 768
PITCH = 40
F32 = jnp.float32
BF16 = jnp.bfloat16
NT = (((1,), (1,)), ((), ()))
TN = (((0,), (0,)), ((), ()))


def layer_table():
    places = [(NS0, 0, 0), (128, 1, 0), (128, 2, 0), (96, 3, 0), (64, 4, 0), (32, 4, 64)]
    layers = []
    offset = 0

    def add(pieces, outgoing, dilation, shift):
        nonlocal offset
        incoming = sum(n for n, _, _ in pieces)
        row = 9 * incoming
        segments = []
        at = 0
        for n, block, lane in pieces:
            first, over = 9 * at // LANES, 9 * at % LANES
            slot = -(-(9 * lane - over) // LANES)
            back = 9 * lane - over - LANES * slot
            chunks = -(-(over + 9 * n) // LANES)
            segments.append(
                dict(n=n, block=block, lane=lane, first=first, slot=slot, back=back, chunks=chunks)
            )
            at += n
        blocks = 1 + max(b for _, b, _ in pieces)
        layers.append(
            dict(
                out=outgoing,
                row=row,
                chunks=-(-row // LANES),
                start=offset,
                dil=dilation,
                shift=shift,
                segments=segments,
                blocks=blocks,
                bias=offset + row * outgoing,
                shape=(LANES, blocks * LANES) if outgoing == 2 else (3 * LANES, 3 * blocks * LANES),
            )
        )
        offset += row * outgoing + outgoing

    for i, outgoing in enumerate(DENSE):
        add(places[i::-1], outgoing, 1, 64 if i == 4 else 0)
    add(places[::-1], 2, 1, 0)
    add(places[::-1], CONTEXT[0], DILATIONS[0], 0)
    for i in range(1, 7):
        add([(CONTEXT[i - 1], 0, 0)], CONTEXT[i], DILATIONS[i], 0)
    return layers, offset


LAYERS, COUNT = layer_table()
EARLY = (0, 1, 2, 3)
LATE = (4, 5, 6, 7, 8, 9, 10, 11, 12)
CUT = LAYERS[4]["start"] // LANES // 16 * 16


def sort_groups(indices):
    order = [(segment["back"], i, s) for i in indices for s, segment in enumerate(LAYERS[i]["segments"])]
    order.sort(key=lambda t: -t[0])
    at = 0
    groups = {}
    classes = []
    for back, i, s in order:
        if not classes or classes[-1][0] != back:
            classes.append([back, at, at])
        groups[i, s] = at
        at += -(-LAYERS[i]["out"] // 16) * 16
        classes[-1][2] = at
    return groups, classes, at


def iota(shape, dim):
    return lax.broadcasted_iota(jnp.int32, shape, dim)


def rows_at(start, size, step=8):
    return pl.ds(pl.multiple_of(start, step), size)


def sigmoid(v):
    return 0.5 * jnp.tanh(0.5 * v) + 0.5


def leaky(v):
    return SLOPE * v + (1.0 - SLOPE) * v * sigmoid(v)


def leaky_slope(v):
    s = sigmoid(v)
    return SLOPE + (1.0 - SLOPE) * (s + v * s * (1.0 - s))


def loop(count, body):
    def step(i, carry):
        body(i)
        return carry

    lax.fori_loop(0, count, step, 0)


def fill_order(order):
    order[:LANES, :] = jnp.zeros((LANES, 9 * LANES), BF16)
    order[10 * LANES :, :] = jnp.zeros((LANES, 9 * LANES), BF16)
    for k in range(9):
        for m in range(9):
            row = iota((LANES, LANES), 0) + m * LANES
            col = iota((LANES, LANES), 1)
            order[(m + 1) * LANES : (m + 2) * LANES, k * LANES : (k + 1) * LANES] = jnp.where(
                row == 9 * col + k, 1.0, 0.0
            ).astype(BF16)


def within(n, lane):
    spot = iota((1, LANES), 1)
    return jnp.where((spot >= lane) & (spot < lane + n), 1.0, 0.0).astype(BF16)


def pitch_of(chunks):
    return -(-chunks // 8) * 8


def unpack_kernel(indices, base, n_parts, *refs):
    place_at = refs[0]
    parts = refs[1 : 1 + n_parts]
    carried = refs[1 + n_parts]
    outs = refs[2 + n_parts : 2 + n_parts + len(indices)]
    bias_out = refs[2 + n_parts + len(indices)]
    carry_out = refs[3 + n_parts + len(indices)]
    whole, slabs, aligned, result, order, heads = refs[-6:]
    count = whole.shape[0] - 64
    fill_order(order)
    groups, classes, _ = sort_groups(indices)
    if base:
        whole[: carried.shape[0], :] = carried[...].astype(F32)
    for at_part, part in enumerate(parts):
        size = part.shape[1]
        for j in range(part.shape[0]):
            to = place_at[at_part, j] - base

            def widen(i, part=part, j=j, to=to):
                whole[pl.ds(to + i * 16, 16), :] = part[j, rows_at(i * 16, 16, 16), :].astype(F32)

            lax.fori_loop(0, size // 16, lambda i, c: (widen(i), c)[1], 0, unroll=8)
    whole[count:, :] = jnp.zeros((64, LANES), F32)
    if not base:
        carry_out[...] = whole[CUT:count, :].astype(BF16)
    else:
        carry_out[...] = jnp.zeros_like(carry_out)
    lane = iota((8, LANES), 1)
    bias_out[...] = jnp.zeros_like(bias_out)

    for at_out, index in enumerate(indices):
        layer = LAYERS[index]
        outgoing = layer["out"]
        kept = -(-outgoing // 16) * 16
        start = layer["start"] - base * LANES
        spot = iota((kept, LANES), 1)
        pitch = pitch_of(layer["chunks"] + 1)
        still = layer["row"] % LANES == 0
        if not still:
            unroll = min(8, outgoing)

            def take(i, unroll=unroll, row=layer["row"], start=start, pitch=pitch):
                for u in range(unroll):
                    o = i * unroll + u
                    first = start + o * row
                    turn = (LANES - (first & (LANES - 1))) & (LANES - 1)
                    for v in range(pitch // 8):
                        tile = whole[pl.ds((first >> 7) + 8 * v, 8), :]
                        slabs[rows_at(o * pitch + 8 * v, 8), :] = pltpu.roll(tile, turn, 1)

            loop(outgoing // unroll, take)
            off = (start + iota((kept, LANES), 0) * layer["row"]) & (LANES - 1)
        chunks = {}
        for t in range(layer["chunks"]):
            if still:
                row, fixed = divmod(start, LANES)
                step = layer["row"] // LANES
                here = whole[pl.ds(row + t, kept, stride=step), :]
                after = whole[pl.ds(row + t + 1, kept, stride=step), :]
                chunk = jnp.where(spot >= fixed, here, after)
                chunk = pltpu.roll(chunk, (LANES - fixed) % LANES, 1)
            else:
                here = slabs[pl.ds(t, kept, stride=pitch), :]
                after = slabs[pl.ds(t + 1, kept, stride=pitch), :]
                chunk = jnp.where(spot < LANES - off, here, after)
            chunk = chunk.astype(BF16)
            for s, segment in enumerate(layer["segments"]):
                to = t - segment["first"]
                if 0 <= to < segment["chunks"]:
                    to += segment["slot"]
                    at = groups[index, s]
                    aligned[at : at + kept, to * LANES : (to + 1) * LANES] = chunk
        for s, segment in enumerate(layer["segments"]):
            at = groups[index, s]
            for to in range(10):
                if not segment["slot"] <= to < segment["slot"] + segment["chunks"]:
                    aligned[at : at + kept, to * LANES : (to + 1) * LANES] = jnp.zeros(
                        (kept, LANES), BF16
                    )
        shift = layer["shift"]
        first = layer["bias"] - base * LANES - shift
        row, fixed = divmod(first, LANES)
        here = pltpu.roll(whole[row : row + 1, :], (LANES - fixed) % LANES, 1)
        after = pltpu.roll(whole[row + 1 : row + 2, :], (LANES - fixed) % LANES, 1)
        line = iota((1, LANES), 1)
        value = jnp.where(line < LANES - fixed, here, after)
        bias_out[index : index + 1, :] = jnp.where(
            (line >= shift) & (line < shift + outgoing), value, 0.0
        )

    for back, low, high in classes:
        wide = 9 if back == 0 else 10
        result[low:high, :] = jnp.dot(
            aligned[low:high, : wide * LANES],
            order[LANES + back : LANES + back + wide * LANES, :],
            preferred_element_type=F32,
        ).astype(BF16)

    for at_out, index in enumerate(indices):
        layer = LAYERS[index]
        outgoing = layer["out"]
        shift = layer["shift"]
        out = outs[at_out]
        width = layer["blocks"] * LANES
        if outgoing == 2:
            heads[...] = jnp.zeros_like(heads)
        elif outgoing < LANES:
            out[...] = jnp.zeros_like(out)
        kept = -(-outgoing // 16) * 16
        for block in range(layer["blocks"]):
            for k in range(9):
                total = None
                for s, segment in enumerate(layer["segments"]):
                    if segment["block"] != block:
                        continue
                    at = groups[index, s]
                    tile = result[at : at + kept, k * LANES : (k + 1) * LANES]
                    if segment["n"] < LANES:
                        tile = tile * within(segment["n"], segment["lane"])
                    total = tile if total is None else total + tile
                if outgoing == 2:
                    heads[2 * k : 2 * k + 2, block * LANES : (block + 1) * LANES] = total.astype(
                        F32
                    )[:2]
                else:
                    ky, kx = divmod(k, 3)
                    at = kx * width + block * LANES
                    out[ky * LANES + shift : ky * LANES + shift + outgoing, at : at + LANES] = total
        if outgoing == 2:
            out[...] = heads[:, :width].astype(BF16)


def unpack(indices, base, end, place_at, parts, carried):
    _, _, group_rows = sort_groups(indices)
    count = end - base
    shapes = [jax.ShapeDtypeStruct(LAYERS[i]["shape"], BF16) for i in indices]
    shapes.append(jax.ShapeDtypeStruct((16, LANES), F32))
    shapes.append(jax.ShapeDtypeStruct((16 if base else end - CUT, LANES), BF16))
    outs = pl.pallas_call(
        functools.partial(unpack_kernel, indices, base, len(parts)),
        out_shape=shapes,
        in_specs=[pl.BlockSpec(memory_space=pltpu.SMEM)]
        + [pl.BlockSpec(memory_space=pltpu.VMEM)] * (len(parts) + 1),
        scratch_shapes=[
            pltpu.VMEM((count + 64, LANES), F32),
            pltpu.VMEM((48 * LANES, LANES), F32),
            pltpu.VMEM((group_rows, 10 * LANES), BF16),
            pltpu.VMEM((group_rows, 9 * LANES), BF16),
            pltpu.VMEM((11 * LANES, 9 * LANES), BF16),
            pltpu.VMEM((LANES, 5 * LANES), F32),
        ],
        compiler_params=pltpu.CompilerParams(vmem_limit_bytes=50 * 2**20),
        cost_estimate=pl.CostEstimate(
            flops=25_000_000_000, bytes_accessed=8_000_000, transcendentals=0
        ),
        name="unpack_weights",
    )(place_at, *parts, carried)
    return outs[: len(indices)], outs[-2], outs[-1]


def pack_kernel(indices, base, *refs):
    place_at = refs[0]
    grads = refs[1 : 1 + len(indices)]
    bias_in = refs[1 + len(indices)]
    carried = refs[2 + len(indices)]
    halves = refs[3 + len(indices) : 5 + len(indices)]
    carry_out = refs[5 + len(indices)]
    whole, slabs, gathered, result, order, heads = refs[-6:]
    count = whole.shape[0] - 64
    fill_order(order)
    groups, classes, _ = sort_groups(indices)
    for at_in, index in enumerate(indices):
        layer = LAYERS[index]
        outgoing = layer["out"]
        shift = layer["shift"]
        grad = grads[at_in]
        width = layer["blocks"] * LANES
        if outgoing == 2:
            heads[:LANES, :width] = grad[...].astype(F32)
            heads[LANES:, :] = jnp.zeros((16, heads.shape[1]), F32)
        for s, segment in enumerate(layer["segments"]):
            at = groups[index, s]
            block = segment["block"]
            for k in range(9):
                if outgoing == 2:
                    tile = heads[2 * k : 2 * k + 16, block * LANES : (block + 1) * LANES]
                    tile = tile.astype(BF16)
                else:
                    ky, kx = divmod(k, 3)
                    column = kx * width + block * LANES
                    tile = grad[
                        ky * LANES + shift : ky * LANES + shift + outgoing, column : column + LANES
                    ]
                if segment["n"] < LANES:
                    tile = tile * within(segment["n"], segment["lane"])
                gathered[at : at + tile.shape[0], k * LANES : (k + 1) * LANES] = tile

    for back, low, high in classes:
        wide = 9 if back == 0 else 10
        result[low:high, : wide * LANES] = lax.dot_general(
            gathered[low:high, :],
            order[LANES + back : LANES + back + wide * LANES, :],
            NT,
            preferred_element_type=F32,
        )

    lane = iota((8, LANES), 1)
    sub = iota((8, LANES), 0)

    for at_in, index in enumerate(indices):
        layer = LAYERS[index]
        outgoing = layer["out"]
        start = layer["start"] - base * LANES
        still = layer["row"] % LANES == 0
        pitch = pitch_of(layer["chunks"])
        spot = iota((outgoing, LANES), 1)
        turned = []
        for t in range(layer["chunks"]):
            chunk = None
            for s, segment in enumerate(layer["segments"]):
                to = t - segment["first"]
                if 0 <= to < segment["chunks"]:
                    to += segment["slot"]
                    at = groups[index, s]
                    tile = result[at : at + outgoing, to * LANES : (to + 1) * LANES]
                    chunk = tile if chunk is None else chunk + tile
            if still:
                turned.append(pltpu.roll(chunk, start % LANES, 1))
            else:
                slabs[pl.ds(t, outgoing, stride=pitch), :] = chunk
        if still:
            row, fixed = divmod(start, LANES)
            step = layer["row"] // LANES
            for t in range(step):
                before = turned[t - 1] if t else pltpu.roll(turned[-1], 1, 0)
                value = jnp.where(spot >= fixed, turned[t], before)
                if t == 0:
                    kept = whole[row : row + 1, :]
                    top = (iota((outgoing, LANES), 0) == 0) & (spot < fixed)
                    value = jnp.where(top, kept, value)
                whole[pl.ds(row + t, outgoing, stride=step), :] = value
            last = pltpu.roll(turned[-1][outgoing - 8 :, :], 1, 0)
            end = row + step * outgoing
            pltpu.store(whole.at[end : end + 8, :], last, mask=(sub == 0) & (lane < fixed))
        else:
            unroll = min(4, outgoing)

            def put(i, start=start, row=layer["row"], pitch=pitch, unroll=unroll):
                for u in range(unroll):
                    o = i * unroll + u
                    first = start + o * row
                    off = first & (LANES - 1)
                    for v in range(pitch // 8):
                        tile = pltpu.roll(slabs[rows_at(o * pitch + 8 * v, 8), :], off, 1)
                        to = (first >> 7) + 8 * v
                        pltpu.store(whole.at[pl.ds(to, 8), :], tile, mask=lane >= off)
                        pltpu.store(whole.at[pl.ds(to + 1, 8), :], tile, mask=lane < off)

            loop(outgoing // unroll, put)
        line = bias_in[index : index + 1, :]
        first = layer["bias"] - base * LANES
        row, fixed = divmod(first, LANES)
        line = pltpu.roll(line, (fixed - layer["shift"]) % LANES, 1)
        line = jnp.broadcast_to(line, (8, LANES))
        pltpu.store(whole.at[row : row + 8, :], line, mask=(sub == 0) & (lane >= fixed))
        pltpu.store(whole.at[row + 1 : row + 9, :], line, mask=(sub == 0) & (lane < fixed))
    if base:
        end, off = divmod(COUNT - base * LANES, LANES)
        pltpu.store(
            whole.at[end : end + 8, :], jnp.zeros((8, LANES), F32), mask=(sub > 0) | (lane >= off)
        )
        if count > end + 8:
            whole[end + 8 : count, :] = jnp.zeros((count - end - 8, LANES), F32)
        carry_out[...] = whole[: carry_out.shape[0], :].astype(BF16)
    else:
        end, off = divmod(LAYERS[4]["start"], LANES)
        line = carried[...].astype(F32)
        keep = (iota(line.shape, 0) > end - CUT) | (
            (iota(line.shape, 0) == end - CUT) & (iota(line.shape, 1) >= off)
        )
        whole[CUT:count, :] = jnp.where(keep, line, whole[CUT:count, :])
        carry_out[...] = jnp.zeros_like(carry_out)
    for half in range(2):
        size = halves[half].shape[1]
        for j in range(halves[half].shape[0]):
            begin = place_at[half, j] - base

            def narrow(i, half=half, j=j, begin=begin):
                halves[half][j, rows_at(i * 16, 16, 16), :] = whole[
                    pl.ds(begin + i * 16, 16), :
                ].astype(BF16)

            lax.fori_loop(0, size // 16, lambda i, c: (narrow(i), c)[1], 0, unroll=8)


def pack(indices, base, end, place_at, grads, bias, carried, pieces, size):
    _, _, group_rows = sort_groups(indices)
    count = end - base
    return pl.pallas_call(
        functools.partial(pack_kernel, indices, base),
        out_shape=[jax.ShapeDtypeStruct((pieces, size, LANES), BF16)] * 2
        + [jax.ShapeDtypeStruct((end // 2 - CUT if base else 16, LANES), BF16)],
        in_specs=[pl.BlockSpec(memory_space=pltpu.SMEM)]
        + [pl.BlockSpec(memory_space=pltpu.VMEM)] * (len(indices) + 2),
        scratch_shapes=[
            pltpu.VMEM((count + 64, LANES), F32),
            pltpu.VMEM((40 * LANES + 64, LANES), F32),
            pltpu.VMEM((group_rows, 9 * LANES), BF16),
            pltpu.VMEM((group_rows, 10 * LANES), F32),
            pltpu.VMEM((11 * LANES, 9 * LANES), BF16),
            pltpu.VMEM((LANES + 16, 5 * LANES), F32),
        ],
        compiler_params=pltpu.CompilerParams(vmem_limit_bytes=50 * 2**20),
        cost_estimate=pl.CostEstimate(
            flops=25_000_000_000, bytes_accessed=8_000_000, transcendentals=0
        ),
        name="pack_gradients",
    )(place_at, *grads, bias, carried)


ROWS4 = 4 * PW
SEC_ROWS = (PH + 2 * SR) * PITCH + LANES


def load_second(joined, second):
    second[...] = jnp.zeros_like(second)
    keep = iota((PW, LANES), 1) < FC
    for y in range(MARGIN, PH - MARGIN):
        row = joined[y * PW : (y + 1) * PW, :].astype(F32)
        row = jnp.where(keep, pltpu.roll(row, LANES - FC, 1), 0.0)
        at = (y + SR) * PITCH + 8
        second[at : at + PW, :] = row


def band_shift(dy, third):
    return EXT * dy - PITCH * third - (8 - SR)


def correlate_kernel(received, stack0, cost, joined, second):
    joined[...] = jnp.zeros_like(joined)
    blocks = received.shape[0]
    for s in range(blocks):
        tile = received[s].astype(F32).T
        joined[RIM // 2 + s * ROWS4 : RIM // 2 + (s + 1) * ROWS4, :] = tile.astype(BF16)
    load_second(joined, second)
    row = iota((ROWS4, ROWS4), 0)
    col = iota((ROWS4, ROWS4), 1)
    flip = jnp.where((row // PW == col // PW) & (row % PW + col % PW == PW - 1), 1.0, 0.0).astype(
        BF16
    )
    lane = iota((ROWS4, LANES), 1)
    narrow = iota((PW, LANES), 1)

    def body(i):
        own = joined[rows_at(i * ROWS4, ROWS4, ROWS4), :]
        first = jnp.where(lane < FC, own.astype(F32), 0.0).astype(BF16)
        first = jnp.dot(flip, first, preferred_element_type=F32).astype(BF16)
        bands = []
        for g in range(4):
            window = second[rows_at((4 * i + 3 * g) * PITCH, LANES), :].astype(BF16)
            bands.append(lax.dot_general(first, window, NT, preferred_element_type=F32))
        pieces = []
        for yy in range(4):
            total = jnp.zeros((PW, LANES), F32)
            turned = [
                pltpu.roll(band[yy * PW : (yy + 1) * PW, :], 0, 1, stride=1, stride_axis=0)
                for band in bands
            ]
            for dy in range(EXT):
                t = yy + dy
                shift = (band_shift(dy, t % 3) - (PW - 1)) % LANES
                band = pltpu.roll(turned[t // 3], shift, 1)
                total = jnp.where((narrow >= EXT * dy) & (narrow < EXT * (dy + 1)), band, total)
            pieces.append(total * (1.0 / FC))
        total = jnp.concatenate(pieces, axis=0)
        high = total.astype(BF16)
        low = (total - high.astype(F32)).astype(BF16)
        total = jnp.dot(flip, high, preferred_element_type=F32) + jnp.dot(
            flip, low, preferred_element_type=F32
        )
        cost[rows_at(i * ROWS4, ROWS4, ROWS4), :] = total
        wide = own.astype(F32)
        filled = jnp.where(lane < NCOST, leaky(total), pltpu.roll(wide, NCOST, 1))
        coarse = pltpu.roll(wide, NCOST + FC - 2 * FC, 1)
        filled = jnp.where(lane >= NCOST + FC, coarse, filled)
        filled = jnp.where(lane < NS0, filled, 0.0)
        stack0[rows_at(i * ROWS4, ROWS4, ROWS4), :] = filled.astype(BF16)

    loop(PH // 4, body)


def correlate(received):
    return pl.pallas_call(
        correlate_kernel,
        out_shape=[
            jax.ShapeDtypeStruct((PX, LANES), BF16),
            jax.ShapeDtypeStruct((PX, LANES), F32),
            jax.ShapeDtypeStruct((PX, LANES), BF16),
        ],
        scratch_shapes=[pltpu.VMEM((SEC_ROWS, LANES), F32)],
        compiler_params=pltpu.CompilerParams(vmem_limit_bytes=32 * 2**20),
        name="correlate",
    )(received)


class Work:
    def __init__(self, taps, moved, partial):
        self.taps = taps
        self.moved = moved
        self.partial = partial
        self.column = iota((STRIP, LANES), 0) % PW
        self.lane = iota((STRIP, LANES), 1)
        if taps is not None:
            taps[:, :RIM, :] = jnp.zeros((3, RIM, LANES), F32)
            taps[:, RIM + PX :, :] = jnp.zeros((3, RIM, LANES), F32)
        if moved is not None:
            moved[:, :RIM, :] = jnp.zeros((3, RIM, LANES), BF16)
            moved[:, RIM + PX :, :] = jnp.zeros((3, RIM, LANES), BF16)

    def strips(self, body):
        loop(PX // STRIP, lambda i: body(rows_at(i * STRIP, STRIP, STRIP), i * STRIP))

    def inside(self, tile, shift):
        if shift == 0:
            return tile
        valid = (self.column + shift >= 0) & (self.column + shift < PW)
        return jnp.where(valid, pltpu.roll(tile, (-shift) % STRIP, 0), 0.0)

    def spread(self, store, tile, dilation):
        for kx in range(3):
            store(kx, self.inside(tile, (kx - 1) * dilation).astype(BF16))

    def multiply(self, load, kernel):
        def body(i):
            rows = rows_at(i * MT, MT, MT)
            value = jnp.concatenate([load(kx, rows) for kx in range(3)], axis=1)
            product = lax.dot_general(value, kernel[...], NT, preferred_element_type=F32)
            for ky in range(3):
                self.taps[ky, rows_at(RIM + i * MT, MT, MT), :] = product[
                    :, ky * LANES : (ky + 1) * LANES
                ]

        loop(PX // MT, body)

    def collect(self, at, dilation):
        total = None
        for ky in range(3):
            tile = self.taps[ky, rows_at(RIM + at + (ky - 1) * dilation * PW, STRIP, PW), :]
            total = tile if total is None else total + tile
        return total

    def spread_grad(self, at, grad, dilation):
        for kx in range(3):
            self.moved[kx, rows_at(RIM + at, STRIP, STRIP), :] = self.inside(
                grad, -(kx - 1) * dilation
            ).astype(BF16)

    def count_bias(self, index, grad):
        self.partial[index] += grad.reshape(STRIP // 8, 8, LANES).sum(0)

    def back(self, index, load_grad, load_pre, load_input, kernel, out, store):
        layer = LAYERS[index]
        dilation = layer["dil"]
        width = layer["blocks"] * LANES

        def through(rows, at):
            grad = load_grad(rows) * leaky_slope(load_pre(rows))
            grad = grad.astype(BF16).astype(F32)
            self.count_bias(index, grad)
            self.spread_grad(at, grad, dilation)

        self.strips(through)
        grad = jnp.concatenate(
            [
                self.moved[1, RIM - (ky - 1) * dilation * PW : RIM - (ky - 1) * dilation * PW + PX, :]
                for ky in range(3)
            ],
            axis=1,
        )
        for kx in range(3):
            out[:, kx * width : (kx + 1) * width] = lax.dot_general(
                grad, load_input(kx), TN, preferred_element_type=F32
            ).astype(BF16)

        def input_grad(i):
            tiles = [
                self.moved[kx, rows_at(RIM + i * MT - (ky - 1) * dilation * PW, MT, PW), :]
                for ky in range(3)
                for kx in range(3)
            ]
            weights = [
                kernel[ky * LANES : (ky + 1) * LANES, kx * width : (kx + 1) * width]
                for ky in range(3)
                for kx in range(3)
            ]
            store(
                rows_at(i * MT, MT, MT),
                jnp.dot(
                    jnp.concatenate(tiles, axis=1),
                    jnp.concatenate(weights, axis=0),
                    preferred_element_type=F32,
                ),
            )

        loop(PX // MT, input_grad)


def forward_kernel(stack0, k1, k2, k3, k4, biases, stack, top, pre, taps):
    work = Work(taps, None, None)

    def first(rows, at):
        tile = stack0[rows, :].astype(F32)

        def keep(kx, value):
            stack[kx, rows, :LANES] = value

        work.spread(keep, tile, 1)

    work.strips(first)
    for index, kernel in enumerate((k1, k2, k3, k4)):
        width = LAYERS[index]["blocks"] * LANES
        work.multiply(lambda kx, rows, width=width: stack[kx, rows, :width], kernel)

        def finish(rows, at, index=index):
            value = work.collect(at, 1) + biases[index : index + 1, :]
            pre[index, rows, :] = value
            place = slice((index + 1) * LANES, (index + 2) * LANES)

            def keep(kx, value):
                if index == 3:
                    top[kx, rows, :] = value
                else:
                    stack[kx, rows, place] = value

            work.spread(keep, leaky(value), 1)

        work.strips(finish)


def vmem_call(kernel, name, shapes, scratch, limit, flops):
    return pl.pallas_call(
        kernel,
        out_shape=shapes,
        scratch_shapes=scratch,
        compiler_params=pltpu.CompilerParams(vmem_limit_bytes=limit * 2**20),
        cost_estimate=pl.CostEstimate(flops=flops, bytes_accessed=20_000_000, transcendentals=0),
        name=name,
    )


def forward(stack0, kernels, biases):
    return vmem_call(
        forward_kernel,
        "dense_forward",
        [
            jax.ShapeDtypeStruct((3, PX, 4 * LANES), BF16),
            jax.ShapeDtypeStruct((3, PX, LANES), BF16),
            jax.ShapeDtypeStruct((4, PX, LANES), F32),
        ],
        [pltpu.VMEM((3, PX + 2 * RIM, LANES), F32)],
        32,
        20_000_000_000,
    )(stack0, *kernels, biases)


def middle_kernel(*refs):
    stack, below, joined, weighting, biases = refs[:5]
    kernels = dict(zip(LATE, refs[5:14]))
    motion_out, dstack, bias_out = refs[14:17]
    grads = dict(zip(LATE, refs[17:26]))
    top, ctx, pre, taps, moved, dcur, ghead, partial = refs[26:]
    work = Work(taps, moved, partial)
    partial[...] = jnp.zeros_like(partial)
    lane = work.lane

    def wide(kx, rows):
        return jnp.concatenate([stack[kx, rows, :], top[kx, rows, :]], axis=1)

    work.multiply(
        lambda kx, rows: jnp.concatenate([stack[kx, rows, :], below[kx, rows, :]], axis=1),
        kernels[4],
    )

    def finish_top(rows, at):
        value = work.collect(at, 1) + biases[4:5, :]
        pre[0, rows, :] = value

        def keep(kx, value):
            top[kx, rows, :] = value + below[kx, rows, :]

        work.spread(keep, leaky(value), 1)

    work.strips(finish_top)
    for index in range(6, 12):
        if index == 6:
            work.multiply(wide, kernels[index])
        else:
            work.multiply(lambda kx, rows, index=index: ctx[index - 7, kx, rows, :], kernels[index])

        def finish(rows, at, index=index):
            value = work.collect(at, LAYERS[index]["dil"]) + biases[index : index + 1, :]
            pre[index - 5, rows, :] = value

            def keep(kx, value):
                ctx[index - 6, kx, rows, :] = value

            work.spread(keep, leaky(value), LAYERS[index + 1]["dil"])

        work.strips(finish)

    def head(i):
        rows = rows_at(i * MT, MT, MT)
        product = lax.dot_general(wide(1, rows), kernels[5][...], NT, preferred_element_type=F32)
        product = product + lax.dot_general(
            ctx[5, 1, rows, :], kernels[12][...], NT, preferred_element_type=F32
        )
        taps[0, rows_at(RIM + i * MT, MT, MT), :] = product

    loop(PX // MT, head)

    row = iota((LANES, LANES), 0)
    col = iota((LANES, LANES), 1)
    used = (col < 18) & (row % 2 == col % 2)
    fold = jnp.where(used & (row < 18), 1.0, 0.0)
    copies = jnp.where(used & (row < 2), 1.0, 0.0).astype(BF16)
    pick = jnp.where(used & (row >= 2 * FC + 4) & (row < 2 * FC + 6), 1.0, 0.0).astype(BF16)
    marked = jnp.where(row == 2 * FC + 6, 1.0, 0.0).astype(BF16)
    shared = sum(
        jnp.dot(jnp.broadcast_to(b, (8, LANES)).astype(BF16), copies, preferred_element_type=F32)
        for b in (biases[5:6, :], biases[12:13, :])
    )[:1]

    def settle(rows, at):
        total = None
        for kx in range(3):
            part = None
            for ky in range(3):
                tile = taps[0, rows_at(RIM + at + (ky - 1) * PW, STRIP, PW), :]
                tile = jnp.where(lane // 2 == ky * 3 + kx, tile, 0.0)
                part = tile if part is None else part + tile
            part = work.inside(part, kx - 1)
            total = part if total is None else total + part
        motion = (
            jnp.dot(total, fold, preferred_element_type=F32, precision=lax.Precision.HIGHEST)
            + shared
        )
        motion_out[:, rows] = motion.T[: motion_out.shape[0]]
        own = joined[rows, :]
        aim = jnp.dot(own, pick, preferred_element_type=F32)
        mask = jnp.dot(own, marked, preferred_element_type=F32)
        mismatch = motion - aim
        square = mismatch * mismatch
        other = jnp.where(
            lane % 2 == 0, pltpu.roll(square, LANES - 1, 1), pltpu.roll(square, 1, 1)
        )
        length = jnp.sqrt(square + other + EPE_EPS)
        height = (iota((STRIP, LANES), 0) + at) // PW
        interior = (
            (height >= MARGIN)
            & (height < PH - MARGIN)
            & (work.column >= MARGIN)
            & (work.column < PW - MARGIN)
            & (lane < 18)
        )
        grad = jnp.where(interior, weighting[...] * mask * mismatch / length, 0.0)
        grad = grad.astype(BF16).astype(F32)
        work.count_bias(5, grad)
        work.spread_grad(at, grad, 1)

    work.strips(settle)
    partial[12] = partial[5]

    def choose(rows, at):
        total = None
        for kx in range(3):
            for ky in range(3):
                tile = moved[kx, rows_at(RIM + at - (ky - 1) * PW, STRIP, PW), :].astype(F32)
                tile = jnp.where(lane // 2 == ky * 3 + kx, tile, 0.0)
                total = tile if total is None else total + tile
        ghead[rows, :] = total.astype(BF16)

    work.strips(choose)
    grads[5][:, : 4 * LANES] = lax.dot_general(
        ghead[...], stack[1], TN, preferred_element_type=F32
    ).astype(BF16)
    grads[5][:, 4 * LANES :] = lax.dot_general(
        ghead[...], top[1], TN, preferred_element_type=F32
    ).astype(BF16)
    grads[12][...] = lax.dot_general(
        ghead[...], ctx[5, 1], TN, preferred_element_type=F32
    ).astype(BF16)

    def head_back(i):
        rows = rows_at(i * MT, MT, MT)
        dstack[rows, :] = jnp.dot(ghead[rows, :], kernels[5][...], preferred_element_type=F32)
        dcur[rows, :] = jnp.dot(ghead[rows, :], kernels[12][...], preferred_element_type=F32)

    loop(PX // MT, head_back)

    def store_current(rows, value):
        dcur[rows, :] = value

    def store_stack(rows, value):
        dstack[rows, :] += value

    for index in range(11, 6, -1):
        work.back(
            index,
            lambda rows: dcur[rows, :],
            lambda rows, index=index: pre[index - 5, rows, :],
            lambda kx, index=index: ctx[index - 7, kx],
            kernels[index],
            grads[index],
            store_current,
        )
    work.back(
        6,
        lambda rows: dcur[rows, :],
        lambda rows: pre[1, rows, :],
        lambda kx: jnp.concatenate([stack[kx], top[kx]], axis=1),
        kernels[6],
        grads[6],
        store_stack,
    )
    work.back(
        4,
        lambda rows: dstack[rows, 4 * LANES :],
        lambda rows: pre[0, rows, :],
        lambda kx: jnp.concatenate([stack[kx], top[kx]], axis=1),
        kernels[4],
        grads[4],
        store_stack,
    )
    bias_out[...] = partial[...].sum(1)


def middle(stack, below, joined, weighting, biases, kernels):
    outs = vmem_call(
        middle_kernel,
        "context",
        [
            jax.ShapeDtypeStruct((8, PX), F32),
            jax.ShapeDtypeStruct((PX, 5 * LANES), F32),
            jax.ShapeDtypeStruct((16, LANES), F32),
            *[jax.ShapeDtypeStruct(k.shape, BF16) for k in kernels],
        ],
        [
            pltpu.VMEM((3, PX, LANES), BF16),
            pltpu.VMEM((6, 3, PX, LANES), BF16),
            pltpu.VMEM((7, PX, LANES), F32),
            pltpu.VMEM((3, PX + 2 * RIM, LANES), F32),
            pltpu.VMEM((3, PX + 2 * RIM, LANES), BF16),
            pltpu.VMEM((PX, LANES), F32),
            pltpu.VMEM((PX, LANES), BF16),
            pltpu.VMEM((16, 8, LANES), F32),
        ],
        56,
        60_000_000_000,
    )(stack, below, joined, weighting, biases, *kernels)
    return outs[0], outs[1], outs[2], outs[3:]


def correlate_back(joined, cost, grads, second, dsecond, collected, out):
    load_second(joined, second)
    dsecond[...] = jnp.zeros_like(dsecond)
    lane = iota((ROWS4, LANES), 1)
    narrow = iota((PW, LANES), 1)

    def body(i):
        rows = rows_at(i * ROWS4, ROWS4, ROWS4)
        own = joined[rows, :]
        first = jnp.where(lane < FC, own.astype(F32), 0.0).astype(BF16)
        grad = grads[rows, :LANES]
        volume = grad * leaky_slope(cost[rows, :]) * (1.0 / FC)
        dfirst = jnp.zeros((ROWS4, LANES), F32)
        for g in range(4):
            pieces = []
            for yy in range(4):
                piece = jnp.zeros((PW, LANES), F32)
                own_rows = volume[yy * PW : (yy + 1) * PW, :]
                for t in range(3 * g, 3 * g + 3):
                    dy = t - yy
                    if dy < 0 or dy >= EXT:
                        continue
                    part = jnp.where(
                        (narrow >= EXT * dy) & (narrow < EXT * (dy + 1)), own_rows, 0.0
                    )
                    shift = (-band_shift(dy, t % 3)) % LANES
                    piece = piece + pltpu.roll(part, shift, 1)
                pieces.append(pltpu.roll(piece, 0, 1, stride=1, stride_axis=0))
            band = jnp.concatenate(pieces, axis=0).astype(BF16)
            at = rows_at((4 * i + 3 * g) * PITCH, LANES)
            dfirst = dfirst + jnp.dot(
                band, second[at, :].astype(BF16), preferred_element_type=F32
            )
            dsecond[at, :] += lax.dot_general(band, first, TN, preferred_element_type=F32)
        direct = pltpu.roll(grad, LANES - NCOST, 1)
        coarse = pltpu.roll(grad, LANES + 2 * FC - NCOST - FC, 1)
        filled = jnp.where(lane < FC, dfirst + direct, 0.0)
        filled = jnp.where((lane >= 2 * FC) & (lane < 2 * FC + 4), coarse, filled)
        collected[rows, :] = filled

    loop(PH // 4, body)
    for s in range((PH - 2 * MARGIN) // 4):
        pieces = []
        for yy in range(4):
            at = (MARGIN + 4 * s + yy + SR) * PITCH + 8
            pieces.append(dsecond[at : at + PW, :])
        other = pltpu.roll(jnp.concatenate(pieces, axis=0), FC, 1)
        start = (MARGIN + 4 * s) * PW
        tile = collected[start : start + ROWS4, :]
        tile = jnp.where((lane >= FC) & (lane < 2 * FC), other, tile)
        out[s] = tile.T[: out.shape[1]].astype(BF16)


def backward_kernel(*refs):
    stack, pre, dstack, cost, joined, bias_in = refs[:6]
    kernels = refs[6:10]
    picture_out, bias_out = refs[10:12]
    grads = refs[12:16]
    moved, dwide, partial, second, dsecond, collected = refs[16:]
    work = Work(None, moved, partial)
    partial[...] = jnp.zeros_like(partial)
    dwide[...] = dstack[:, : 4 * LANES]

    def store_stack(rows, value):
        dwide[rows, : value.shape[1]] += value

    for index in range(3, -1, -1):
        width = LAYERS[index]["blocks"] * LANES

        def load_grad(rows, index=index):
            if index == 3:
                return dstack[rows, 4 * LANES :]
            return dwide[rows, (index + 1) * LANES : (index + 2) * LANES]

        work.back(
            index,
            load_grad,
            lambda rows, index=index: pre[index, rows, :],
            lambda kx, width=width: stack[kx, :, :width],
            kernels[index],
            grads[index],
            store_stack,
        )
    bias_out[...] = partial[...].sum(1) + bias_in[...]
    correlate_back(joined, cost, dwide, second, dsecond, collected, picture_out)


def backward(stack, pre, dstack, cost, joined, bias_grads, kernels, blocks, channels):
    outs = vmem_call(
        backward_kernel,
        "dense_backward",
        [
            jax.ShapeDtypeStruct((blocks, channels, LANES), BF16),
            jax.ShapeDtypeStruct((16, LANES), F32),
            *[jax.ShapeDtypeStruct(k.shape, BF16) for k in kernels],
        ],
        [
            pltpu.VMEM((3, PX + 2 * RIM, LANES), BF16),
            pltpu.VMEM((PX, 4 * LANES), F32),
            pltpu.VMEM((16, 8, LANES), F32),
            pltpu.VMEM((SEC_ROWS, LANES), F32),
            pltpu.VMEM((SEC_ROWS, LANES), F32),
            pltpu.VMEM((PX, LANES), F32),
        ],
        48,
        40_000_000_000,
    )(stack, pre, dstack, cost, joined, bias_grads, *kernels)
    return outs[0], outs[1], outs[2:]


def update(weights, momentum, average, gradient):
    gradient = gradient + DECAY_RATE * weights
    renewed = MOMENTUM_RATE * momentum + gradient
    stepped = weights - LEARN_RATE * (gradient + MOMENTUM_RATE * renewed)
    return (stepped, renewed, AVERAGE_DECAY * average + (1.0 - AVERAGE_DECAY) * stepped)


CHANNELS = 72


def swapped(value, axis, step):
    count = lax.axis_size(axis)
    return lax.ppermute(value, axis, [(i, i ^ step) for i in range(count)])


def added(one, two):
    return (one.astype(F32) + two.astype(F32)).astype(BF16)


def reduced(keep, send, devices, groups, late):
    half = devices // 2
    x_size = groups // 2
    value = added(keep, swapped(send, "grp", 1))
    pieces, size, _ = value.shape
    value = value.reshape(pieces, x_size, size // x_size, LANES)
    value = lax.all_to_all(
        value,
        "grp",
        split_axis=1,
        concat_axis=1,
        axis_index_groups=[[2 * x + c for x in range(x_size)] for c in range(2)],
        tiled=True,
    )
    value = jnp.sum(value.astype(F32), axis=1).astype(BF16)
    value = lax.all_to_all(
        value,
        "dev",
        split_axis=0,
        concat_axis=0,
        axis_index_groups=[list(range(half)), list(range(half, devices))],
        tiled=True,
    )
    value = jnp.sum(value.astype(F32), axis=0)
    far = [(i, i + half) if late else (i + half, i) for i in range(half)]
    return value + lax.ppermute(value.astype(BF16), "dev", far).astype(F32)


def shared_x(value, groups):
    x_size = groups // 2
    x = lax.axis_index("grp") // 2
    held = [0]
    parts = [value]
    step = 1
    while step < x_size:
        parts = parts + [swapped(p, "grp", 2 * step) for p in parts]
        held = held + [j ^ step for j in held]
        step *= 2
    out = []
    for i in range(x_size):
        piece = parts[0]
        for j, part in zip(held[1:], parts[1:]):
            piece = jnp.where((x ^ j) == i, part, piece)
        out.append(piece)
    return jnp.concatenate(out)


def shards(features, coarse_flow, target, valid_mask, weights, momentum, average):
    groups = lax.axis_size("grp")
    devices = lax.axis_size("dev")
    own_rows = features.shape[2]
    width = features.shape[3]
    breadth = width // devices
    height = own_rows * devices
    assert breadth + 2 * MARGIN == PW and height + 2 * MARGIN == PH
    core = lax.axis_index("grp") % 2
    me = lax.axis_index("dev")
    half = devices // 2
    early = me < half
    rows = weights.shape[0] // LANES
    size = -(-(rows // 2) // 32) * 32
    table = weights.reshape(rows, LANES)
    own = lax.dynamic_slice(table, (core * (rows - size), 0), (size, LANES)).astype(BF16)

    marked = valid_mask.astype(BF16)[:, None]
    picture = jnp.concatenate([features, coarse_flow, target, marked], axis=1)[0]
    counts = jnp.sum(valid_mask.astype(F32).reshape(own_rows, -1, PW), axis=1).astype(BF16)
    picture = jnp.pad(picture, ((0, 0), (0, 0), (MARGIN, MARGIN)))
    windows = jnp.stack([picture[:, :, t * breadth : t * breadth + PW] for t in range(devices)])
    counts = jnp.broadcast_to(counts[None, None], (devices, 1, own_rows, PW))
    windows = jnp.concatenate([windows, counts], axis=1)
    received = lax.all_to_all(windows, "dev", split_axis=0, concat_axis=0, tiled=True)

    across = swapped(own, "dev", half)
    both = jnp.stack([core, 1 - core])[:, None] * (rows - size)
    parts = []
    places = []
    for late in range(2):
        part = (jnp.where(early, across, own) if late else jnp.where(early, own, across))[None]
        held = [0]
        step = half // 2
        while step:
            part = jnp.concatenate([part, swapped(part, "dev", step)])
            held = held + [j ^ step for j in held]
            step //= 2
        parts.append((part, swapped(part, "grp", 1)))
        sources = (jnp.array(held, jnp.int32) ^ (me % half)) + half * late
        places.append(sources[None] * rows + both)

    counted = jnp.full((8, LANES), jnp.sum(received[:, CHANNELS - 1].astype(F32)))
    step = 1
    while step < groups:
        counted = counted + swapped(counted, "grp", step)
        step *= 2
    weighting = groups * height * width / counted[:1]
    per = 4 // own_rows
    blocks = devices // per
    received = received.reshape(blocks, per, CHANNELS, own_rows * PW)
    received = jnp.swapaxes(received, 1, 2).reshape(blocks, CHANNELS, LANES)
    received = jnp.pad(received, ((0, 0), (0, LANES - CHANNELS), (0, 0)))

    stack0, cost, joined = correlate(received)
    nothing = jnp.zeros((16, LANES), BF16)
    kernels, biases, carried = unpack(EARLY, 0, half * rows, places[0], parts[0], nothing)
    stack, below, pre = forward(stack0, kernels, biases)
    late_kernels, late_biases, _ = unpack(
        LATE, CUT, devices * rows, places[1], parts[1], carried
    )
    motion, dstack, bias_grads, late_grads = middle(
        stack, below, joined, weighting, late_biases, late_kernels
    )
    flow = motion[:2].reshape(1, 2, PH, PW)[
        :, :, MARGIN : MARGIN + height, MARGIN : MARGIN + breadth
    ]
    pack_at = jnp.arange(half, dtype=jnp.int32)[None] * rows + both
    keep, send, carried = pack(
        LATE, CUT, devices * rows, pack_at + half * rows, late_grads, bias_grads, nothing, half, size
    )
    late_total = reduced(keep, send, devices, groups, True)
    tiles, bias_grads, grads = backward(
        stack, pre, dstack, cost, joined, bias_grads, kernels, blocks, CHANNELS
    )
    keep, send, _ = pack(
        EARLY, 0, half * rows, pack_at, grads, bias_grads, carried, half, size
    )
    early_total = reduced(keep, send, devices, groups, False)
    total = jnp.where(early, early_total, late_total).astype(BF16)
    total = shared_x(total, groups)
    rest = swapped(total, "grp", 1)
    low = jnp.where(core == 0, total, rest)
    high = jnp.where(core == 0, rest, total)
    total_grad = jnp.concatenate([low[: rows - size], high]).astype(F32).reshape(-1)

    tiles = tiles.reshape(blocks, CHANNELS, per, own_rows, PW)
    tiles = jnp.swapaxes(tiles, 1, 2).reshape(devices, CHANNELS, own_rows, PW)
    returned = lax.all_to_all(tiles, "dev", split_axis=0, concat_axis=0, tiled=True)
    returned = returned.astype(F32)
    wide = jnp.transpose(returned, (1, 2, 0, 3))
    centre = wide[..., MARGIN : MARGIN + breadth]
    left = wide[:, :, 1:, :MARGIN]
    right = wide[:, :, :-1, MARGIN + breadth :]
    none = ((0, 0), (0, 0))
    centre = centre + jnp.pad(left, (*none, (0, 1), (breadth - MARGIN, 0)))
    centre = centre + jnp.pad(right, (*none, (1, 0), (0, breadth - MARGIN)))
    row_grad = centre.reshape(1, CHANNELS, own_rows, width)
    feature_grad = row_grad[:, : 2 * FC]
    coarse_grad = row_grad[:, 2 * FC : 2 * FC + 4]

    new_weights, new_momentum, new_average = update(weights, momentum, average, total_grad)
    return (
        flow,
        feature_grad,
        coarse_grad,
        new_weights,
        new_momentum,
        new_average,
        new_weights.astype(BF16),
    )


def solution(mesh):
    in_specs = (
        P("grp", None, "dev", None),
        P("grp", None, "dev", None),
        P("grp", None, "dev", None),
        P("grp", "dev", None),
        P("dev"),
        P("dev"),
        P("dev"),
    )
    out_specs = (
        P("grp", None, None, "dev"),
        P("grp", None, "dev", None),
        P("grp", None, "dev", None),
        P("dev"),
        P("dev"),
        P("dev"),
        P("dev"),
    )
    return jax.shard_map(shards, mesh=mesh, in_specs=in_specs, out_specs=out_specs, check_vma=False)
```

```python
import functools

import jax
import jax.numpy as jnp
from jax import lax
from jax.experimental import pallas as pl
from jax.experimental.pallas import tpu as pltpu
from jax.sharding import PartitionSpec as P

FC = 32
SR = 4
EXT = 2 * SR + 1
NCOST = EXT * EXT
NS0 = NCOST + FC + 4
DENSE = (128, 128, 96, 64, 32)
CONTEXT = (128, 128, 128, 96, 64, 32, 2)
DILATIONS = (1, 2, 4, 8, 16, 1, 1)
MARGIN = 8

SLOPE = 0.1
EPE_EPS = 0.01
MOMENTUM_RATE = 0.5
AVERAGE_DECAY = 0.5
LEARN_RATE = 0.001
DECAY_RATE = 0.0001

LANES = 128
PH = 48
PW = 32
PX = PH * PW
RIM = 16 * PW
STRIP = 128
MT = 768
PITCH = 40
F32 = jnp.float32
BF16 = jnp.bfloat16
NT = (((1,), (1,)), ((), ()))
TN = (((0,), (0,)), ((), ()))


def layer_table():
    places = [(NS0, 0, 0), (128, 1, 0), (128, 2, 0), (96, 3, 0), (64, 4, 0), (32, 4, 64)]
    layers = []
    offset = 0

    def add(pieces, outgoing, dilation, shift):
        nonlocal offset
        incoming = sum(n for n, _, _ in pieces)
        row = 9 * incoming
        segments = []
        at = 0
        for n, block, lane in pieces:
            first, over = 9 * at // LANES, 9 * at % LANES
            slot = -(-(9 * lane - over) // LANES)
            back = 9 * lane - over - LANES * slot
            chunks = -(-(over + 9 * n) // LANES)
            segments.append(
                dict(n=n, block=block, lane=lane, first=first, slot=slot, back=back, chunks=chunks)
            )
            at += n
        blocks = 1 + max(b for _, b, _ in pieces)
        layers.append(
            dict(
                out=outgoing,
                row=row,
                chunks=-(-row // LANES),
                start=offset,
                dil=dilation,
                shift=shift,
                segments=segments,
                blocks=blocks,
                bias=offset + row * outgoing,
                shape=(LANES, blocks * LANES) if outgoing == 2 else (3 * LANES, 3 * blocks * LANES),
            )
        )
        offset += row * outgoing + outgoing

    for i, outgoing in enumerate(DENSE):
        add(places[i::-1], outgoing, 1, 64 if i == 4 else 0)
    add(places[::-1], 2, 1, 0)
    add(places[::-1], CONTEXT[0], DILATIONS[0], 0)
    for i in range(1, 7):
        add([(CONTEXT[i - 1], 0, 0)], CONTEXT[i], DILATIONS[i], 0)
    return layers, offset


LAYERS, COUNT = layer_table()
EARLY = (0, 1, 2, 3)
LATE = (4, 5, 6, 7, 8, 9, 10, 11, 12)
CUT = LAYERS[4]["start"] // LANES // 16 * 16


def sort_groups(indices):
    order = [(segment["back"], i, s) for i in indices for s, segment in enumerate(LAYERS[i]["segments"])]
    order.sort(key=lambda t: -t[0])
    at = 0
    groups = {}
    classes = []
    for back, i, s in order:
        if not classes or classes[-1][0] != back:
            classes.append([back, at, at])
        groups[i, s] = at
        at += -(-LAYERS[i]["out"] // 16) * 16
        classes[-1][2] = at
    return groups, classes, at


def iota(shape, dim):
    return lax.broadcasted_iota(jnp.int32, shape, dim)


def rows_at(start, size, step=8):
    if isinstance(start, int):
        return pl.ds(start, size)
    return pl.ds(pl.multiple_of(start, step), size)


def sigmoid(v):
    return 0.5 * jnp.tanh(0.5 * v) + 0.5


def leaky(v):
    return SLOPE * v + (1.0 - SLOPE) * v * sigmoid(v)


def leaky_slope(v):
    s = sigmoid(v)
    return SLOPE + (1.0 - SLOPE) * (s + v * s * (1.0 - s))


def loop(count, body):
    def step(i, carry):
        body(i)
        return carry

    lax.fori_loop(0, count, step, 0)


def fill_order(order):
    order[:LANES, :] = jnp.zeros((LANES, 9 * LANES), BF16)
    order[10 * LANES :, :] = jnp.zeros((LANES, 9 * LANES), BF16)
    for k in range(9):
        for m in range(9):
            row = iota((LANES, LANES), 0) + m * LANES
            col = iota((LANES, LANES), 1)
            order[(m + 1) * LANES : (m + 2) * LANES, k * LANES : (k + 1) * LANES] = jnp.where(
                row == 9 * col + k, 1.0, 0.0
            ).astype(BF16)


ORDER = pltpu.VMEM((11 * LANES, 9 * LANES), BF16)


def within(n, lane):
    spot = iota((1, LANES), 1)
    return jnp.where((spot >= lane) & (spot < lane + n), 1.0, 0.0).astype(BF16)


def pitch_of(chunks):
    return -(-chunks // 8) * 8


def unpack_scratch(indices, count):
    _, _, group_rows = sort_groups(indices)
    return (
        pltpu.VMEM((count + 64, LANES), F32),
        pltpu.VMEM((48 * LANES, LANES), F32),
        pltpu.VMEM((group_rows, 10 * LANES), BF16),
        pltpu.VMEM((group_rows, 9 * LANES), BF16),
        pltpu.VMEM((LANES, 5 * LANES), F32),
    )


def unpack_weights(indices, base, place_at, parts, carried, outs, bias_out, carry_out, order, scratch):
    whole, slabs, aligned, result, heads = scratch
    count = whole.shape[0] - 64
    groups, classes, _ = sort_groups(indices)
    if base:
        whole[: carried.shape[0], :] = carried[...].astype(F32)
    for at_part, part in enumerate(parts):
        size = part.shape[1]
        for j in range(part.shape[0]):
            to = place_at[at_part, j] - base

            def widen(i, part=part, j=j, to=to):
                whole[pl.ds(to + i * 16, 16), :] = part[j, rows_at(i * 16, 16, 16), :].astype(F32)

            lax.fori_loop(0, size // 16, lambda i, c: (widen(i), c)[1], 0, unroll=8)
    whole[count:, :] = jnp.zeros((64, LANES), F32)
    if not base:
        carry_out[...] = whole[CUT:count, :].astype(BF16)
    bias_out[...] = jnp.zeros_like(bias_out)

    for at_out, index in enumerate(indices):
        layer = LAYERS[index]
        outgoing = layer["out"]
        kept = -(-outgoing // 16) * 16
        start = layer["start"] - base * LANES
        spot = iota((kept, LANES), 1)
        pitch = pitch_of(layer["chunks"] + 1)
        still = layer["row"] % LANES == 0
        if not still:
            unroll = min(32, outgoing)

            def take(i, unroll=unroll, row=layer["row"], start=start, pitch=pitch):
                for u in range(unroll):
                    o = i * unroll + u
                    first = start + o * row
                    turn = (LANES - (first & (LANES - 1))) & (LANES - 1)
                    for v in range(pitch // 8):
                        tile = whole[pl.ds((first >> 7) + 8 * v, 8), :]
                        slabs[rows_at(o * pitch + 8 * v, 8), :] = pltpu.roll(tile, turn, 1)

            loop(outgoing // unroll, take)
            off = (start + iota((kept, LANES), 0) * layer["row"]) & (LANES - 1)
        chunks = {}
        for t in range(layer["chunks"]):
            if still:
                row, fixed = divmod(start, LANES)
                step = layer["row"] // LANES
                here = whole[pl.ds(row + t, kept, stride=step), :]
                after = whole[pl.ds(row + t + 1, kept, stride=step), :]
                chunk = jnp.where(spot >= fixed, here, after)
                chunk = pltpu.roll(chunk, (LANES - fixed) % LANES, 1)
            else:
                here = slabs[pl.ds(t, kept, stride=pitch), :]
                after = slabs[pl.ds(t + 1, kept, stride=pitch), :]
                chunk = jnp.where(spot < LANES - off, here, after)
            chunk = chunk.astype(BF16)
            for s, segment in enumerate(layer["segments"]):
                to = t - segment["first"]
                if 0 <= to < segment["chunks"]:
                    to += segment["slot"]
                    at = groups[index, s]
                    aligned[at : at + kept, to * LANES : (to + 1) * LANES] = chunk
        for s, segment in enumerate(layer["segments"]):
            at = groups[index, s]
            for to in range(10):
                if not segment["slot"] <= to < segment["slot"] + segment["chunks"]:
                    aligned[at : at + kept, to * LANES : (to + 1) * LANES] = jnp.zeros(
                        (kept, LANES), BF16
                    )
        shift = layer["shift"]
        first = layer["bias"] - base * LANES - shift
        row, fixed = divmod(first, LANES)
        here = pltpu.roll(whole[row : row + 1, :], (LANES - fixed) % LANES, 1)
        after = pltpu.roll(whole[row + 1 : row + 2, :], (LANES - fixed) % LANES, 1)
        line = iota((1, LANES), 1)
        value = jnp.where(line < LANES - fixed, here, after)
        bias_out[index : index + 1, :] = jnp.where(
            (line >= shift) & (line < shift + outgoing), value, 0.0
        )

    for back, low, high in classes:
        wide = 9 if back == 0 else 10
        result[low:high, :] = jnp.dot(
            aligned[low:high, : wide * LANES],
            order[LANES + back : LANES + back + wide * LANES, :],
            preferred_element_type=F32,
        ).astype(BF16)

    for at_out, index in enumerate(indices):
        layer = LAYERS[index]
        outgoing = layer["out"]
        shift = layer["shift"]
        out = outs[at_out]
        width = layer["blocks"] * LANES
        if outgoing == 2:
            heads[...] = jnp.zeros_like(heads)
        elif outgoing < LANES:
            out[...] = jnp.zeros_like(out)
        kept = -(-outgoing // 16) * 16
        for block in range(layer["blocks"]):
            for k in range(9):
                total = None
                for s, segment in enumerate(layer["segments"]):
                    if segment["block"] != block:
                        continue
                    at = groups[index, s]
                    tile = result[at : at + kept, k * LANES : (k + 1) * LANES]
                    if segment["n"] < LANES:
                        tile = tile * within(segment["n"], segment["lane"])
                    total = tile if total is None else total + tile
                if outgoing == 2:
                    heads[2 * k : 2 * k + 2, block * LANES : (block + 1) * LANES] = total.astype(
                        F32
                    )[:2]
                else:
                    ky, kx = divmod(k, 3)
                    at = kx * width + block * LANES
                    out[ky * LANES + shift : ky * LANES + shift + outgoing, at : at + LANES] = total
        if outgoing == 2:
            out[...] = heads[:, :width].astype(BF16)


def pack_scratch(indices, count):
    _, _, group_rows = sort_groups(indices)
    return (
        pltpu.VMEM((count + 64, LANES), F32),
        pltpu.VMEM((40 * LANES + 64, LANES), F32),
        pltpu.VMEM((group_rows, 9 * LANES), BF16),
        pltpu.VMEM((group_rows, 10 * LANES), F32),
        pltpu.VMEM((LANES + 16, 5 * LANES), F32),
    )


def pack_gradients(indices, base, place_at, grads, bias_in, carried, halves, carry_out, order, scratch):
    whole, slabs, gathered, result, heads = scratch
    count = whole.shape[0] - 64
    groups, classes, _ = sort_groups(indices)
    for at_in, index in enumerate(indices):
        layer = LAYERS[index]
        outgoing = layer["out"]
        shift = layer["shift"]
        grad = grads[at_in]
        width = layer["blocks"] * LANES
        if outgoing == 2:
            heads[:LANES, :width] = grad[...].astype(F32)
            heads[LANES:, :] = jnp.zeros((16, heads.shape[1]), F32)
        for s, segment in enumerate(layer["segments"]):
            at = groups[index, s]
            block = segment["block"]
            for k in range(9):
                if outgoing == 2:
                    tile = heads[2 * k : 2 * k + 16, block * LANES : (block + 1) * LANES]
                    tile = tile.astype(BF16)
                else:
                    ky, kx = divmod(k, 3)
                    column = kx * width + block * LANES
                    tile = grad[
                        ky * LANES + shift : ky * LANES + shift + outgoing, column : column + LANES
                    ]
                if segment["n"] < LANES:
                    tile = tile * within(segment["n"], segment["lane"])
                gathered[at : at + tile.shape[0], k * LANES : (k + 1) * LANES] = tile

    for back, low, high in classes:
        wide = 9 if back == 0 else 10
        result[low:high, : wide * LANES] = lax.dot_general(
            gathered[low:high, :],
            order[LANES + back : LANES + back + wide * LANES, :],
            NT,
            preferred_element_type=F32,
        )

    lane = iota((8, LANES), 1)
    sub = iota((8, LANES), 0)

    for at_in, index in enumerate(indices):
        layer = LAYERS[index]
        outgoing = layer["out"]
        start = layer["start"] - base * LANES
        still = layer["row"] % LANES == 0
        pitch = pitch_of(layer["chunks"])
        spot = iota((outgoing, LANES), 1)
        turned = []
        for t in range(layer["chunks"]):
            chunk = None
            for s, segment in enumerate(layer["segments"]):
                to = t - segment["first"]
                if 0 <= to < segment["chunks"]:
                    to += segment["slot"]
                    at = groups[index, s]
                    tile = result[at : at + outgoing, to * LANES : (to + 1) * LANES]
                    chunk = tile if chunk is None else chunk + tile
            if still:
                turned.append(pltpu.roll(chunk, start % LANES, 1))
            else:
                slabs[pl.ds(t, outgoing, stride=pitch), :] = chunk
        if still:
            row, fixed = divmod(start, LANES)
            step = layer["row"] // LANES
            for t in range(step):
                before = turned[t - 1] if t else pltpu.roll(turned[-1], 1, 0)
                value = jnp.where(spot >= fixed, turned[t], before)
                if t == 0:
                    kept = whole[row : row + 1, :]
                    top = (iota((outgoing, LANES), 0) == 0) & (spot < fixed)
                    value = jnp.where(top, kept, value)
                whole[pl.ds(row + t, outgoing, stride=step), :] = value
            last = pltpu.roll(turned[-1][outgoing - 8 :, :], 1, 0)
            end = row + step * outgoing
            pltpu.store(whole.at[end : end + 8, :], last, mask=(sub == 0) & (lane < fixed))
        else:
            unroll = min(32, outgoing)

            def put(i, start=start, row=layer["row"], pitch=pitch, unroll=unroll):
                for u in range(unroll):
                    o = i * unroll + u
                    first = start + o * row
                    off = first & (LANES - 1)
                    for v in range(pitch // 8):
                        tile = pltpu.roll(slabs[rows_at(o * pitch + 8 * v, 8), :], off, 1)
                        to = (first >> 7) + 8 * v
                        pltpu.store(whole.at[pl.ds(to, 8), :], tile, mask=lane >= off)
                        pltpu.store(whole.at[pl.ds(to + 1, 8), :], tile, mask=lane < off)

            loop(outgoing // unroll, put)
        line = bias_in[index : index + 1, :]
        first = layer["bias"] - base * LANES
        row, fixed = divmod(first, LANES)
        line = pltpu.roll(line, (fixed - layer["shift"]) % LANES, 1)
        line = jnp.broadcast_to(line, (8, LANES))
        pltpu.store(whole.at[row : row + 8, :], line, mask=(sub == 0) & (lane >= fixed))
        pltpu.store(whole.at[row + 1 : row + 9, :], line, mask=(sub == 0) & (lane < fixed))
    if base:
        end, off = divmod(COUNT - base * LANES, LANES)
        pltpu.store(
            whole.at[end : end + 8, :], jnp.zeros((8, LANES), F32), mask=(sub > 0) | (lane >= off)
        )
        if count > end + 8:
            whole[end + 8 : count, :] = jnp.zeros((count - end - 8, LANES), F32)
        carry_out[...] = whole[: carry_out.shape[0], :].astype(BF16)
    else:
        end, off = divmod(LAYERS[4]["start"], LANES)
        line = carried[...].astype(F32)
        keep = (iota(line.shape, 0) > end - CUT) | (
            (iota(line.shape, 0) == end - CUT) & (iota(line.shape, 1) >= off)
        )
        whole[CUT:count, :] = jnp.where(keep, line, whole[CUT:count, :])
    for half in range(2):
        size = halves[half].shape[1]
        for j in range(halves[half].shape[0]):
            begin = place_at[half, j] - base

            def narrow(i, half=half, j=j, begin=begin):
                halves[half][j, rows_at(i * 16, 16, 16), :] = whole[
                    pl.ds(begin + i * 16, 16), :
                ].astype(BF16)

            lax.fori_loop(0, size // 16, lambda i, c: (narrow(i), c)[1], 0, unroll=8)


def pack_kernel(place_at, *refs):
    grads = refs[:4]
    bias_in, carried = refs[4:6]
    halves = refs[6:8]
    order = refs[8]
    fill_order(order)
    pack_gradients(EARLY, 0, place_at, grads, bias_in, carried, halves, None, order, refs[9:])


def pack(place_at, grads, bias, carried, count, pieces, size):
    return pl.pallas_call(
        pack_kernel,
        out_shape=[jax.ShapeDtypeStruct((pieces, size, LANES), BF16)] * 2,
        in_specs=[pl.BlockSpec(memory_space=pltpu.SMEM)]
        + [pl.BlockSpec(memory_space=pltpu.VMEM)] * 6,
        scratch_shapes=[ORDER, *pack_scratch(EARLY, count)],
        compiler_params=pltpu.CompilerParams(vmem_limit_bytes=40 * 2**20),
        cost_estimate=pl.CostEstimate(
            flops=12_000_000_000, bytes_accessed=8_000_000, transcendentals=0
        ),
        name="pack_gradients",
    )(place_at, *grads, bias, carried)


ROWS4 = 4 * PW
SEC_ROWS = (PH + 2 * SR) * PITCH + LANES


def load_second(joined, second):
    second[...] = jnp.zeros_like(second)
    keep = iota((PW, LANES), 1) < FC
    for y in range(MARGIN, PH - MARGIN):
        row = joined[y * PW : (y + 1) * PW, :].astype(F32)
        row = jnp.where(keep, pltpu.roll(row, LANES - FC, 1), 0.0)
        at = (y + SR) * PITCH + 8
        second[at : at + PW, :] = row


def band_shift(dy, third):
    return EXT * dy - PITCH * third - (8 - SR)


def correlate_kernel(received, stack0, cost, joined, second):
    joined[...] = jnp.zeros_like(joined)
    blocks = received.shape[0]
    for s in range(blocks):
        tile = received[s].astype(F32).T
        joined[RIM // 2 + s * ROWS4 : RIM // 2 + (s + 1) * ROWS4, :] = tile.astype(BF16)
    load_second(joined, second)
    row = iota((ROWS4, ROWS4), 0)
    col = iota((ROWS4, ROWS4), 1)
    flip = jnp.where((row // PW == col // PW) & (row % PW + col % PW == PW - 1), 1.0, 0.0).astype(
        BF16
    )
    lane = iota((ROWS4, LANES), 1)
    narrow = iota((PW, LANES), 1)

    def body(i):
        own = joined[rows_at(i * ROWS4, ROWS4, ROWS4), :]
        first = jnp.where(lane < FC, own.astype(F32), 0.0).astype(BF16)
        first = jnp.dot(flip, first, preferred_element_type=F32).astype(BF16)
        bands = []
        for g in range(4):
            window = second[rows_at((4 * i + 3 * g) * PITCH, LANES), :].astype(BF16)
            bands.append(lax.dot_general(first, window, NT, preferred_element_type=F32))
        pieces = []
        for yy in range(4):
            total = jnp.zeros((PW, LANES), F32)
            turned = [
                pltpu.roll(band[yy * PW : (yy + 1) * PW, :], 0, 1, stride=1, stride_axis=0)
                for band in bands
            ]
            for dy in range(EXT):
                t = yy + dy
                shift = (band_shift(dy, t % 3) - (PW - 1)) % LANES
                band = pltpu.roll(turned[t // 3], shift, 1)
                total = jnp.where((narrow >= EXT * dy) & (narrow < EXT * (dy + 1)), band, total)
            pieces.append(total * (1.0 / FC))
        total = jnp.concatenate(pieces, axis=0)
        high = total.astype(BF16)
        low = (total - high.astype(F32)).astype(BF16)
        total = jnp.dot(flip, high, preferred_element_type=F32) + jnp.dot(
            flip, low, preferred_element_type=F32
        )
        cost[rows_at(i * ROWS4, ROWS4, ROWS4), :] = total
        wide = own.astype(F32)
        filled = jnp.where(lane < NCOST, leaky(total), pltpu.roll(wide, NCOST, 1))
        coarse = pltpu.roll(wide, NCOST + FC - 2 * FC, 1)
        filled = jnp.where(lane >= NCOST + FC, coarse, filled)
        filled = jnp.where(lane < NS0, filled, 0.0)
        stack0[rows_at(i * ROWS4, ROWS4, ROWS4), :] = filled.astype(BF16)

    loop(PH // 4, body)


def correlate(received):
    return pl.pallas_call(
        correlate_kernel,
        out_shape=[
            jax.ShapeDtypeStruct((PX, LANES), BF16),
            jax.ShapeDtypeStruct((PX, LANES), F32),
            jax.ShapeDtypeStruct((PX, LANES), BF16),
        ],
        scratch_shapes=[pltpu.VMEM((SEC_ROWS, LANES), F32)],
        compiler_params=pltpu.CompilerParams(vmem_limit_bytes=32 * 2**20),
        name="correlate",
    )(received)


class Work:
    def __init__(self, taps, moved, partial):
        self.taps = taps
        self.moved = moved
        self.partial = partial
        self.column = iota((STRIP, LANES), 0) % PW
        self.lane = iota((STRIP, LANES), 1)
        if taps is not None:
            taps[:, :RIM, :] = jnp.zeros((3, RIM, LANES), F32)
            taps[:, RIM + PX :, :] = jnp.zeros((3, RIM, LANES), F32)
        if moved is not None:
            moved[:, :RIM, :] = jnp.zeros((3, RIM, LANES), BF16)
            moved[:, RIM + PX :, :] = jnp.zeros((3, RIM, LANES), BF16)

    def strips(self, body):
        for at in range(0, PX, STRIP):
            body(pl.ds(at, STRIP), at)

    def inside(self, tile, shift):
        if shift == 0:
            return tile
        valid = (self.column + shift >= 0) & (self.column + shift < PW)
        return jnp.where(valid, pltpu.roll(tile, (-shift) % STRIP, 0), 0.0)

    def spread(self, store, tile, dilation):
        for kx in range(3):
            store(kx, self.inside(tile, (kx - 1) * dilation).astype(BF16))

    def multiply(self, load, kernel):
        def body(i):
            rows = rows_at(i * MT, MT, MT)
            value = jnp.concatenate([load(kx, rows) for kx in range(3)], axis=1)
            product = lax.dot_general(value, kernel[...], NT, preferred_element_type=F32)
            for ky in range(3):
                self.taps[ky, rows_at(RIM + i * MT, MT, MT), :] = product[
                    :, ky * LANES : (ky + 1) * LANES
                ]

        for i in range(PX // MT):
            body(i)

    def collect(self, at, dilation):
        total = None
        for ky in range(3):
            tile = self.taps[ky, rows_at(RIM + at + (ky - 1) * dilation * PW, STRIP, PW), :]
            total = tile if total is None else total + tile
        return total

    def spread_grad(self, at, grad, dilation):
        for kx in range(3):
            self.moved[kx, rows_at(RIM + at, STRIP, STRIP), :] = self.inside(
                grad, -(kx - 1) * dilation
            ).astype(BF16)

    def count_bias(self, index, grad):
        self.partial[index] += grad.reshape(STRIP // 8, 8, LANES).sum(0)

    def back(self, index, load_grad, load_pre, load_input, kernel, out, store):
        layer = LAYERS[index]
        dilation = layer["dil"]
        width = layer["blocks"] * LANES

        def through(rows, at):
            grad = load_grad(rows) * leaky_slope(load_pre(rows))
            grad = grad.astype(BF16).astype(F32)
            self.count_bias(index, grad)
            self.spread_grad(at, grad, dilation)

        self.strips(through)
        grad = jnp.concatenate(
            [
                self.moved[1, RIM - (ky - 1) * dilation * PW : RIM - (ky - 1) * dilation * PW + PX, :]
                for ky in range(3)
            ],
            axis=1,
        )
        for kx in range(3):
            out[:, kx * width : (kx + 1) * width] = lax.dot_general(
                grad, load_input(kx), TN, preferred_element_type=F32
            ).astype(BF16)

        def input_grad(i):
            tiles = [
                self.moved[kx, rows_at(RIM + i * MT - (ky - 1) * dilation * PW, MT, PW), :]
                for ky in range(3)
                for kx in range(3)
            ]
            weights = [
                kernel[ky * LANES : (ky + 1) * LANES, kx * width : (kx + 1) * width]
                for ky in range(3)
                for kx in range(3)
            ]
            store(
                rows_at(i * MT, MT, MT),
                jnp.dot(
                    jnp.concatenate(tiles, axis=1),
                    jnp.concatenate(weights, axis=0),
                    preferred_element_type=F32,
                ),
            )

        for i in range(PX // MT):
            input_grad(i)


def forward_kernel(place_at, own, other, stack0, *refs):
    kernels = refs[:4]
    biases, carry_out, stack, top, pre, order, taps = refs[4:11]
    fill_order(order)
    unpack_weights(
        EARLY, 0, place_at, (own, other), None, kernels, biases, carry_out, order, refs[11:]
    )
    work = Work(taps, None, None)

    def first(rows, at):
        tile = stack0[rows, :].astype(F32)

        def keep(kx, value):
            stack[kx, rows, :LANES] = value

        work.spread(keep, tile, 1)

    work.strips(first)
    for index, kernel in enumerate(kernels):
        width = LAYERS[index]["blocks"] * LANES
        work.multiply(lambda kx, rows, width=width: stack[kx, rows, :width], kernel)

        def finish(rows, at, index=index):
            value = work.collect(at, 1) + biases[index : index + 1, :]
            pre[index, rows, :] = value
            place = slice((index + 1) * LANES, (index + 2) * LANES)

            def keep(kx, value):
                if index == 3:
                    top[kx, rows, :] = value
                else:
                    stack[kx, rows, place] = value

            work.spread(keep, leaky(value), 1)

        work.strips(finish)


def forward(place_at, parts, stack0, count):
    outs = pl.pallas_call(
        forward_kernel,
        out_shape=[jax.ShapeDtypeStruct(LAYERS[i]["shape"], BF16) for i in EARLY]
        + [
            jax.ShapeDtypeStruct((16, LANES), F32),
            jax.ShapeDtypeStruct((count - CUT, LANES), BF16),
            jax.ShapeDtypeStruct((3, PX, 4 * LANES), BF16),
            jax.ShapeDtypeStruct((3, PX, LANES), BF16),
            jax.ShapeDtypeStruct((4, PX, LANES), F32),
        ],
        in_specs=[pl.BlockSpec(memory_space=pltpu.SMEM)]
        + [pl.BlockSpec(memory_space=pltpu.VMEM)] * 3,
        scratch_shapes=[
            ORDER,
            pltpu.VMEM((3, PX + 2 * RIM, LANES), F32),
            *unpack_scratch(EARLY, count),
        ],
        compiler_params=pltpu.CompilerParams(vmem_limit_bytes=52 * 2**20),
        cost_estimate=pl.CostEstimate(
            flops=25_000_000_000, bytes_accessed=20_000_000, transcendentals=0
        ),
        name="dense_forward",
    )(place_at, *parts, stack0)
    return outs[:4], *outs[5:]


def late_kernel(
    rows,
    gather_at,
    pack_at,
    own,
    other,
    carried,
    stack_in,
    below_in,
    joined_in,
    weighting,
    motion_out,
    dstack_out,
    bias_out,
    keep,
    send,
    carry_out,
    order,
    biases,
    dstack,
    stack,
    below,
    joined,
    copied,
    *refs,
):
    kernels = refs[:9]
    grads = refs[9:]
    loads = [
        pltpu.make_async_copy(source, target, copied.at[i])
        for i, (source, target) in enumerate(zip((stack_in, below_in, joined_in), (stack, below, joined)))
    ]
    for load in loads:
        load.start()
    fill_order(order)

    def first(*scratch):
        unpack_weights(
            LATE, CUT, gather_at, (own, other), carried, kernels, biases, None, order, scratch
        )

    pl.run_scoped(first, *unpack_scratch(LATE, rows))
    for load in loads:
        load.wait()

    def second(*scratch):
        context(
            stack, below, joined, weighting, biases, kernels, motion_out, dstack, bias_out, grads, *scratch
        )

    pl.run_scoped(second, *CONTEXT_SCRATCH)
    store = pltpu.make_async_copy(dstack, dstack_out, copied.at[3])
    store.start()

    def third(*scratch):
        pack_gradients(
            LATE, CUT, pack_at, grads, bias_out, None, (keep, send), carry_out, order, scratch
        )

    pl.run_scoped(third, *pack_scratch(LATE, rows))
    store.wait()


def context(
    stack, below, joined, weighting, biases, kernels, motion_out, dstack, bias_out, grads, *scratch
):
    kernels = dict(zip(LATE, kernels))
    grads = dict(zip(LATE, grads))
    top, ctx, pre, taps, moved, dcur, ghead, partial = scratch
    work = Work(taps, moved, partial)
    partial[...] = jnp.zeros_like(partial)
    lane = work.lane

    def wide(kx, rows):
        return jnp.concatenate([stack[kx, rows, :], top[kx, rows, :]], axis=1)

    work.multiply(
        lambda kx, rows: jnp.concatenate([stack[kx, rows, :], below[kx, rows, :]], axis=1),
        kernels[4],
    )

    def finish_top(rows, at):
        value = work.collect(at, 1) + biases[4:5, :]
        pre[0, rows, :] = value

        def keep(kx, value):
            top[kx, rows, :] = value + below[kx, rows, :]

        work.spread(keep, leaky(value), 1)

    work.strips(finish_top)
    for index in range(6, 12):
        if index == 6:
            work.multiply(wide, kernels[index])
        else:
            work.multiply(lambda kx, rows, index=index: ctx[index - 7, kx, rows, :], kernels[index])

        def finish(rows, at, index=index):
            value = work.collect(at, LAYERS[index]["dil"]) + biases[index : index + 1, :]
            pre[index - 5, rows, :] = value

            def keep(kx, value):
                ctx[index - 6, kx, rows, :] = value

            work.spread(keep, leaky(value), LAYERS[index + 1]["dil"])

        work.strips(finish)

    def head(i):
        rows = rows_at(i * MT, MT, MT)
        product = lax.dot_general(wide(1, rows), kernels[5][...], NT, preferred_element_type=F32)
        product = product + lax.dot_general(
            ctx[5, 1, rows, :], kernels[12][...], NT, preferred_element_type=F32
        )
        taps[0, rows_at(RIM + i * MT, MT, MT), :] = product

    for i in range(PX // MT):
        head(i)

    row = iota((LANES, LANES), 0)
    col = iota((LANES, LANES), 1)
    used = (col < 18) & (row % 2 == col % 2)
    fold = jnp.where(used & (row < 18), 1.0, 0.0)
    copies = jnp.where(used & (row < 2), 1.0, 0.0).astype(BF16)
    pick = jnp.where(used & (row >= 2 * FC + 4) & (row < 2 * FC + 6), 1.0, 0.0).astype(BF16)
    marked = jnp.where(row == 2 * FC + 6, 1.0, 0.0).astype(BF16)
    shared = sum(
        jnp.dot(jnp.broadcast_to(b, (8, LANES)).astype(BF16), copies, preferred_element_type=F32)
        for b in (biases[5:6, :], biases[12:13, :])
    )[:1]

    def settle(rows, at):
        total = None
        for kx in range(3):
            part = None
            for ky in range(3):
                tile = taps[0, rows_at(RIM + at + (ky - 1) * PW, STRIP, PW), :]
                tile = jnp.where(lane // 2 == ky * 3 + kx, tile, 0.0)
                part = tile if part is None else part + tile
            part = work.inside(part, kx - 1)
            total = part if total is None else total + part
        motion = (
            jnp.dot(total, fold, preferred_element_type=F32, precision=lax.Precision.HIGHEST)
            + shared
        )
        motion_out[:, rows] = motion.T[: motion_out.shape[0]]
        own = joined[rows, :]
        aim = jnp.dot(own, pick, preferred_element_type=F32)
        mask = jnp.dot(own, marked, preferred_element_type=F32)
        mismatch = motion - aim
        square = mismatch * mismatch
        other = jnp.where(
            lane % 2 == 0, pltpu.roll(square, LANES - 1, 1), pltpu.roll(square, 1, 1)
        )
        length = jnp.sqrt(square + other + EPE_EPS)
        height = (iota((STRIP, LANES), 0) + at) // PW
        interior = (
            (height >= MARGIN)
            & (height < PH - MARGIN)
            & (work.column >= MARGIN)
            & (work.column < PW - MARGIN)
            & (lane < 18)
        )
        grad = jnp.where(interior, weighting[...] * mask * mismatch / length, 0.0)
        grad = grad.astype(BF16).astype(F32)
        work.count_bias(5, grad)
        work.spread_grad(at, grad, 1)

    work.strips(settle)
    partial[12] = partial[5]

    def choose(rows, at):
        total = None
        for kx in range(3):
            for ky in range(3):
                tile = moved[kx, rows_at(RIM + at - (ky - 1) * PW, STRIP, PW), :].astype(F32)
                tile = jnp.where(lane // 2 == ky * 3 + kx, tile, 0.0)
                total = tile if total is None else total + tile
        ghead[rows, :] = total.astype(BF16)

    work.strips(choose)
    grads[5][:, : 4 * LANES] = lax.dot_general(
        ghead[...], stack[1], TN, preferred_element_type=F32
    ).astype(BF16)
    grads[5][:, 4 * LANES :] = lax.dot_general(
        ghead[...], top[1], TN, preferred_element_type=F32
    ).astype(BF16)
    grads[12][...] = lax.dot_general(
        ghead[...], ctx[5, 1], TN, preferred_element_type=F32
    ).astype(BF16)

    def head_back(i):
        rows = rows_at(i * MT, MT, MT)
        dstack[rows, :] = jnp.dot(ghead[rows, :], kernels[5][...], preferred_element_type=F32)
        dcur[rows, :] = jnp.dot(ghead[rows, :], kernels[12][...], preferred_element_type=F32)

    for i in range(PX // MT):
        head_back(i)

    def store_current(rows, value):
        dcur[rows, :] = value

    def store_stack(rows, value):
        dstack[rows, :] += value

    for index in range(11, 6, -1):
        work.back(
            index,
            lambda rows: dcur[rows, :],
            lambda rows, index=index: pre[index - 5, rows, :],
            lambda kx, index=index: ctx[index - 7, kx],
            kernels[index],
            grads[index],
            store_current,
        )
    work.back(
        6,
        lambda rows: dcur[rows, :],
        lambda rows: pre[1, rows, :],
        lambda kx: jnp.concatenate([stack[kx], top[kx]], axis=1),
        kernels[6],
        grads[6],
        store_stack,
    )
    work.back(
        4,
        lambda rows: dstack[rows, 4 * LANES :],
        lambda rows: pre[0, rows, :],
        lambda kx: jnp.concatenate([stack[kx], top[kx]], axis=1),
        kernels[4],
        grads[4],
        store_stack,
    )
    bias_out[...] = partial[...].sum(1)


CONTEXT_SCRATCH = (
    pltpu.VMEM((3, PX, LANES), BF16),
    pltpu.VMEM((6, 3, PX, LANES), BF16),
    pltpu.VMEM((7, PX, LANES), F32),
    pltpu.VMEM((3, PX + 2 * RIM, LANES), F32),
    pltpu.VMEM((3, PX + 2 * RIM, LANES), BF16),
    pltpu.VMEM((PX, LANES), F32),
    pltpu.VMEM((PX, LANES), BF16),
    pltpu.VMEM((16, 8, LANES), F32),
)


def late(gather_at, pack_at, parts, carried, stack, below, joined, weighting, end, pieces, size):
    smem = pl.BlockSpec(memory_space=pltpu.SMEM)
    vmem = pl.BlockSpec(memory_space=pltpu.VMEM)
    anywhere = pl.BlockSpec(memory_space=pl.ANY)
    shapes = [pltpu.VMEM(LAYERS[i]["shape"], BF16) for i in LATE]
    return pl.pallas_call(
        functools.partial(late_kernel, end - CUT),
        out_shape=[
            jax.ShapeDtypeStruct((8, PX), F32),
            jax.ShapeDtypeStruct((PX, 5 * LANES), F32),
            jax.ShapeDtypeStruct((16, LANES), F32),
            jax.ShapeDtypeStruct((pieces, size, LANES), BF16),
            jax.ShapeDtypeStruct((pieces, size, LANES), BF16),
            jax.ShapeDtypeStruct((end // 2 - CUT, LANES), BF16),
        ],
        in_specs=[smem] * 2 + [vmem] * 3 + [anywhere] * 3 + [vmem],
        out_specs=[vmem, anywhere, vmem, vmem, vmem, vmem],
        scratch_shapes=[
            ORDER,
            pltpu.VMEM((16, LANES), F32),
            pltpu.VMEM((PX, 5 * LANES), F32),
            pltpu.VMEM(stack.shape, BF16),
            pltpu.VMEM(below.shape, BF16),
            pltpu.VMEM(joined.shape, BF16),
            pltpu.SemaphoreType.DMA((4,)),
            *shapes,
            *shapes,
        ],
        compiler_params=pltpu.CompilerParams(vmem_limit_bytes=60 * 2**20),
        cost_estimate=pl.CostEstimate(
            flops=80_000_000_000, bytes_accessed=20_000_000, transcendentals=0
        ),
        name="context",
    )(gather_at, pack_at, *parts, carried, stack, below, joined, weighting)


def correlate_back(joined, cost, grads, second, dsecond, collected, out):
    load_second(joined, second)
    dsecond[...] = jnp.zeros_like(dsecond)
    lane = iota((ROWS4, LANES), 1)
    narrow = iota((PW, LANES), 1)

    def body(i):
        rows = rows_at(i * ROWS4, ROWS4, ROWS4)
        own = joined[rows, :]
        first = jnp.where(lane < FC, own.astype(F32), 0.0).astype(BF16)
        grad = grads[rows, :LANES]
        volume = grad * leaky_slope(cost[rows, :]) * (1.0 / FC)
        dfirst = jnp.zeros((ROWS4, LANES), F32)
        for g in range(4):
            pieces = []
            for yy in range(4):
                piece = jnp.zeros((PW, LANES), F32)
                own_rows = volume[yy * PW : (yy + 1) * PW, :]
                for t in range(3 * g, 3 * g + 3):
                    dy = t - yy
                    if dy < 0 or dy >= EXT:
                        continue
                    part = jnp.where(
                        (narrow >= EXT * dy) & (narrow < EXT * (dy + 1)), own_rows, 0.0
                    )
                    shift = (-band_shift(dy, t % 3)) % LANES
                    piece = piece + pltpu.roll(part, shift, 1)
                pieces.append(pltpu.roll(piece, 0, 1, stride=1, stride_axis=0))
            band = jnp.concatenate(pieces, axis=0).astype(BF16)
            at = rows_at((4 * i + 3 * g) * PITCH, LANES)
            dfirst = dfirst + jnp.dot(
                band, second[at, :].astype(BF16), preferred_element_type=F32
            )
            dsecond[at, :] += lax.dot_general(band, first, TN, preferred_element_type=F32)
        direct = pltpu.roll(grad, LANES - NCOST, 1)
        coarse = pltpu.roll(grad, LANES + 2 * FC - NCOST - FC, 1)
        filled = jnp.where(lane < FC, dfirst + direct, 0.0)
        filled = jnp.where((lane >= 2 * FC) & (lane < 2 * FC + 4), coarse, filled)
        collected[rows, :] = filled

    loop(PH // 4, body)
    for s in range((PH - 2 * MARGIN) // 4):
        pieces = []
        for yy in range(4):
            at = (MARGIN + 4 * s + yy + SR) * PITCH + 8
            pieces.append(dsecond[at : at + PW, :])
        other = pltpu.roll(jnp.concatenate(pieces, axis=0), FC, 1)
        start = (MARGIN + 4 * s) * PW
        tile = collected[start : start + ROWS4, :]
        tile = jnp.where((lane >= FC) & (lane < 2 * FC), other, tile)
        out[s] = tile.T[: out.shape[1]].astype(BF16)


def backward_kernel(*refs):
    stack, pre, dstack, cost, joined, bias_in = refs[:6]
    kernels = refs[6:10]
    picture_out, bias_out = refs[10:12]
    grads = refs[12:16]
    moved, dwide, partial, second, dsecond, collected = refs[16:]
    work = Work(None, moved, partial)
    partial[...] = jnp.zeros_like(partial)
    dwide[...] = dstack[:, : 4 * LANES]

    def store_stack(rows, value):
        dwide[rows, : value.shape[1]] += value

    for index in range(3, -1, -1):
        width = LAYERS[index]["blocks"] * LANES

        def load_grad(rows, index=index):
            if index == 3:
                return dstack[rows, 4 * LANES :]
            return dwide[rows, (index + 1) * LANES : (index + 2) * LANES]

        work.back(
            index,
            load_grad,
            lambda rows, index=index: pre[index, rows, :],
            lambda kx, width=width: stack[kx, :, :width],
            kernels[index],
            grads[index],
            store_stack,
        )
    bias_out[...] = partial[...].sum(1) + bias_in[...]
    correlate_back(joined, cost, dwide, second, dsecond, collected, picture_out)


def backward(stack, pre, dstack, cost, joined, bias_grads, kernels, blocks, channels):
    outs = pl.pallas_call(
        backward_kernel,
        out_shape=[
            jax.ShapeDtypeStruct((blocks, channels, LANES), BF16),
            jax.ShapeDtypeStruct((16, LANES), F32),
            *[jax.ShapeDtypeStruct(k.shape, BF16) for k in kernels],
        ],
        scratch_shapes=[
            pltpu.VMEM((3, PX + 2 * RIM, LANES), BF16),
            pltpu.VMEM((PX, 4 * LANES), F32),
            pltpu.VMEM((16, 8, LANES), F32),
            pltpu.VMEM((SEC_ROWS, LANES), F32),
            pltpu.VMEM((SEC_ROWS, LANES), F32),
            pltpu.VMEM((PX, LANES), F32),
        ],
        compiler_params=pltpu.CompilerParams(vmem_limit_bytes=48 * 2**20),
        cost_estimate=pl.CostEstimate(
            flops=30_000_000_000, bytes_accessed=20_000_000, transcendentals=0
        ),
        name="dense_backward",
    )(stack, pre, dstack, cost, joined, bias_grads, *kernels)
    return outs[0], outs[1], outs[2:]


def update(weights, momentum, average, gradient):
    gradient = gradient + DECAY_RATE * weights
    renewed = MOMENTUM_RATE * momentum + gradient
    stepped = weights - LEARN_RATE * (gradient + MOMENTUM_RATE * renewed)
    return (stepped, renewed, AVERAGE_DECAY * average + (1.0 - AVERAGE_DECAY) * stepped)


CHANNELS = 72


def swapped(value, axis, step):
    count = lax.axis_size(axis)
    return lax.ppermute(value, axis, [(i, i ^ step) for i in range(count)])


def added(one, two):
    return (one.astype(F32) + two.astype(F32)).astype(BF16)


def core_sum(keep, send, groups, devices):
    got = swapped(send, "grp", 1)
    pieces = keep.shape[0] // 2
    if groups == 2:
        return [added(keep, got)]
    return [added(keep[pieces:], got[pieces:]), added(keep[:pieces], got[:pieces])]


def x_sum(value, groups, devices):
    half = devices // 2
    step = groups // 4
    if not step:
        value = value[0]
        return [value[j] for j in range(half)]
    away, value = value
    got = swapped(away, "grp", 2 * step)
    while step > 1:
        value = added(value, got)
        step //= 2
        pieces = value.shape[0] // 2
        got = swapped(value[pieces:], "grp", 2 * step)
        value = value[:pieces]
    return [added(value[j], got[j]) for j in range(half)]


def dev_sum(pieces):
    total = pieces[0].astype(F32)
    for j in range(1, len(pieces)):
        total = total + swapped(pieces[j], "dev", j).astype(F32)
    return total


def far_sum(value, devices, late):
    half = devices // 2
    far = [(i, i + half) if late else (i + half, i) for i in range(half)]
    return value + lax.ppermute(value.astype(BF16), "dev", far).astype(F32)


def shared_x(value, groups):
    x_size = groups // 2
    x = lax.axis_index("grp") // 2
    held = [0]
    parts = [value]
    step = 1
    while step < x_size:
        parts = parts + [swapped(p, "grp", 2 * step) for p in parts]
        held = held + [j ^ step for j in held]
        step *= 2
    out = []
    for i in range(x_size):
        piece = parts[0]
        for j, part in zip(held[1:], parts[1:]):
            piece = jnp.where((x ^ j) == i, part, piece)
        out.append(piece)
    return jnp.concatenate(out)


def shards(features, coarse_flow, target, valid_mask, weights, momentum, average):
    groups = lax.axis_size("grp")
    devices = lax.axis_size("dev")
    own_rows = features.shape[2]
    width = features.shape[3]
    breadth = width // devices
    height = own_rows * devices
    assert breadth + 2 * MARGIN == PW and height + 2 * MARGIN == PH
    core = lax.axis_index("grp") % 2
    me = lax.axis_index("dev")
    half = devices // 2
    early = me < half
    rows = weights.shape[0] // LANES
    x_size = groups // 2
    size = -(-(rows // 2) // (16 * x_size)) * 16 * x_size
    table = weights.reshape(rows, LANES)
    own = lax.dynamic_slice(table, (core * (rows - size), 0), (size, LANES)).astype(BF16)

    marked = valid_mask.astype(BF16)[:, None]
    picture = jnp.concatenate([features, coarse_flow, target, marked], axis=1)[0]
    counts = jnp.sum(valid_mask.astype(F32).reshape(own_rows, -1, PW), axis=1).astype(BF16)
    picture = jnp.pad(picture, ((0, 0), (0, 0), (MARGIN, MARGIN)))
    windows = jnp.stack([picture[:, :, t * breadth : t * breadth + PW] for t in range(devices)])
    counts = jnp.broadcast_to(counts[None, None], (devices, 1, own_rows, PW))
    windows = jnp.concatenate([windows, counts], axis=1)
    received = lax.all_to_all(windows, "dev", split_axis=0, concat_axis=0, tiled=True)

    across = swapped(own, "dev", half)
    across, received = lax.optimization_barrier((across, received))
    both = jnp.stack([core, 1 - core])[:, None] * (rows - size)
    part, last = jnp.where(early, own, across)[None], jnp.where(early, across, own)[None]
    held = [0]
    step = half // 2
    while step:
        part = jnp.concatenate([part, swapped(part, "dev", step)])
        held = held + [j ^ step for j in held]
        if step == half // 2:
            part, last, received = lax.optimization_barrier((part, last, received))
        step //= 2
    sources = jnp.array(held, jnp.int32) ^ (me % half)
    places = [(sources + half * late)[None] * rows + both for late in range(2)]

    counted = jnp.full((8, LANES), jnp.sum(received[:, CHANNELS - 1].astype(F32)))
    step = 1
    while step < groups:
        counted = counted + swapped(counted, "grp", step)
        step *= 2
    weighting = groups * height * width / counted[:1]
    per = 4 // own_rows
    blocks = devices // per
    received = received.reshape(blocks, per, CHANNELS, own_rows * PW)
    received = jnp.swapaxes(received, 1, 2).reshape(blocks, CHANNELS, LANES)
    received = jnp.pad(received, ((0, 0), (0, LANES - CHANNELS), (0, 0)))

    stack0, cost, joined = correlate(received)
    part, stack0 = lax.optimization_barrier((part, stack0))
    parts = [(part, swapped(part, "grp", 1))]
    kernels, carried, stack, below, pre = forward(places[0], parts[0], stack0, half * rows)
    step = half // 2
    while step:
        moved = swapped(last, "dev", step)
        if step == 1:
            moved, stack = lax.optimization_barrier((moved, stack))
        last = jnp.concatenate([last, moved])
        step //= 2
    parts.append((last, swapped(last, "grp", 1)))
    x = lax.axis_index("grp") // 2
    part_x = (jnp.arange(x_size, dtype=jnp.int32) ^ x) * (size // x_size)
    part_dev = (jnp.arange(half, dtype=jnp.int32) ^ (me % half)) * rows
    pack_at = (part_x[:, None] + part_dev[None]).reshape(1, -1) + both
    pieces = (half * x_size, size // x_size)
    motion, dstack, bias_grads, keep, send, carried = late(
        places[1],
        pack_at + half * rows,
        parts[1],
        carried,
        stack,
        below,
        joined,
        weighting,
        devices * rows,
        *pieces,
    )
    flow = motion[:2].reshape(1, 2, PH, PW)[
        :, :, MARGIN : MARGIN + height, MARGIN : MARGIN + breadth
    ]
    late_sum = core_sum(keep, send, groups, devices)
    late_sum, dstack = lax.optimization_barrier((late_sum, dstack))
    late_sum = x_sum(late_sum, groups, devices)
    tiles, bias_grads, grads = backward(
        stack, pre, dstack, cost, joined, bias_grads, kernels, blocks, CHANNELS
    )
    late_sum, bias_grads = lax.optimization_barrier((late_sum, bias_grads))
    late_sum = dev_sum(late_sum)
    keep, send = pack(pack_at, grads, bias_grads, carried, half * rows, *pieces)
    late_sum, keep, send = lax.optimization_barrier((late_sum, keep, send))
    early_sum = core_sum(keep, send, groups, devices)
    late_total = far_sum(late_sum, devices, True)
    early_sum = x_sum(early_sum, groups, devices)
    early_sum, late_total = lax.optimization_barrier((early_sum, late_total))
    early_total = far_sum(dev_sum(early_sum), devices, False)
    total = jnp.where(early, early_total, late_total).astype(BF16)
    total = shared_x(total, groups)
    rest = swapped(total, "grp", 1)
    low = jnp.where(core == 0, total, rest)
    high = jnp.where(core == 0, rest, total)
    total_grad = jnp.concatenate([low[: rows - size], high]).astype(F32).reshape(-1)

    tiles = tiles.reshape(blocks, CHANNELS, per, own_rows, PW)
    tiles = jnp.swapaxes(tiles, 1, 2).reshape(devices, CHANNELS, own_rows, PW)
    returned = lax.all_to_all(tiles, "dev", split_axis=0, concat_axis=0, tiled=True)
    returned = returned.astype(F32)
    wide = jnp.transpose(returned, (1, 2, 0, 3))
    centre = wide[..., MARGIN : MARGIN + breadth]
    left = wide[:, :, 1:, :MARGIN]
    right = wide[:, :, :-1, MARGIN + breadth :]
    none = ((0, 0), (0, 0))
    centre = centre + jnp.pad(left, (*none, (0, 1), (breadth - MARGIN, 0)))
    centre = centre + jnp.pad(right, (*none, (1, 0), (0, breadth - MARGIN)))
    row_grad = centre.reshape(1, CHANNELS, own_rows, width)
    feature_grad = row_grad[:, : 2 * FC]
    coarse_grad = row_grad[:, 2 * FC : 2 * FC + 4]

    new_weights, new_momentum, new_average = update(weights, momentum, average, total_grad)
    return (
        flow,
        feature_grad,
        coarse_grad,
        new_weights,
        new_momentum,
        new_average,
        new_weights.astype(BF16),
    )


def solution(mesh):
    in_specs = (
        P("grp", None, "dev", None),
        P("grp", None, "dev", None),
        P("grp", None, "dev", None),
        P("grp", "dev", None),
        P("dev"),
        P("dev"),
        P("dev"),
    )
    out_specs = (
        P("grp", None, None, "dev"),
        P("grp", None, "dev", None),
        P("grp", None, "dev", None),
        P("dev"),
        P("dev"),
        P("dev"),
        P("dev"),
    )
    return jax.shard_map(shards, mesh=mesh, in_specs=in_specs, out_specs=out_specs, check_vma=False)
```

```python
import functools

import jax
import jax.numpy as jnp
from jax import lax
from jax.experimental import pallas as pl
from jax.experimental.pallas import tpu as pltpu
from jax.sharding import PartitionSpec as P

FC = 32
SR = 4
EXT = 2 * SR + 1
NCOST = EXT * EXT
NS0 = NCOST + FC + 4
DENSE = (128, 128, 96, 64, 32)
CONTEXT = (128, 128, 128, 96, 64, 32, 2)
DILATIONS = (1, 2, 4, 8, 16, 1, 1)
MARGIN = 8

SLOPE = 0.1
EPE_EPS = 0.01
MOMENTUM_RATE = 0.5
AVERAGE_DECAY = 0.5
LEARN_RATE = 0.001
DECAY_RATE = 0.0001

LANES = 128
CHANNELS = 72
PH = 48
PW = 32
PX = PH * PW
RIM = 16 * PW
STRIP = 128
MT = 768
PITCH = 40
F32 = jnp.float32
BF16 = jnp.bfloat16
NT = (((1,), (1,)), ((), ()))
TN = (((0,), (0,)), ((), ()))


def layer_table():
    places = [(NS0, 0, 0), (128, 1, 0), (128, 2, 0), (96, 3, 0), (64, 4, 0), (32, 4, 64)]
    layers = []
    offset = 0

    def add(pieces, outgoing, dilation, shift):
        nonlocal offset
        incoming = sum(n for n, _, _ in pieces)
        row = 9 * incoming
        segments = []
        at = 0
        for n, block, lane in pieces:
            first, over = 9 * at // LANES, 9 * at % LANES
            slot = -(-(9 * lane - over) // LANES)
            back = 9 * lane - over - LANES * slot
            chunks = -(-(over + 9 * n) // LANES)
            segments.append(
                dict(n=n, block=block, lane=lane, first=first, slot=slot, back=back, chunks=chunks)
            )
            at += n
        blocks = 1 + max(b for _, b, _ in pieces)
        layers.append(
            dict(
                out=outgoing,
                row=row,
                chunks=-(-row // LANES),
                start=offset,
                dil=dilation,
                shift=shift,
                segments=segments,
                blocks=blocks,
                bias=offset + row * outgoing,
                shape=(LANES, blocks * LANES) if outgoing == 2 else (3 * LANES, 3 * blocks * LANES),
            )
        )
        offset += row * outgoing + outgoing

    for i, outgoing in enumerate(DENSE):
        add(places[i::-1], outgoing, 1, 64 if i == 4 else 0)
    add(places[::-1], 2, 1, 0)
    add(places[::-1], CONTEXT[0], DILATIONS[0], 0)
    for i in range(1, 7):
        add([(CONTEXT[i - 1], 0, 0)], CONTEXT[i], DILATIONS[i], 0)
    return layers, offset


LAYERS, COUNT = layer_table()
EARLY = (0, 1, 2, 3)
LATE = (4, 5, 6, 7, 8, 9, 10, 11, 12)
CUT = LAYERS[4]["start"] // LANES // 16 * 16


def sort_groups(indices):
    order = [(segment["back"], i, s) for i in indices for s, segment in enumerate(LAYERS[i]["segments"])]
    order.sort(key=lambda t: -t[0])
    at = 0
    groups = {}
    classes = []
    for back, i, s in order:
        if not classes or classes[-1][0] != back:
            classes.append([back, at, at])
        groups[i, s] = at
        at += -(-LAYERS[i]["out"] // 16) * 16
        classes[-1][2] = at
    return groups, classes, at


def iota(shape, dim):
    return lax.broadcasted_iota(jnp.int32, shape, dim)


def rows_at(start, size, step=8):
    if isinstance(start, int):
        return pl.ds(start, size)
    return pl.ds(pl.multiple_of(start, step), size)


def sigmoid(v):
    return 0.5 * jnp.tanh(0.5 * v) + 0.5


def leaky(v):
    return SLOPE * v + (1.0 - SLOPE) * v * sigmoid(v)


def leaky_slope(v):
    s = sigmoid(v)
    return SLOPE + (1.0 - SLOPE) * (s + v * s * (1.0 - s))


def loop(count, body):
    def step(i, carry):
        body(i)
        return carry

    lax.fori_loop(0, count, step, 0)


def fill_order(order):
    order[:LANES, :] = jnp.zeros((LANES, 9 * LANES), BF16)
    order[10 * LANES :, :] = jnp.zeros((LANES, 9 * LANES), BF16)
    for k in range(9):
        for m in range(9):
            row = iota((LANES, LANES), 0) + m * LANES
            col = iota((LANES, LANES), 1)
            order[(m + 1) * LANES : (m + 2) * LANES, k * LANES : (k + 1) * LANES] = jnp.where(
                row == 9 * col + k, 1.0, 0.0
            ).astype(BF16)


ORDER = pltpu.VMEM((11 * LANES, 9 * LANES), BF16)


def within(n, lane):
    spot = iota((1, LANES), 1)
    return jnp.where((spot >= lane) & (spot < lane + n), 1.0, 0.0).astype(BF16)


def pitch_of(chunks):
    return -(-chunks // 8) * 8


def unpack_scratch(indices, count):
    _, _, group_rows = sort_groups(indices)
    return (
        pltpu.VMEM((count + 64, LANES), F32),
        pltpu.VMEM((48 * LANES, LANES), F32),
        pltpu.VMEM((group_rows, 10 * LANES), BF16),
        pltpu.VMEM((group_rows, 9 * LANES), BF16),
        pltpu.VMEM((LANES, 5 * LANES), F32),
    )


def unpack_weights(indices, base, place_at, parts, carried, outs, bias_out, carry_out, order, scratch):
    whole, slabs, aligned, result, heads = scratch
    count = whole.shape[0] - 64
    groups, classes, _ = sort_groups(indices)
    if base:
        whole[: carried.shape[0], :] = carried[...].astype(F32)
    for at_part, pieces in enumerate(parts):
        for j, piece in enumerate(pieces):
            size = piece.shape[0]
            to = place_at[at_part, j] - base

            def widen(i, piece=piece, to=to):
                whole[pl.ds(to + i * 16, 16), :] = piece[rows_at(i * 16, 16, 16), :].astype(F32)

            lax.fori_loop(0, size // 16, lambda i, c: (widen(i), c)[1], 0, unroll=8)
    whole[count:, :] = jnp.zeros((64, LANES), F32)
    if not base:
        carry_out[...] = whole[CUT:count, :].astype(BF16)
    bias_out[...] = jnp.zeros_like(bias_out)

    for at_out, index in enumerate(indices):
        layer = LAYERS[index]
        outgoing = layer["out"]
        kept = -(-outgoing // 16) * 16
        start = layer["start"] - base * LANES
        spot = iota((kept, LANES), 1)
        pitch = pitch_of(layer["chunks"] + 1)
        still = layer["row"] % LANES == 0
        if not still:
            unroll = min(32, outgoing)

            def take(i, unroll=unroll, row=layer["row"], start=start, pitch=pitch):
                for u in range(unroll):
                    o = i * unroll + u
                    first = start + o * row
                    turn = (LANES - (first & (LANES - 1))) & (LANES - 1)
                    for v in range(pitch // 8):
                        tile = whole[pl.ds((first >> 7) + 8 * v, 8), :]
                        slabs[rows_at(o * pitch + 8 * v, 8), :] = pltpu.roll(tile, turn, 1)

            for i in range(outgoing // unroll):
                take(i)
            off = (start + iota((kept, LANES), 0) * layer["row"]) & (LANES - 1)
        chunks = {}
        for t in range(layer["chunks"]):
            if still:
                row, fixed = divmod(start, LANES)
                step = layer["row"] // LANES
                here = whole[pl.ds(row + t, kept, stride=step), :]
                after = whole[pl.ds(row + t + 1, kept, stride=step), :]
                chunk = jnp.where(spot >= fixed, here, after)
                chunk = pltpu.roll(chunk, (LANES - fixed) % LANES, 1)
            else:
                here = slabs[pl.ds(t, kept, stride=pitch), :]
                after = slabs[pl.ds(t + 1, kept, stride=pitch), :]
                chunk = jnp.where(spot < LANES - off, here, after)
            chunk = chunk.astype(BF16)
            for s, segment in enumerate(layer["segments"]):
                to = t - segment["first"]
                if 0 <= to < segment["chunks"]:
                    to += segment["slot"]
                    at = groups[index, s]
                    aligned[at : at + kept, to * LANES : (to + 1) * LANES] = chunk
        for s, segment in enumerate(layer["segments"]):
            at = groups[index, s]
            for to in range(10):
                if not segment["slot"] <= to < segment["slot"] + segment["chunks"]:
                    aligned[at : at + kept, to * LANES : (to + 1) * LANES] = jnp.zeros(
                        (kept, LANES), BF16
                    )
        shift = layer["shift"]
        first = layer["bias"] - base * LANES - shift
        row, fixed = divmod(first, LANES)
        here = pltpu.roll(whole[row : row + 1, :], (LANES - fixed) % LANES, 1)
        after = pltpu.roll(whole[row + 1 : row + 2, :], (LANES - fixed) % LANES, 1)
        line = iota((1, LANES), 1)
        value = jnp.where(line < LANES - fixed, here, after)
        bias_out[index : index + 1, :] = jnp.where(
            (line >= shift) & (line < shift + outgoing), value, 0.0
        )

    for back, low, high in classes:
        wide = 9 if back == 0 else 10
        result[low:high, :] = jnp.dot(
            aligned[low:high, : wide * LANES],
            order[LANES + back : LANES + back + wide * LANES, :],
            preferred_element_type=F32,
        ).astype(BF16)

    for at_out, index in enumerate(indices):
        layer = LAYERS[index]
        outgoing = layer["out"]
        shift = layer["shift"]
        out = outs[at_out]
        width = layer["blocks"] * LANES
        if outgoing == 2:
            heads[...] = jnp.zeros_like(heads)
        elif outgoing < LANES:
            out[...] = jnp.zeros_like(out)
        kept = -(-outgoing // 16) * 16
        for block in range(layer["blocks"]):
            for k in range(9):
                total = None
                for s, segment in enumerate(layer["segments"]):
                    if segment["block"] != block:
                        continue
                    at = groups[index, s]
                    tile = result[at : at + kept, k * LANES : (k + 1) * LANES]
                    if segment["n"] < LANES:
                        tile = tile * within(segment["n"], segment["lane"])
                    total = tile if total is None else total + tile
                if outgoing == 2:
                    heads[2 * k : 2 * k + 2, block * LANES : (block + 1) * LANES] = total.astype(
                        F32
                    )[:2]
                else:
                    ky, kx = divmod(k, 3)
                    at = kx * width + block * LANES
                    out[ky * LANES + shift : ky * LANES + shift + outgoing, at : at + LANES] = total
        if outgoing == 2:
            out[...] = heads[:, :width].astype(BF16)


def pack_scratch(indices, count):
    _, _, group_rows = sort_groups(indices)
    return (
        pltpu.VMEM((count + 64, LANES), F32),
        pltpu.VMEM((40 * LANES + 64, LANES), F32),
        pltpu.VMEM((group_rows, 9 * LANES), BF16),
        pltpu.VMEM((group_rows, 10 * LANES), F32),
        pltpu.VMEM((LANES + 16, 5 * LANES), F32),
    )


def pack_gradients(indices, base, place_at, grads, bias_in, carried, halves, carry_out, order, scratch):
    whole, slabs, gathered, result, heads = scratch
    count = whole.shape[0] - 64
    groups, classes, _ = sort_groups(indices)
    for at_in, index in enumerate(indices):
        layer = LAYERS[index]
        outgoing = layer["out"]
        shift = layer["shift"]
        grad = grads[at_in]
        width = layer["blocks"] * LANES
        if outgoing == 2:
            heads[:LANES, :width] = grad[...].astype(F32)
            heads[LANES:, :] = jnp.zeros((16, heads.shape[1]), F32)
        for s, segment in enumerate(layer["segments"]):
            at = groups[index, s]
            block = segment["block"]
            for k in range(9):
                if outgoing == 2:
                    tile = heads[2 * k : 2 * k + 16, block * LANES : (block + 1) * LANES]
                    tile = tile.astype(BF16)
                else:
                    ky, kx = divmod(k, 3)
                    column = kx * width + block * LANES
                    tile = grad[
                        ky * LANES + shift : ky * LANES + shift + outgoing, column : column + LANES
                    ]
                if segment["n"] < LANES:
                    tile = tile * within(segment["n"], segment["lane"])
                gathered[at : at + tile.shape[0], k * LANES : (k + 1) * LANES] = tile

    for back, low, high in classes:
        wide = 9 if back == 0 else 10
        result[low:high, : wide * LANES] = lax.dot_general(
            gathered[low:high, :],
            order[LANES + back : LANES + back + wide * LANES, :],
            NT,
            preferred_element_type=F32,
        )

    lane = iota((8, LANES), 1)
    sub = iota((8, LANES), 0)

    for at_in, index in enumerate(indices):
        layer = LAYERS[index]
        outgoing = layer["out"]
        start = layer["start"] - base * LANES
        still = layer["row"] % LANES == 0
        pitch = pitch_of(layer["chunks"])
        spot = iota((outgoing, LANES), 1)
        turned = []
        for t in range(layer["chunks"]):
            chunk = None
            for s, segment in enumerate(layer["segments"]):
                to = t - segment["first"]
                if 0 <= to < segment["chunks"]:
                    to += segment["slot"]
                    at = groups[index, s]
                    tile = result[at : at + outgoing, to * LANES : (to + 1) * LANES]
                    chunk = tile if chunk is None else chunk + tile
            if still:
                turned.append(pltpu.roll(chunk, start % LANES, 1))
            else:
                slabs[pl.ds(t, outgoing, stride=pitch), :] = chunk
        if still:
            row, fixed = divmod(start, LANES)
            step = layer["row"] // LANES
            for t in range(step):
                before = turned[t - 1] if t else pltpu.roll(turned[-1], 1, 0)
                value = jnp.where(spot >= fixed, turned[t], before)
                if t == 0:
                    kept = whole[row : row + 1, :]
                    top = (iota((outgoing, LANES), 0) == 0) & (spot < fixed)
                    value = jnp.where(top, kept, value)
                whole[pl.ds(row + t, outgoing, stride=step), :] = value
            last = pltpu.roll(turned[-1][outgoing - 8 :, :], 1, 0)
            end = row + step * outgoing
            pltpu.store(whole.at[end : end + 8, :], last, mask=(sub == 0) & (lane < fixed))
        else:
            unroll = min(32, outgoing)

            def put(i, start=start, row=layer["row"], pitch=pitch, unroll=unroll):
                for u in range(unroll):
                    o = i * unroll + u
                    first = start + o * row
                    off = first & (LANES - 1)
                    for v in range(pitch // 8):
                        tile = pltpu.roll(slabs[rows_at(o * pitch + 8 * v, 8), :], off, 1)
                        to = (first >> 7) + 8 * v
                        pltpu.store(whole.at[pl.ds(to, 8), :], tile, mask=lane >= off)
                        pltpu.store(whole.at[pl.ds(to + 1, 8), :], tile, mask=lane < off)

            for i in range(outgoing // unroll):
                put(i)
        line = bias_in[index : index + 1, :]
        first = layer["bias"] - base * LANES
        row, fixed = divmod(first, LANES)
        line = pltpu.roll(line, (fixed - layer["shift"]) % LANES, 1)
        line = jnp.broadcast_to(line, (8, LANES))
        pltpu.store(whole.at[row : row + 8, :], line, mask=(sub == 0) & (lane >= fixed))
        pltpu.store(whole.at[row + 1 : row + 9, :], line, mask=(sub == 0) & (lane < fixed))
    if base:
        end, off = divmod(COUNT - base * LANES, LANES)
        pltpu.store(
            whole.at[end : end + 8, :], jnp.zeros((8, LANES), F32), mask=(sub > 0) | (lane >= off)
        )
        if count > end + 8:
            whole[end + 8 : count, :] = jnp.zeros((count - end - 8, LANES), F32)
        carry_out[...] = whole[: carry_out.shape[0], :].astype(BF16)
    else:
        end, off = divmod(LAYERS[4]["start"], LANES)
        line = carried[...].astype(F32)
        keep = (iota(line.shape, 0) > end - CUT) | (
            (iota(line.shape, 0) == end - CUT) & (iota(line.shape, 1) >= off)
        )
        whole[CUT:count, :] = jnp.where(keep, line, whole[CUT:count, :])
    for half in range(2):
        size = halves[half].shape[1]
        for j in range(halves[half].shape[0]):
            begin = place_at[half, j] - base

            def narrow(i, half=half, j=j, begin=begin):
                halves[half][j, rows_at(i * 16, 16, 16), :] = whole[
                    pl.ds(begin + i * 16, 16), :
                ].astype(BF16)

            lax.fori_loop(0, size // 16, lambda i, c: (narrow(i), c)[1], 0, unroll=8)


ROWS4 = 4 * PW
SEC_ROWS = (PH + 2 * SR) * PITCH + LANES


def load_second(joined, second):
    second[...] = jnp.zeros_like(second)
    keep = iota((PW, LANES), 1) < FC
    for y in range(MARGIN, PH - MARGIN):
        row = joined[y * PW : (y + 1) * PW, :].astype(F32)
        row = jnp.where(keep, pltpu.roll(row, LANES - FC, 1), 0.0)
        at = (y + SR) * PITCH + 8
        second[at : at + PW, :] = row


def start_copies(sources, targets, semaphores):
    copies = [
        pltpu.make_async_copy(source, target, semaphores.at[i])
        for i, (source, target) in enumerate(zip(sources, targets))
    ]
    for copy in copies:
        copy.start()
    return copies


def windows_kernel(*refs):
    out = refs[4]
    features, coarse, target, mask = refs[5:9]
    for copy in start_copies(refs[:4], refs[5:9], refs[9]):
        copy.wait()
    own_rows, width = mask.shape[1:]
    devices = out.shape[0]
    breadth = width // devices
    side = jnp.zeros((CHANNELS - 1, MARGIN), F32)
    arrays = [features[0].astype(F32), coarse[0].astype(F32), target[0].astype(F32)]
    marks = mask[0].astype(F32)
    for r in range(own_rows):
        valid = marks[r : r + 1, :]
        tall = jnp.concatenate([a[:, r, :] for a in arrays] + [valid], axis=0)
        tall = jnp.concatenate([side, tall, side], axis=1)
        count = sum(valid[:, at : at + PW] for at in range(0, width, PW))
        for t in range(devices):
            tile = jnp.concatenate([tall[:, t * breadth : t * breadth + PW], count], axis=0)
            out[t, :, r * PW : (r + 1) * PW] = tile.astype(BF16)


def windows(features, coarse, target, mask, devices):
    return pl.pallas_call(
        windows_kernel,
        out_shape=jax.ShapeDtypeStruct((devices, CHANNELS, mask.shape[1] * PW), BF16),
        in_specs=[pl.BlockSpec(memory_space=pltpu.HBM)] * 4,
        scratch_shapes=[pltpu.VMEM(a.shape, a.dtype) for a in (features, coarse, target, mask)]
        + [pltpu.SemaphoreType.DMA((4,))],
        compiler_params=pltpu.CompilerParams(vmem_limit_bytes=60 * 2**20),
        name="windows",
    )(features, coarse, target, mask)


def band_shift(dy, third):
    return EXT * dy - PITCH * third - (8 - SR)


def correlate_kernel(received, stack0, cost_out, joined_out, counted, second, cost, joined, copied):
    joined[...] = jnp.zeros_like(joined)
    blocks = received.shape[0]
    spare = jnp.zeros((LANES - received.shape[1], LANES), F32)
    number = jnp.zeros((1, LANES), F32)
    for s in range(blocks):
        tile = received[s].astype(F32)
        number = number + tile[CHANNELS - 1 :, :]
        tile = jnp.concatenate([tile, spare], axis=0).T
        joined[RIM // 2 + s * ROWS4 : RIM // 2 + (s + 1) * ROWS4, :] = tile.astype(BF16)
    copies = start_copies([joined], [joined_out], copied)
    number = jnp.sum(number, axis=1, keepdims=True)
    counted[...] = jnp.broadcast_to(number, counted.shape)
    load_second(joined, second)
    row = iota((ROWS4, ROWS4), 0)
    col = iota((ROWS4, ROWS4), 1)
    flip = jnp.where((row // PW == col // PW) & (row % PW + col % PW == PW - 1), 1.0, 0.0).astype(
        BF16
    )
    lane = iota((ROWS4, LANES), 1)
    narrow = iota((PW, LANES), 1)

    def body(i):
        own = joined[rows_at(i * ROWS4, ROWS4, ROWS4), :]
        first = jnp.where(lane < FC, own.astype(F32), 0.0).astype(BF16)
        first = jnp.dot(flip, first, preferred_element_type=F32).astype(BF16)
        bands = []
        for g in range(4):
            window = second[rows_at((4 * i + 3 * g) * PITCH, LANES), :].astype(BF16)
            bands.append(lax.dot_general(first, window, NT, preferred_element_type=F32))
        pieces = []
        for yy in range(4):
            total = jnp.zeros((PW, LANES), F32)
            turned = [
                pltpu.roll(band[yy * PW : (yy + 1) * PW, :], 0, 1, stride=1, stride_axis=0)
                for band in bands
            ]
            for dy in range(EXT):
                t = yy + dy
                shift = (band_shift(dy, t % 3) - (PW - 1)) % LANES
                band = pltpu.roll(turned[t // 3], shift, 1)
                total = jnp.where((narrow >= EXT * dy) & (narrow < EXT * (dy + 1)), band, total)
            pieces.append(total * (1.0 / FC))
        total = jnp.concatenate(pieces, axis=0)
        high = total.astype(BF16)
        low = (total - high.astype(F32)).astype(BF16)
        total = jnp.dot(flip, high, preferred_element_type=F32) + jnp.dot(
            flip, low, preferred_element_type=F32
        )
        cost[rows_at(i * ROWS4, ROWS4, ROWS4), :] = total
        wide = own.astype(F32)
        filled = jnp.where(lane < NCOST, leaky(total), pltpu.roll(wide, NCOST, 1))
        coarse = pltpu.roll(wide, NCOST + FC - 2 * FC, 1)
        filled = jnp.where(lane >= NCOST + FC, coarse, filled)
        filled = jnp.where(lane < NS0, filled, 0.0)
        stack0[rows_at(i * ROWS4, ROWS4, ROWS4), :] = filled.astype(BF16)

    for i in range(PH // 4):
        body(i)
    copies.append(pltpu.make_async_copy(cost, cost_out, copied.at[1]))
    copies[1].start()
    for copy in copies:
        copy.wait()


def correlate(received):
    vmem = pl.BlockSpec(memory_space=pltpu.VMEM)
    anywhere = pl.BlockSpec(memory_space=pltpu.HBM)
    return pl.pallas_call(
        correlate_kernel,
        out_shape=[
            jax.ShapeDtypeStruct((PX, LANES), BF16),
            jax.ShapeDtypeStruct((PX, LANES), F32),
            jax.ShapeDtypeStruct((PX, LANES), BF16),
            jax.ShapeDtypeStruct((8, LANES), F32),
        ],
        out_specs=[vmem, anywhere, anywhere, vmem],
        scratch_shapes=[
            pltpu.VMEM((SEC_ROWS, LANES), F32),
            pltpu.VMEM((PX, LANES), F32),
            pltpu.VMEM((PX, LANES), BF16),
            pltpu.SemaphoreType.DMA((2,)),
        ],
        compiler_params=pltpu.CompilerParams(vmem_limit_bytes=60 * 2**20),
        cost_estimate=pl.CostEstimate(
            flops=8_000_000_000, bytes_accessed=2_000_000, transcendentals=0
        ),
        name="correlate",
    )(received)


class Work:
    def __init__(self, taps, moved, partial):
        self.taps = taps
        self.moved = moved
        self.partial = partial
        self.column = iota((STRIP, LANES), 0) % PW
        self.lane = iota((STRIP, LANES), 1)
        if taps is not None:
            taps[:, :RIM, :] = jnp.zeros((3, RIM, LANES), F32)
            taps[:, RIM + PX :, :] = jnp.zeros((3, RIM, LANES), F32)
        if moved is not None:
            moved[:, :RIM, :] = jnp.zeros((3, RIM, LANES), BF16)
            moved[:, RIM + PX :, :] = jnp.zeros((3, RIM, LANES), BF16)

    def strips(self, body):
        for at in range(0, PX, STRIP):
            body(pl.ds(at, STRIP), at)

    def inside(self, tile, shift):
        if shift == 0:
            return tile
        valid = (self.column + shift >= 0) & (self.column + shift < PW)
        return jnp.where(valid, pltpu.roll(tile, (-shift) % STRIP, 0), 0.0)

    def spread(self, store, tile, dilation):
        for kx in range(3):
            store(kx, self.inside(tile, (kx - 1) * dilation).astype(BF16))

    def multiply(self, load, kernel):
        def body(i):
            rows = rows_at(i * MT, MT, MT)
            value = jnp.concatenate([load(kx, rows) for kx in range(3)], axis=1)
            product = lax.dot_general(value, kernel[...], NT, preferred_element_type=F32)
            for ky in range(3):
                self.taps[ky, rows_at(RIM + i * MT, MT, MT), :] = product[
                    :, ky * LANES : (ky + 1) * LANES
                ]

        for i in range(PX // MT):
            body(i)

    def collect(self, at, dilation):
        total = None
        for ky in range(3):
            tile = self.taps[ky, rows_at(RIM + at + (ky - 1) * dilation * PW, STRIP, PW), :]
            total = tile if total is None else total + tile
        return total

    def spread_grad(self, at, grad, dilation):
        for kx in range(3):
            self.moved[kx, rows_at(RIM + at, STRIP, STRIP), :] = self.inside(
                grad, -(kx - 1) * dilation
            ).astype(BF16)

    def count_bias(self, index, grad):
        self.partial[index] += grad.reshape(STRIP // 8, 8, LANES).sum(0)

    def back(self, index, load_grad, load_pre, load_input, kernel, out, store, waits=()):
        layer = LAYERS[index]
        dilation = layer["dil"]
        width = layer["blocks"] * LANES

        def through(rows, at):
            grad = load_grad(rows) * leaky_slope(load_pre(rows))
            grad = grad.astype(BF16).astype(F32)
            self.count_bias(index, grad)
            self.spread_grad(at, grad, dilation)

        self.strips(through)
        for load in waits:
            load.wait()
        grad = jnp.concatenate(
            [
                self.moved[1, RIM - (ky - 1) * dilation * PW : RIM - (ky - 1) * dilation * PW + PX, :]
                for ky in range(3)
            ],
            axis=1,
        )
        for kx in range(3):
            out[:, kx * width : (kx + 1) * width] = lax.dot_general(
                grad, load_input(kx), TN, preferred_element_type=F32
            ).astype(BF16)

        def input_grad(i):
            tiles = [
                self.moved[kx, rows_at(RIM + i * MT - (ky - 1) * dilation * PW, MT, PW), :]
                for ky in range(3)
                for kx in range(3)
            ]
            weights = [
                kernel[ky * LANES : (ky + 1) * LANES, kx * width : (kx + 1) * width]
                for ky in range(3)
                for kx in range(3)
            ]
            store(
                rows_at(i * MT, MT, MT),
                jnp.dot(
                    jnp.concatenate(tiles, axis=1),
                    jnp.concatenate(weights, axis=0),
                    preferred_element_type=F32,
                ),
            )

        for i in range(PX // MT):
            input_grad(i)


def forward_kernel(half, place_at, stack0, *refs):
    own, other, refs = refs[:half], refs[half : 2 * half], refs[2 * half :]
    kernels_out, carry_out, (stack_out, top_out, pre_out) = refs[:4], refs[4], refs[5:8]
    kernels, refs = refs[8:12], refs[12:]
    stack, top, pre, biases, order, taps, copied = refs[:7]
    fill_order(order)
    unpack_weights(
        EARLY, 0, place_at, (own, other), None, kernels, biases, carry_out, order, refs[7:]
    )
    copies = start_copies(kernels, kernels_out, copied)
    work = Work(taps, None, None)

    def first(rows, at):
        tile = stack0[rows, :].astype(F32)

        def keep(kx, value):
            stack[kx, rows, :LANES] = value

        work.spread(keep, tile, 1)

    work.strips(first)
    for index, kernel in enumerate(kernels):
        width = LAYERS[index]["blocks"] * LANES
        work.multiply(lambda kx, rows, width=width: stack[kx, rows, :width], kernel)

        def finish(rows, at, index=index):
            value = work.collect(at, 1) + biases[index : index + 1, :]
            pre[index, rows, :] = value
            place = slice((index + 1) * LANES, (index + 2) * LANES)

            def keep(kx, value):
                if index == 3:
                    top[kx, rows, :] = value
                else:
                    stack[kx, rows, place] = value

            work.spread(keep, leaky(value), 1)

        work.strips(finish)
        copies.append(
            pltpu.make_async_copy(pre.at[index], pre_out.at[index], copied.at[4 + index])
        )
        copies[-1].start()
    for i, (source, target) in enumerate(((stack, stack_out), (top, top_out))):
        copies.append(pltpu.make_async_copy(source, target, copied.at[8 + i]))
        copies[-1].start()
    for copy in copies:
        copy.wait()


def forward(place_at, parts, stack0, count):
    vmem = pl.BlockSpec(memory_space=pltpu.VMEM)
    anywhere = pl.BlockSpec(memory_space=pltpu.HBM)
    kernels = [(LAYERS[i]["shape"], BF16) for i in EARLY]
    states = [((3, PX, 4 * LANES), BF16), ((3, PX, LANES), BF16), ((4, PX, LANES), F32)]
    outs = pl.pallas_call(
        functools.partial(forward_kernel, len(parts[0])),
        out_shape=[
            jax.ShapeDtypeStruct(*a) for a in (*kernels, ((count - CUT, LANES), BF16), *states)
        ],
        in_specs=[pl.BlockSpec(memory_space=pltpu.SMEM)] + [vmem] * (1 + 2 * len(parts[0])),
        out_specs=[anywhere] * 4 + [vmem] + [anywhere] * 3,
        scratch_shapes=[
            *[pltpu.VMEM(*a) for a in (*kernels, *states)],
            pltpu.VMEM((16, LANES), F32),
            ORDER,
            pltpu.VMEM((3, PX + 2 * RIM, LANES), F32),
            pltpu.SemaphoreType.DMA((10,)),
            *unpack_scratch(EARLY, count),
        ],
        compiler_params=pltpu.CompilerParams(vmem_limit_bytes=60 * 2**20),
        cost_estimate=pl.CostEstimate(
            flops=25_000_000_000, bytes_accessed=20_000_000, transcendentals=0
        ),
        name="dense_forward",
    )(place_at, stack0, *parts[0], *parts[1])
    return outs[:4], *outs[4:]


def late_kernel(
    rows,
    half,
    groups,
    pixels,
    gather_at,
    pack_at,
    carried,
    stack_in,
    below_in,
    joined_in,
    *refs,
):
    counts, refs = refs[:groups], refs[groups:]
    own, other, refs = refs[:half], refs[half : 2 * half], refs[2 * half :]
    motion_out, dstack_out, bias_out, keep, send, carry_out = refs[:6]
    order, biases, dstack, stack, below, joined, copied = refs[6:13]
    refs = refs[13:]
    kernels = refs[:9]
    grads = refs[9:]
    loads = [
        pltpu.make_async_copy(source, target, copied.at[i])
        for i, (source, target) in enumerate(zip((stack_in, below_in, joined_in), (stack, below, joined)))
    ]
    for load in loads:
        load.start()
    fill_order(order)

    def first(*scratch):
        unpack_weights(
            LATE, CUT, gather_at, (own, other), carried, kernels, biases, None, order, scratch
        )

    pl.run_scoped(first, *unpack_scratch(LATE, rows))
    for load in loads:
        load.wait()

    weighting = pixels / sum(count[:1, :] for count in counts)

    def second(*scratch):
        context(
            stack, below, joined, weighting, biases, kernels, motion_out, dstack, bias_out, grads, *scratch
        )

    pl.run_scoped(second, *CONTEXT_SCRATCH)
    store = pltpu.make_async_copy(dstack, dstack_out, copied.at[3])
    store.start()

    def third(*scratch):
        pack_gradients(
            LATE, CUT, pack_at, grads, bias_out, None, (keep, send), carry_out, order, scratch
        )

    pl.run_scoped(third, *pack_scratch(LATE, rows))
    store.wait()


def context(
    stack, below, joined, weighting, biases, kernels, motion_out, dstack, bias_out, grads, *scratch
):
    kernels = dict(zip(LATE, kernels))
    grads = dict(zip(LATE, grads))
    top, ctx, pre, taps, moved, dcur, ghead, partial = scratch
    work = Work(taps, moved, partial)
    partial[...] = jnp.zeros_like(partial)
    lane = work.lane

    def wide(kx, rows):
        return jnp.concatenate([stack[kx, rows, :], top[kx, rows, :]], axis=1)

    work.multiply(
        lambda kx, rows: jnp.concatenate([stack[kx, rows, :], below[kx, rows, :]], axis=1),
        kernels[4],
    )

    def finish_top(rows, at):
        value = work.collect(at, 1) + biases[4:5, :]
        pre[0, rows, :] = value

        def keep(kx, value):
            top[kx, rows, :] = value + below[kx, rows, :]

        work.spread(keep, leaky(value), 1)

    work.strips(finish_top)
    for index in range(6, 12):
        if index == 6:
            work.multiply(wide, kernels[index])
        else:
            work.multiply(lambda kx, rows, index=index: ctx[index - 7, kx, rows, :], kernels[index])

        def finish(rows, at, index=index):
            value = work.collect(at, LAYERS[index]["dil"]) + biases[index : index + 1, :]
            pre[index - 5, rows, :] = value

            def keep(kx, value):
                ctx[index - 6, kx, rows, :] = value

            work.spread(keep, leaky(value), LAYERS[index + 1]["dil"])

        work.strips(finish)

    def head(i):
        rows = rows_at(i * MT, MT, MT)
        product = lax.dot_general(wide(1, rows), kernels[5][...], NT, preferred_element_type=F32)
        product = product + lax.dot_general(
            ctx[5, 1, rows, :], kernels[12][...], NT, preferred_element_type=F32
        )
        taps[0, rows_at(RIM + i * MT, MT, MT), :] = product

    for i in range(PX // MT):
        head(i)

    row = iota((LANES, LANES), 0)
    col = iota((LANES, LANES), 1)
    used = (col < 18) & (row % 2 == col % 2)
    fold = jnp.where(used & (row < 18), 1.0, 0.0)
    copies = jnp.where(used & (row < 2), 1.0, 0.0).astype(BF16)
    pick = jnp.where(used & (row >= 2 * FC + 4) & (row < 2 * FC + 6), 1.0, 0.0).astype(BF16)
    marked = jnp.where(row == 2 * FC + 6, 1.0, 0.0).astype(BF16)
    shared = sum(
        jnp.dot(jnp.broadcast_to(b, (8, LANES)).astype(BF16), copies, preferred_element_type=F32)
        for b in (biases[5:6, :], biases[12:13, :])
    )[:1]

    def settle(rows, at):
        total = None
        for kx in range(3):
            part = None
            for ky in range(3):
                tile = taps[0, rows_at(RIM + at + (ky - 1) * PW, STRIP, PW), :]
                tile = jnp.where(lane // 2 == ky * 3 + kx, tile, 0.0)
                part = tile if part is None else part + tile
            part = work.inside(part, kx - 1)
            total = part if total is None else total + part
        motion = (
            jnp.dot(total, fold, preferred_element_type=F32, precision=lax.Precision.HIGHEST)
            + shared
        )
        motion_out[:, rows] = motion.T[: motion_out.shape[0]]
        own = joined[rows, :]
        aim = jnp.dot(own, pick, preferred_element_type=F32)
        mask = jnp.dot(own, marked, preferred_element_type=F32)
        mismatch = motion - aim
        square = mismatch * mismatch
        other = jnp.where(
            lane % 2 == 0, pltpu.roll(square, LANES - 1, 1), pltpu.roll(square, 1, 1)
        )
        length = jnp.sqrt(square + other + EPE_EPS)
        height = (iota((STRIP, LANES), 0) + at) // PW
        interior = (
            (height >= MARGIN)
            & (height < PH - MARGIN)
            & (work.column >= MARGIN)
            & (work.column < PW - MARGIN)
            & (lane < 18)
        )
        grad = jnp.where(interior, weighting * mask * mismatch / length, 0.0)
        grad = grad.astype(BF16).astype(F32)
        work.count_bias(5, grad)
        work.spread_grad(at, grad, 1)

    work.strips(settle)
    partial[12] = partial[5]

    def choose(rows, at):
        total = None
        for kx in range(3):
            for ky in range(3):
                tile = moved[kx, rows_at(RIM + at - (ky - 1) * PW, STRIP, PW), :].astype(F32)
                tile = jnp.where(lane // 2 == ky * 3 + kx, tile, 0.0)
                total = tile if total is None else total + tile
        ghead[rows, :] = total.astype(BF16)

    work.strips(choose)
    grads[5][:, : 4 * LANES] = lax.dot_general(
        ghead[...], stack[1], TN, preferred_element_type=F32
    ).astype(BF16)
    grads[5][:, 4 * LANES :] = lax.dot_general(
        ghead[...], top[1], TN, preferred_element_type=F32
    ).astype(BF16)
    grads[12][...] = lax.dot_general(
        ghead[...], ctx[5, 1], TN, preferred_element_type=F32
    ).astype(BF16)

    def head_back(i):
        rows = rows_at(i * MT, MT, MT)
        dstack[rows, :] = jnp.dot(ghead[rows, :], kernels[5][...], preferred_element_type=F32)
        dcur[rows, :] = jnp.dot(ghead[rows, :], kernels[12][...], preferred_element_type=F32)

    for i in range(PX // MT):
        head_back(i)

    def store_current(rows, value):
        dcur[rows, :] = value

    def store_stack(rows, value):
        dstack[rows, :] += value

    for index in range(11, 6, -1):
        work.back(
            index,
            lambda rows: dcur[rows, :],
            lambda rows, index=index: pre[index - 5, rows, :],
            lambda kx, index=index: ctx[index - 7, kx],
            kernels[index],
            grads[index],
            store_current,
        )
    work.back(
        6,
        lambda rows: dcur[rows, :],
        lambda rows: pre[1, rows, :],
        lambda kx: jnp.concatenate([stack[kx], top[kx]], axis=1),
        kernels[6],
        grads[6],
        store_stack,
    )
    work.back(
        4,
        lambda rows: dstack[rows, 4 * LANES :],
        lambda rows: pre[0, rows, :],
        lambda kx: jnp.concatenate([stack[kx], top[kx]], axis=1),
        kernels[4],
        grads[4],
        store_stack,
    )
    bias_out[...] = partial[...].sum(1)


CONTEXT_SCRATCH = (
    pltpu.VMEM((3, PX, LANES), BF16),
    pltpu.VMEM((6, 3, PX, LANES), BF16),
    pltpu.VMEM((7, PX, LANES), F32),
    pltpu.VMEM((3, PX + 2 * RIM, LANES), F32),
    pltpu.VMEM((3, PX + 2 * RIM, LANES), BF16),
    pltpu.VMEM((PX, LANES), F32),
    pltpu.VMEM((PX, LANES), BF16),
    pltpu.VMEM((16, 8, LANES), F32),
)


def late(gather_at, pack_at, parts, carried, stack, below, joined, counts, pixels, end, pieces, size):
    smem = pl.BlockSpec(memory_space=pltpu.SMEM)
    vmem = pl.BlockSpec(memory_space=pltpu.VMEM)
    anywhere = pl.BlockSpec(memory_space=pltpu.HBM)
    shapes = [pltpu.VMEM(LAYERS[i]["shape"], BF16) for i in LATE]
    return pl.pallas_call(
        functools.partial(late_kernel, end - CUT, len(parts[0]), len(counts), float(pixels)),
        out_shape=[
            jax.ShapeDtypeStruct((8, PX), F32),
            jax.ShapeDtypeStruct((PX, 5 * LANES), F32),
            jax.ShapeDtypeStruct((16, LANES), F32),
            jax.ShapeDtypeStruct((pieces, size, LANES), BF16),
            jax.ShapeDtypeStruct((pieces, size, LANES), BF16),
            jax.ShapeDtypeStruct((end // 2 - CUT, LANES), BF16),
        ],
        in_specs=[smem] * 2 + [vmem] + [anywhere] * 3 + [vmem] * (len(counts) + 2 * len(parts[0])),
        out_specs=[vmem, anywhere, vmem, vmem, vmem, vmem],
        scratch_shapes=[
            ORDER,
            pltpu.VMEM((16, LANES), F32),
            pltpu.VMEM((PX, 5 * LANES), F32),
            pltpu.VMEM(stack.shape, BF16),
            pltpu.VMEM(below.shape, BF16),
            pltpu.VMEM(joined.shape, BF16),
            pltpu.SemaphoreType.DMA((4,)),
            *shapes,
            *shapes,
        ],
        compiler_params=pltpu.CompilerParams(vmem_limit_bytes=60 * 2**20),
        cost_estimate=pl.CostEstimate(
            flops=80_000_000_000, bytes_accessed=20_000_000, transcendentals=0
        ),
        name="context",
    )(gather_at, pack_at, carried, stack, below, joined, *counts, *parts[0], *parts[1])


def correlate_back(joined, cost, grads, second, dsecond, collected, out):
    load_second(joined, second)
    dsecond[...] = jnp.zeros_like(dsecond)
    lane = iota((ROWS4, LANES), 1)
    narrow = iota((PW, LANES), 1)

    def body(i):
        rows = rows_at(i * ROWS4, ROWS4, ROWS4)
        own = joined[rows, :]
        first = jnp.where(lane < FC, own.astype(F32), 0.0).astype(BF16)
        grad = grads[rows, :LANES]
        volume = grad * leaky_slope(cost[rows, :]) * (1.0 / FC)
        dfirst = jnp.zeros((ROWS4, LANES), F32)
        for g in range(4):
            pieces = []
            for yy in range(4):
                piece = jnp.zeros((PW, LANES), F32)
                own_rows = volume[yy * PW : (yy + 1) * PW, :]
                for t in range(3 * g, 3 * g + 3):
                    dy = t - yy
                    if dy < 0 or dy >= EXT:
                        continue
                    part = jnp.where(
                        (narrow >= EXT * dy) & (narrow < EXT * (dy + 1)), own_rows, 0.0
                    )
                    shift = (-band_shift(dy, t % 3)) % LANES
                    piece = piece + pltpu.roll(part, shift, 1)
                pieces.append(pltpu.roll(piece, 0, 1, stride=1, stride_axis=0))
            band = jnp.concatenate(pieces, axis=0).astype(BF16)
            at = rows_at((4 * i + 3 * g) * PITCH, LANES)
            dfirst = dfirst + jnp.dot(
                band, second[at, :].astype(BF16), preferred_element_type=F32
            )
            dsecond[at, :] += lax.dot_general(band, first, TN, preferred_element_type=F32)
        direct = pltpu.roll(grad, LANES - NCOST, 1)
        coarse = pltpu.roll(grad, LANES + 2 * FC - NCOST - FC, 1)
        filled = jnp.where(lane < FC, dfirst + direct, 0.0)
        filled = jnp.where((lane >= 2 * FC) & (lane < 2 * FC + 4), coarse, filled)
        collected[rows, :] = filled

    for i in range(PH // 4):
        body(i)
    for s in range((PH - 2 * MARGIN) // 4):
        pieces = []
        for yy in range(4):
            at = (MARGIN + 4 * s + yy + SR) * PITCH + 8
            pieces.append(dsecond[at : at + PW, :])
        other = pltpu.roll(jnp.concatenate(pieces, axis=0), FC, 1)
        start = (MARGIN + 4 * s) * PW
        tile = collected[start : start + ROWS4, :]
        tile = jnp.where((lane >= FC) & (lane < 2 * FC), other, tile)
        out[s] = tile.T[: out.shape[1]].astype(BF16)


def early_kernel(
    pack_at,
    stack_in,
    pre_in,
    dstack_in,
    cost_in,
    joined_in,
    bias_in,
    carried,
    k1,
    k2,
    k3,
    k4,
    picture_out,
    keep,
    send,
    order,
    stack,
    pre,
    dstack,
    cost,
    joined,
    bias_out,
    copied,
    *grads,
):
    sources = (dstack_in, pre_in, stack_in, cost_in, joined_in)
    targets = (dstack, pre, stack, cost, joined)
    loads = [
        pltpu.make_async_copy(source, target, copied.at[i])
        for i, (source, target) in enumerate(zip(sources, targets))
    ]
    for load in loads:
        load.start()
    fill_order(order)
    for load in loads[:2]:
        load.wait()

    def first(*scratch):
        dense_back(
            stack,
            pre,
            dstack,
            cost,
            joined,
            bias_in,
            (k1, k2, k3, k4),
            picture_out,
            bias_out,
            grads,
            loads[2:],
            *scratch,
        )

    pl.run_scoped(first, *DENSE_SCRATCH)

    def second(*scratch):
        pack_gradients(
            EARLY, 0, pack_at, grads, bias_out, carried, (keep, send), None, order, scratch
        )

    pl.run_scoped(second, *pack_scratch(EARLY, CUT + carried.shape[0]))


def dense_back(
    stack,
    pre,
    dstack,
    cost,
    joined,
    bias_in,
    kernels,
    picture_out,
    bias_out,
    grads,
    loads,
    moved,
    dwide,
    partial,
    second,
    dsecond,
    collected,
):
    work = Work(None, moved, partial)
    partial[...] = jnp.zeros_like(partial)
    dwide[...] = dstack[:, : 4 * LANES]

    def store_stack(rows, value):
        dwide[rows, : value.shape[1]] += value

    for index in range(3, -1, -1):
        width = LAYERS[index]["blocks"] * LANES

        def load_grad(rows, index=index):
            if index == 3:
                return dstack[rows, 4 * LANES :]
            return dwide[rows, (index + 1) * LANES : (index + 2) * LANES]

        work.back(
            index,
            load_grad,
            lambda rows, index=index: pre[index, rows, :],
            lambda kx, width=width: stack[kx, :, :width],
            kernels[index],
            grads[index],
            store_stack,
            loads if index == 3 else (),
        )
    bias_out[...] = partial[...].sum(1) + bias_in[...]
    correlate_back(joined, cost, dwide, second, dsecond, collected, picture_out)


DENSE_SCRATCH = (
    pltpu.VMEM((3, PX + 2 * RIM, LANES), BF16),
    pltpu.VMEM((PX, 4 * LANES), F32),
    pltpu.VMEM((16, 8, LANES), F32),
    pltpu.VMEM((SEC_ROWS, LANES), F32),
    pltpu.VMEM((SEC_ROWS, LANES), F32),
    pltpu.VMEM((PX, LANES), F32),
)


def backward(
    pack_at, stack, pre, dstack, cost, joined, bias_grads, carried, kernels, blocks, channels, pieces, size
):
    vmem = pl.BlockSpec(memory_space=pltpu.VMEM)
    large = (stack, pre, dstack, cost, joined)
    return pl.pallas_call(
        early_kernel,
        out_shape=[
            jax.ShapeDtypeStruct((blocks, channels, LANES), BF16),
            jax.ShapeDtypeStruct((pieces, size, LANES), BF16),
            jax.ShapeDtypeStruct((pieces, size, LANES), BF16),
        ],
        in_specs=[pl.BlockSpec(memory_space=pltpu.SMEM)]
        + [pl.BlockSpec(memory_space=pltpu.HBM)] * 5
        + [vmem] * 6,
        scratch_shapes=[
            ORDER,
            *[pltpu.VMEM(a.shape, a.dtype) for a in large],
            pltpu.VMEM((16, LANES), F32),
            pltpu.SemaphoreType.DMA((5,)),
            *[pltpu.VMEM(LAYERS[i]["shape"], BF16) for i in EARLY],
        ],
        compiler_params=pltpu.CompilerParams(vmem_limit_bytes=60 * 2**20),
        cost_estimate=pl.CostEstimate(
            flops=40_000_000_000, bytes_accessed=20_000_000, transcendentals=0
        ),
        name="dense_backward",
    )(pack_at, *large, bias_grads, carried, *kernels)


def update(weights, momentum, average, gradient):
    gradient = gradient + DECAY_RATE * weights
    renewed = MOMENTUM_RATE * momentum + gradient
    stepped = weights - LEARN_RATE * (gradient + MOMENTUM_RATE * renewed)
    return (stepped, renewed, AVERAGE_DECAY * average + (1.0 - AVERAGE_DECAY) * stepped)


def swapped(value, axis, step):
    count = lax.axis_size(axis)
    return lax.ppermute(value, axis, [(i, i ^ step) for i in range(count)])


def added(one, two):
    return (one.astype(F32) + two.astype(F32)).astype(BF16)


def core_sum(keep, send, groups, devices):
    got = swapped(send, "grp", 1)
    pieces = keep.shape[0] // 2
    if groups == 2:
        return [added(keep, got)]
    return [added(keep[pieces:], got[pieces:]), added(keep[:pieces], got[:pieces])]


def x_sum(value, groups, devices):
    half = devices // 2
    step = groups // 4
    if not step:
        value = value[0]
        return [value[j] for j in range(half)]
    away, value = value
    got = swapped(away, "grp", 2 * step)
    while step > 1:
        value = added(value, got)
        step //= 2
        pieces = value.shape[0] // 2
        got = swapped(value[pieces:], "grp", 2 * step)
        value = value[:pieces]
    return [added(value[j], got[j]) for j in range(half)]


def dev_sum(pieces):
    total = pieces[0].astype(F32)
    for j in range(1, len(pieces)):
        total = total + swapped(pieces[j], "dev", j).astype(F32)
    return total


def shared_x(value, groups):
    x_size = groups // 2
    x = lax.axis_index("grp") // 2
    held = [0]
    parts = [value]
    step = 1
    while step < x_size:
        parts = parts + [swapped(p, "grp", 2 * step) for p in parts]
        held = held + [j ^ step for j in held]
        step *= 2
    out = []
    for i in range(x_size):
        piece = parts[0]
        for j, part in zip(held[1:], parts[1:]):
            piece = jnp.where((x ^ j) == i, part, piece)
        out.append(piece)
    return jnp.concatenate(out)


def shards(features, coarse_flow, target, valid_mask, weights, momentum, average):
    groups = lax.axis_size("grp")
    devices = lax.axis_size("dev")
    own_rows = features.shape[2]
    width = features.shape[3]
    breadth = width // devices
    height = own_rows * devices
    assert breadth + 2 * MARGIN == PW and height + 2 * MARGIN == PH
    core = lax.axis_index("grp") % 2
    me = lax.axis_index("dev")
    half = devices // 2
    early = me < half
    rows = weights.shape[0] // LANES
    x_size = groups // 2
    size = -(-(rows // 2) // (16 * x_size)) * 16 * x_size
    table = weights.reshape(rows, LANES)
    own = lax.dynamic_slice(table, (core * (rows - size), 0), (size, LANES)).astype(BF16)

    received = windows(features, coarse_flow, target, valid_mask, devices)
    received = lax.all_to_all(received, "dev", split_axis=0, concat_axis=0, tiled=True)

    across = swapped(own, "dev", half)
    across, received = lax.optimization_barrier((across, received))
    both = jnp.stack([core, 1 - core])[:, None] * (rows - size)
    part, last = {0: jnp.where(early, own, across)}, {0: jnp.where(early, across, own)}
    steps = [half >> i for i in range(1, half.bit_length())]

    def grow(pieces, step):
        for j in list(pieces):
            if j ^ step not in pieces:
                pieces[j ^ step] = swapped(pieces[j], "dev", step)

    first_y = swapped(part[0], "dev", 1)
    for step in steps[:-1]:
        grow(part, step)
    held = list(part)
    *tied, received, last[0] = lax.optimization_barrier((*part.values(), received, last[0]))
    part = dict(zip(held, tied))
    part[1] = first_y
    grow(part, 1)
    for step in steps[:-1]:
        grow(last, step)
    per = 4 // own_rows
    blocks = devices // per
    received = received.reshape(blocks, per, CHANNELS, own_rows * PW)
    received = jnp.swapaxes(received, 1, 2).reshape(blocks, CHANNELS, LANES)
    stack0, cost, joined, counted = correlate(received)
    held, held_last = list(part), list(last)
    *tied, stack0 = lax.optimization_barrier((*part.values(), *last.values(), stack0))
    part = dict(zip(held, tied))
    last = dict(zip(held_last, tied[len(held) :]))
    counts = [counted] + [swapped(counted, "grp", j) for j in range(1, groups)]
    grow(last, 1)
    held_last = list(last)

    def gathered(pieces, keys, late_half):
        sources = jnp.array(keys, jnp.int32) ^ (me % half)
        own = [pieces[j] for j in keys]
        place = (sources + half * late_half)[None] * rows + both
        return place, (own, [swapped(p, "grp", 1) for p in own])

    place, parts = gathered(part, held, 0)
    kernels, carried, stack, below, pre = forward(place, parts, stack0, half * rows)
    *tied, stack = lax.optimization_barrier((*counts, *last.values(), stack))
    counts, last = tied[:groups], dict(zip(held_last, tied[groups:]))
    place, parts = gathered(last, held_last, 1)
    x = lax.axis_index("grp") // 2
    part_x = (jnp.arange(x_size, dtype=jnp.int32) ^ x) * (size // x_size)
    part_dev = (jnp.arange(half, dtype=jnp.int32) ^ (me % half)) * rows
    pack_at = (part_x[:, None] + part_dev[None]).reshape(1, -1) + both
    pieces = (half * x_size, size // x_size)
    motion, dstack, bias_grads, keep, send, carried = late(
        place,
        pack_at + half * rows,
        parts,
        carried,
        stack,
        below,
        joined,
        counts,
        groups * height * width,
        devices * rows,
        *pieces,
    )
    flow = motion[:2].reshape(1, 2, PH, PW)[
        :, :, MARGIN : MARGIN + height, MARGIN : MARGIN + breadth
    ]
    late_sum = core_sum(keep, send, groups, devices)
    late_sum, dstack = lax.optimization_barrier((late_sum, dstack))
    late_sum = x_sum(late_sum, groups, devices)
    tiles, keep, send = backward(
        pack_at,
        stack,
        pre,
        dstack,
        cost,
        joined,
        bias_grads,
        carried,
        kernels,
        blocks,
        CHANNELS,
        *pieces,
    )
    late_sum, keep, send = lax.optimization_barrier((late_sum, keep, send))
    late_sum = dev_sum(late_sum)
    early_sum = core_sum(keep, send, groups, devices)
    tiles = tiles.reshape(blocks, CHANNELS, per, own_rows * PW)
    tiles = jnp.swapaxes(tiles, 1, 2).reshape(devices, CHANNELS, own_rows * PW)
    returned = lax.all_to_all(tiles, "dev", split_axis=0, concat_axis=0, tiled=True)
    early_sum = x_sum(early_sum, groups, devices)
    early_sum, late_sum, returned = lax.optimization_barrier((early_sum, late_sum, returned))
    early_sum = dev_sum(early_sum)
    total = jnp.where(early, early_sum, late_sum)
    other = jnp.where(early, late_sum, early_sum).astype(BF16)
    total = (total + swapped(other, "dev", half).astype(F32)).astype(BF16)
    total = shared_x(total, groups)
    rest = swapped(total, "grp", 1)
    low = jnp.where(core == 0, total, rest)
    high = jnp.where(core == 0, rest, total)
    total_grad = jnp.concatenate([low[: rows - size], high]).astype(F32).reshape(-1)

    returned = returned.reshape(devices, CHANNELS, own_rows, PW).astype(F32)
    wide = jnp.transpose(returned, (1, 2, 0, 3))
    centre = wide[..., MARGIN : MARGIN + breadth]
    left = wide[:, :, 1:, :MARGIN]
    right = wide[:, :, :-1, MARGIN + breadth :]
    none = ((0, 0), (0, 0))
    centre = centre + jnp.pad(left, (*none, (0, 1), (breadth - MARGIN, 0)))
    centre = centre + jnp.pad(right, (*none, (1, 0), (0, breadth - MARGIN)))
    row_grad = centre.reshape(1, CHANNELS, own_rows, width)
    feature_grad = row_grad[:, : 2 * FC]
    coarse_grad = row_grad[:, 2 * FC : 2 * FC + 4]

    new_weights, new_momentum, new_average = update(weights, momentum, average, total_grad)
    return (
        flow,
        feature_grad,
        coarse_grad,
        new_weights,
        new_momentum,
        new_average,
        new_weights.astype(BF16),
    )


def solution(mesh):
    in_specs = (
        P("grp", None, "dev", None),
        P("grp", None, "dev", None),
        P("grp", None, "dev", None),
        P("grp", "dev", None),
        P("dev"),
        P("dev"),
        P("dev"),
    )
    out_specs = (
        P("grp", None, None, "dev"),
        P("grp", None, "dev", None),
        P("grp", None, "dev", None),
        P("dev"),
        P("dev"),
        P("dev"),
        P("dev"),
    )
    return jax.shard_map(shards, mesh=mesh, in_specs=in_specs, out_specs=out_specs, check_vma=False)
```

```python
import functools

import jax
import jax.numpy as jnp
from jax import lax
from jax.experimental import pallas as pl
from jax.experimental.pallas import tpu as pltpu
from jax.sharding import PartitionSpec as P

FC = 32
SR = 4
EXT = 2 * SR + 1
NCOST = EXT * EXT
NS0 = NCOST + FC + 4
DENSE = (128, 128, 96, 64, 32)
CONTEXT = (128, 128, 128, 96, 64, 32, 2)
DILATIONS = (1, 2, 4, 8, 16, 1, 1)
MARGIN = 8

SLOPE = 0.1
EPE_EPS = 0.01
MOMENTUM_RATE = 0.5
AVERAGE_DECAY = 0.5
LEARN_RATE = 0.001
DECAY_RATE = 0.0001

LANES = 128
CHANNELS = 72
PH = 48
PW = 32
PX = PH * PW
RIM = 16 * PW
STRIP = 128
MT = 768
PITCH = 40
F32 = jnp.float32
BF16 = jnp.bfloat16
NT = (((1,), (1,)), ((), ()))
TN = (((0,), (0,)), ((), ()))


def layer_table():
    places = [(NS0, 0, 0), (128, 1, 0), (128, 2, 0), (96, 3, 0), (64, 4, 0), (32, 4, 64)]
    layers = []
    offset = 0

    def add(pieces, outgoing, dilation, shift):
        nonlocal offset
        incoming = sum(n for n, _, _ in pieces)
        row = 9 * incoming
        segments = []
        at = 0
        for n, block, lane in pieces:
            first, over = 9 * at // LANES, 9 * at % LANES
            slot = -(-(9 * lane - over) // LANES)
            back = 9 * lane - over - LANES * slot
            chunks = -(-(over + 9 * n) // LANES)
            segments.append(
                dict(n=n, block=block, lane=lane, first=first, slot=slot, back=back, chunks=chunks)
            )
            at += n
        blocks = 1 + max(b for _, b, _ in pieces)
        layers.append(
            dict(
                out=outgoing,
                row=row,
                chunks=-(-row // LANES),
                start=offset,
                dil=dilation,
                shift=shift,
                segments=segments,
                blocks=blocks,
                bias=offset + row * outgoing,
                shape=(LANES, blocks * LANES) if outgoing == 2 else (3 * LANES, 3 * blocks * LANES),
            )
        )
        offset += row * outgoing + outgoing

    for i, outgoing in enumerate(DENSE):
        add(places[i::-1], outgoing, 1, 64 if i == 4 else 0)
    add(places[::-1], 2, 1, 0)
    add(places[::-1], CONTEXT[0], DILATIONS[0], 0)
    for i in range(1, 7):
        add([(CONTEXT[i - 1], 0, 0)], CONTEXT[i], DILATIONS[i], 0)
    return layers, offset


LAYERS, COUNT = layer_table()
EARLY = (0, 1, 2, 3)
LATE = (4, 5, 6, 7, 8, 9, 10, 11, 12)
CUT = LAYERS[4]["start"] // LANES // 16 * 16


def sort_groups(indices):
    order = [(segment["back"], i, s) for i in indices for s, segment in enumerate(LAYERS[i]["segments"])]
    order.sort(key=lambda t: -t[0])
    at = 0
    groups = {}
    classes = []
    for back, i, s in order:
        if not classes or classes[-1][0] != back:
            classes.append([back, at, at])
        groups[i, s] = at
        at += -(-LAYERS[i]["out"] // 16) * 16
        classes[-1][2] = at
    return groups, classes, at


def iota(shape, dim):
    return lax.broadcasted_iota(jnp.int32, shape, dim)


def rows_at(start, size, step=8):
    if isinstance(start, int):
        return pl.ds(start, size)
    return pl.ds(pl.multiple_of(start, step), size)


def sigmoid(v):
    return 0.5 * jnp.tanh(0.5 * v) + 0.5


def leaky(v):
    return SLOPE * v + (1.0 - SLOPE) * v * sigmoid(v)


def leaky_slope(v):
    s = sigmoid(v)
    return SLOPE + (1.0 - SLOPE) * (s + v * s * (1.0 - s))


def loop(count, body):
    def step(i, carry):
        body(i)
        return carry

    lax.fori_loop(0, count, step, 0)


def fill_order(order):
    order[:LANES, :] = jnp.zeros((LANES, 9 * LANES), BF16)
    order[10 * LANES :, :] = jnp.zeros((LANES, 9 * LANES), BF16)
    for k in range(9):
        for m in range(9):
            row = iota((LANES, LANES), 0) + m * LANES
            col = iota((LANES, LANES), 1)
            order[(m + 1) * LANES : (m + 2) * LANES, k * LANES : (k + 1) * LANES] = jnp.where(
                row == 9 * col + k, 1.0, 0.0
            ).astype(BF16)


ORDER = pltpu.VMEM((11 * LANES, 9 * LANES), BF16)


def within(n, lane):
    spot = iota((1, LANES), 1)
    return jnp.where((spot >= lane) & (spot < lane + n), 1.0, 0.0).astype(BF16)


def pitch_of(chunks):
    return -(-chunks // 8) * 8


def unpack_scratch(indices, count):
    _, _, group_rows = sort_groups(indices)
    return (
        pltpu.VMEM((count + 64, LANES), F32),
        pltpu.VMEM((48 * LANES, LANES), F32),
        pltpu.VMEM((group_rows, 10 * LANES), BF16),
        pltpu.VMEM((group_rows, 9 * LANES), BF16),
        pltpu.VMEM((LANES, 5 * LANES), F32),
    )


def unpack_weights(indices, base, place_at, parts, carried, outs, bias_out, carry_out, order, scratch):
    whole, slabs, aligned, result, heads = scratch
    count = whole.shape[0] - 64
    groups, classes, _ = sort_groups(indices)
    if base:
        whole[: carried.shape[0], :] = carried[...].astype(F32)
    for at_part, pieces in enumerate(parts):
        for j, piece in enumerate(pieces):
            size = piece.shape[0]
            to = place_at[at_part, j] - base

            def widen(i, piece=piece, to=to):
                whole[pl.ds(to + i * 16, 16), :] = piece[rows_at(i * 16, 16, 16), :].astype(F32)

            lax.fori_loop(0, size // 16, lambda i, c: (widen(i), c)[1], 0, unroll=8)
    whole[count:, :] = jnp.zeros((64, LANES), F32)
    if not base:
        carry_out[...] = whole[CUT:count, :].astype(BF16)
    bias_out[...] = jnp.zeros_like(bias_out)

    for at_out, index in enumerate(indices):
        layer = LAYERS[index]
        outgoing = layer["out"]
        kept = -(-outgoing // 16) * 16
        start = layer["start"] - base * LANES
        spot = iota((kept, LANES), 1)
        pitch = pitch_of(layer["chunks"] + 1)
        still = layer["row"] % LANES == 0
        if not still:
            unroll = min(32, outgoing)

            def take(i, unroll=unroll, row=layer["row"], start=start, pitch=pitch):
                for u in range(unroll):
                    o = i * unroll + u
                    first = start + o * row
                    turn = (LANES - (first & (LANES - 1))) & (LANES - 1)
                    for v in range(pitch // 8):
                        tile = whole[pl.ds((first >> 7) + 8 * v, 8), :]
                        slabs[rows_at(o * pitch + 8 * v, 8), :] = pltpu.roll(tile, turn, 1)

            for i in range(outgoing // unroll):
                take(i)
            off = (start + iota((kept, LANES), 0) * layer["row"]) & (LANES - 1)
        chunks = {}
        for t in range(layer["chunks"]):
            if still:
                row, fixed = divmod(start, LANES)
                step = layer["row"] // LANES
                here = whole[pl.ds(row + t, kept, stride=step), :]
                after = whole[pl.ds(row + t + 1, kept, stride=step), :]
                chunk = jnp.where(spot >= fixed, here, after)
                chunk = pltpu.roll(chunk, (LANES - fixed) % LANES, 1)
            else:
                here = slabs[pl.ds(t, kept, stride=pitch), :]
                after = slabs[pl.ds(t + 1, kept, stride=pitch), :]
                chunk = jnp.where(spot < LANES - off, here, after)
            chunk = chunk.astype(BF16)
            for s, segment in enumerate(layer["segments"]):
                to = t - segment["first"]
                if 0 <= to < segment["chunks"]:
                    to += segment["slot"]
                    at = groups[index, s]
                    aligned[at : at + kept, to * LANES : (to + 1) * LANES] = chunk
        for s, segment in enumerate(layer["segments"]):
            at = groups[index, s]
            for to in range(10):
                if not segment["slot"] <= to < segment["slot"] + segment["chunks"]:
                    aligned[at : at + kept, to * LANES : (to + 1) * LANES] = jnp.zeros(
                        (kept, LANES), BF16
                    )
        shift = layer["shift"]
        first = layer["bias"] - base * LANES - shift
        row, fixed = divmod(first, LANES)
        here = pltpu.roll(whole[row : row + 1, :], (LANES - fixed) % LANES, 1)
        after = pltpu.roll(whole[row + 1 : row + 2, :], (LANES - fixed) % LANES, 1)
        line = iota((1, LANES), 1)
        value = jnp.where(line < LANES - fixed, here, after)
        bias_out[index : index + 1, :] = jnp.where(
            (line >= shift) & (line < shift + outgoing), value, 0.0
        )

    for back, low, high in classes:
        wide = 9 if back == 0 else 10
        result[low:high, :] = jnp.dot(
            aligned[low:high, : wide * LANES],
            order[LANES + back : LANES + back + wide * LANES, :],
            preferred_element_type=F32,
        ).astype(BF16)

    for at_out, index in enumerate(indices):
        layer = LAYERS[index]
        outgoing = layer["out"]
        shift = layer["shift"]
        out = outs[at_out]
        width = layer["blocks"] * LANES
        if outgoing == 2:
            heads[...] = jnp.zeros_like(heads)
        elif outgoing < LANES:
            out[...] = jnp.zeros_like(out)
        kept = -(-outgoing // 16) * 16
        for block in range(layer["blocks"]):
            for k in range(9):
                total = None
                for s, segment in enumerate(layer["segments"]):
                    if segment["block"] != block:
                        continue
                    at = groups[index, s]
                    tile = result[at : at + kept, k * LANES : (k + 1) * LANES]
                    if segment["n"] < LANES:
                        tile = tile * within(segment["n"], segment["lane"])
                    total = tile if total is None else total + tile
                if outgoing == 2:
                    heads[2 * k : 2 * k + 2, block * LANES : (block + 1) * LANES] = total.astype(
                        F32
                    )[:2]
                else:
                    ky, kx = divmod(k, 3)
                    at = kx * width + block * LANES
                    out[ky * LANES + shift : ky * LANES + shift + outgoing, at : at + LANES] = total
        if outgoing == 2:
            out[...] = heads[:, :width].astype(BF16)


def pack_scratch(indices, count):
    _, _, group_rows = sort_groups(indices)
    return (
        pltpu.VMEM((count + 64, LANES), F32),
        pltpu.VMEM((40 * LANES + 64, LANES), F32),
        pltpu.VMEM((group_rows, 9 * LANES), BF16),
        pltpu.VMEM((group_rows, 10 * LANES), F32),
        pltpu.VMEM((LANES + 16, 5 * LANES), F32),
    )


def pack_gradients(indices, base, place_at, grads, bias_in, carried, halves, carry_out, order, scratch):
    whole, slabs, gathered, result, heads = scratch
    count = whole.shape[0] - 64
    groups, classes, _ = sort_groups(indices)
    for at_in, index in enumerate(indices):
        layer = LAYERS[index]
        outgoing = layer["out"]
        shift = layer["shift"]
        grad = grads[at_in]
        width = layer["blocks"] * LANES
        if outgoing == 2:
            heads[:LANES, :width] = grad[...].astype(F32)
            heads[LANES:, :] = jnp.zeros((16, heads.shape[1]), F32)
        for s, segment in enumerate(layer["segments"]):
            at = groups[index, s]
            block = segment["block"]
            for k in range(9):
                if outgoing == 2:
                    tile = heads[2 * k : 2 * k + 16, block * LANES : (block + 1) * LANES]
                    tile = tile.astype(BF16)
                else:
                    ky, kx = divmod(k, 3)
                    column = kx * width + block * LANES
                    tile = grad[
                        ky * LANES + shift : ky * LANES + shift + outgoing, column : column + LANES
                    ]
                if segment["n"] < LANES:
                    tile = tile * within(segment["n"], segment["lane"])
                gathered[at : at + tile.shape[0], k * LANES : (k + 1) * LANES] = tile

    for back, low, high in classes:
        wide = 9 if back == 0 else 10
        result[low:high, : wide * LANES] = lax.dot_general(
            gathered[low:high, :],
            order[LANES + back : LANES + back + wide * LANES, :],
            NT,
            preferred_element_type=F32,
        )

    lane = iota((8, LANES), 1)
    sub = iota((8, LANES), 0)

    for at_in, index in enumerate(indices):
        layer = LAYERS[index]
        outgoing = layer["out"]
        start = layer["start"] - base * LANES
        still = layer["row"] % LANES == 0
        pitch = pitch_of(layer["chunks"])
        spot = iota((outgoing, LANES), 1)
        turned = []
        for t in range(layer["chunks"]):
            chunk = None
            for s, segment in enumerate(layer["segments"]):
                to = t - segment["first"]
                if 0 <= to < segment["chunks"]:
                    to += segment["slot"]
                    at = groups[index, s]
                    tile = result[at : at + outgoing, to * LANES : (to + 1) * LANES]
                    chunk = tile if chunk is None else chunk + tile
            if still:
                turned.append(pltpu.roll(chunk, start % LANES, 1))
            else:
                slabs[pl.ds(t, outgoing, stride=pitch), :] = chunk
        if still:
            row, fixed = divmod(start, LANES)
            step = layer["row"] // LANES
            for t in range(step):
                before = turned[t - 1] if t else pltpu.roll(turned[-1], 1, 0)
                value = jnp.where(spot >= fixed, turned[t], before)
                if t == 0:
                    kept = whole[row : row + 1, :]
                    top = (iota((outgoing, LANES), 0) == 0) & (spot < fixed)
                    value = jnp.where(top, kept, value)
                whole[pl.ds(row + t, outgoing, stride=step), :] = value
            last = pltpu.roll(turned[-1][outgoing - 8 :, :], 1, 0)
            end = row + step * outgoing
            pltpu.store(whole.at[end : end + 8, :], last, mask=(sub == 0) & (lane < fixed))
        else:
            unroll = min(32, outgoing)

            def put(i, start=start, row=layer["row"], pitch=pitch, unroll=unroll):
                for u in range(unroll):
                    o = i * unroll + u
                    first = start + o * row
                    off = first & (LANES - 1)
                    for v in range(pitch // 8):
                        tile = pltpu.roll(slabs[rows_at(o * pitch + 8 * v, 8), :], off, 1)
                        to = (first >> 7) + 8 * v
                        pltpu.store(whole.at[pl.ds(to, 8), :], tile, mask=lane >= off)
                        pltpu.store(whole.at[pl.ds(to + 1, 8), :], tile, mask=lane < off)

            for i in range(outgoing // unroll):
                put(i)
        line = bias_in[index : index + 1, :]
        first = layer["bias"] - base * LANES
        row, fixed = divmod(first, LANES)
        line = pltpu.roll(line, (fixed - layer["shift"]) % LANES, 1)
        line = jnp.broadcast_to(line, (8, LANES))
        pltpu.store(whole.at[row : row + 8, :], line, mask=(sub == 0) & (lane >= fixed))
        pltpu.store(whole.at[row + 1 : row + 9, :], line, mask=(sub == 0) & (lane < fixed))
    if base:
        end, off = divmod(COUNT - base * LANES, LANES)
        pltpu.store(
            whole.at[end : end + 8, :], jnp.zeros((8, LANES), F32), mask=(sub > 0) | (lane >= off)
        )
        if count > end + 8:
            whole[end + 8 : count, :] = jnp.zeros((count - end - 8, LANES), F32)
        carry_out[...] = whole[: carry_out.shape[0], :].astype(BF16)
    else:
        end, off = divmod(LAYERS[4]["start"], LANES)
        line = carried[...].astype(F32)
        keep = (iota(line.shape, 0) > end - CUT) | (
            (iota(line.shape, 0) == end - CUT) & (iota(line.shape, 1) >= off)
        )
        whole[CUT:count, :] = jnp.where(keep, line, whole[CUT:count, :])
    for half in range(2):
        size = halves[half].shape[1]
        for j in range(halves[half].shape[0]):
            begin = place_at[half, j] - base

            def narrow(i, half=half, j=j, begin=begin):
                halves[half][j, rows_at(i * 16, 16, 16), :] = whole[
                    pl.ds(begin + i * 16, 16), :
                ].astype(BF16)

            lax.fori_loop(0, size // 16, lambda i, c: (narrow(i), c)[1], 0, unroll=8)


ROWS4 = 4 * PW
SEC_ROWS = (PH + 2 * SR) * PITCH + LANES


def load_second(joined, second):
    second[...] = jnp.zeros_like(second)
    keep = iota((PW, LANES), 1) < FC
    for y in range(MARGIN, PH - MARGIN):
        row = joined[y * PW : (y + 1) * PW, :].astype(F32)
        row = jnp.where(keep, pltpu.roll(row, LANES - FC, 1), 0.0)
        at = (y + SR) * PITCH + 8
        second[at : at + PW, :] = row


def start_copies(sources, targets, semaphores):
    copies = [
        pltpu.make_async_copy(source, target, semaphores.at[i])
        for i, (source, target) in enumerate(zip(sources, targets))
    ]
    for copy in copies:
        copy.start()
    return copies


def windows_kernel(*refs):
    out = refs[4]
    features, coarse, target, mask = refs[5:9]
    for copy in start_copies(refs[:4], refs[5:9], refs[9]):
        copy.wait()
    own_rows, width = mask.shape[1:]
    devices = out.shape[0]
    breadth = width // devices
    side = jnp.zeros((CHANNELS - 1, MARGIN), F32)
    arrays = [features[0].astype(F32), coarse[0].astype(F32), target[0].astype(F32)]
    marks = mask[0].astype(F32)
    for r in range(own_rows):
        valid = marks[r : r + 1, :]
        tall = jnp.concatenate([a[:, r, :] for a in arrays] + [valid], axis=0)
        tall = jnp.concatenate([side, tall, side], axis=1)
        count = sum(valid[:, at : at + PW] for at in range(0, width, PW))
        for t in range(devices):
            tile = jnp.concatenate([tall[:, t * breadth : t * breadth + PW], count], axis=0)
            out[t, :, r * PW : (r + 1) * PW] = tile.astype(BF16)


def windows(features, coarse, target, mask, devices):
    return pl.pallas_call(
        windows_kernel,
        out_shape=jax.ShapeDtypeStruct((devices, CHANNELS, mask.shape[1] * PW), BF16),
        in_specs=[pl.BlockSpec(memory_space=pltpu.HBM)] * 4,
        scratch_shapes=[pltpu.VMEM(a.shape, a.dtype) for a in (features, coarse, target, mask)]
        + [pltpu.SemaphoreType.DMA((4,))],
        compiler_params=pltpu.CompilerParams(vmem_limit_bytes=60 * 2**20),
        name="windows",
    )(features, coarse, target, mask)


def band_shift(dy, third):
    return EXT * dy - PITCH * third - (8 - SR)


def correlate_kernel(received, stack0, cost_out, joined_out, second, cost, joined, copied):
    joined[...] = jnp.zeros_like(joined)
    blocks = received.shape[0]
    spare = jnp.zeros((LANES - received.shape[1], LANES), F32)
    for s in range(blocks):
        tile = received[s].astype(F32)
        tile = jnp.concatenate([tile, spare], axis=0).T
        joined[RIM // 2 + s * ROWS4 : RIM // 2 + (s + 1) * ROWS4, :] = tile.astype(BF16)
    copies = start_copies([joined], [joined_out], copied)
    load_second(joined, second)
    row = iota((ROWS4, ROWS4), 0)
    col = iota((ROWS4, ROWS4), 1)
    flip = jnp.where((row // PW == col // PW) & (row % PW + col % PW == PW - 1), 1.0, 0.0).astype(
        BF16
    )
    lane = iota((ROWS4, LANES), 1)
    narrow = iota((PW, LANES), 1)

    def body(i):
        own = joined[rows_at(i * ROWS4, ROWS4, ROWS4), :]
        first = jnp.where(lane < FC, own.astype(F32), 0.0).astype(BF16)
        first = jnp.dot(flip, first, preferred_element_type=F32).astype(BF16)
        bands = []
        for g in range(4):
            window = second[rows_at((4 * i + 3 * g) * PITCH, LANES), :].astype(BF16)
            bands.append(lax.dot_general(first, window, NT, preferred_element_type=F32))
        pieces = []
        for yy in range(4):
            total = jnp.zeros((PW, LANES), F32)
            turned = [
                pltpu.roll(band[yy * PW : (yy + 1) * PW, :], 0, 1, stride=1, stride_axis=0)
                for band in bands
            ]
            for dy in range(EXT):
                t = yy + dy
                shift = (band_shift(dy, t % 3) - (PW - 1)) % LANES
                band = pltpu.roll(turned[t // 3], shift, 1)
                total = jnp.where((narrow >= EXT * dy) & (narrow < EXT * (dy + 1)), band, total)
            pieces.append(total * (1.0 / FC))
        total = jnp.concatenate(pieces, axis=0)
        high = total.astype(BF16)
        low = (total - high.astype(F32)).astype(BF16)
        total = jnp.dot(flip, high, preferred_element_type=F32) + jnp.dot(
            flip, low, preferred_element_type=F32
        )
        cost[rows_at(i * ROWS4, ROWS4, ROWS4), :] = total
        wide = own.astype(F32)
        filled = jnp.where(lane < NCOST, leaky(total), pltpu.roll(wide, NCOST, 1))
        coarse = pltpu.roll(wide, NCOST + FC - 2 * FC, 1)
        filled = jnp.where(lane >= NCOST + FC, coarse, filled)
        filled = jnp.where(lane < NS0, filled, 0.0)
        stack0[rows_at(i * ROWS4, ROWS4, ROWS4), :] = filled.astype(BF16)

    for i in range(PH // 4):
        body(i)
    copies.append(pltpu.make_async_copy(cost, cost_out, copied.at[1]))
    copies[1].start()
    for copy in copies:
        copy.wait()


def correlate(received):
    vmem = pl.BlockSpec(memory_space=pltpu.VMEM)
    anywhere = pl.BlockSpec(memory_space=pltpu.HBM)
    return pl.pallas_call(
        correlate_kernel,
        out_shape=[
            jax.ShapeDtypeStruct((PX, LANES), BF16),
            jax.ShapeDtypeStruct((PX, LANES), F32),
            jax.ShapeDtypeStruct((PX, LANES), BF16),
        ],
        out_specs=[vmem, anywhere, anywhere],
        scratch_shapes=[
            pltpu.VMEM((SEC_ROWS, LANES), F32),
            pltpu.VMEM((PX, LANES), F32),
            pltpu.VMEM((PX, LANES), BF16),
            pltpu.SemaphoreType.DMA((2,)),
        ],
        compiler_params=pltpu.CompilerParams(vmem_limit_bytes=60 * 2**20),
        cost_estimate=pl.CostEstimate(
            flops=8_000_000_000, bytes_accessed=2_000_000, transcendentals=0
        ),
        name="correlate",
    )(received)


class Work:
    def __init__(self, taps, moved, partial):
        self.taps = taps
        self.moved = moved
        self.partial = partial
        self.column = iota((STRIP, LANES), 0) % PW
        self.lane = iota((STRIP, LANES), 1)
        if taps is not None:
            taps[:, :RIM, :] = jnp.zeros((3, RIM, LANES), F32)
            taps[:, RIM + PX :, :] = jnp.zeros((3, RIM, LANES), F32)
        if moved is not None:
            moved[:, :RIM, :] = jnp.zeros((3, RIM, LANES), BF16)
            moved[:, RIM + PX :, :] = jnp.zeros((3, RIM, LANES), BF16)

    def strips(self, body):
        for at in range(0, PX, STRIP):
            body(pl.ds(at, STRIP), at)

    def inside(self, tile, shift):
        if shift == 0:
            return tile
        valid = (self.column + shift >= 0) & (self.column + shift < PW)
        return jnp.where(valid, pltpu.roll(tile, (-shift) % STRIP, 0), 0.0)

    def spread(self, store, tile, dilation):
        for kx in range(3):
            store(kx, self.inside(tile, (kx - 1) * dilation).astype(BF16))

    def multiply(self, load, kernel):
        def body(i):
            rows = rows_at(i * MT, MT, MT)
            value = jnp.concatenate([load(kx, rows) for kx in range(3)], axis=1)
            product = lax.dot_general(value, kernel[...], NT, preferred_element_type=F32)
            for ky in range(3):
                self.taps[ky, rows_at(RIM + i * MT, MT, MT), :] = product[
                    :, ky * LANES : (ky + 1) * LANES
                ]

        for i in range(PX // MT):
            body(i)

    def collect(self, at, dilation):
        total = None
        for ky in range(3):
            tile = self.taps[ky, rows_at(RIM + at + (ky - 1) * dilation * PW, STRIP, PW), :]
            total = tile if total is None else total + tile
        return total

    def spread_grad(self, at, grad, dilation):
        for kx in range(3):
            self.moved[kx, rows_at(RIM + at, STRIP, STRIP), :] = self.inside(
                grad, -(kx - 1) * dilation
            ).astype(BF16)

    def count_bias(self, index, grad):
        self.partial[index] += grad.reshape(STRIP // 8, 8, LANES).sum(0)

    def back(self, index, load_grad, load_pre, load_input, kernel, out, store, waits=()):
        layer = LAYERS[index]
        dilation = layer["dil"]
        width = layer["blocks"] * LANES

        def through(rows, at):
            grad = load_grad(rows) * leaky_slope(load_pre(rows))
            grad = grad.astype(BF16).astype(F32)
            self.count_bias(index, grad)
            self.spread_grad(at, grad, dilation)

        self.strips(through)
        for load in waits:
            load.wait()
        grad = jnp.concatenate(
            [
                self.moved[1, RIM - (ky - 1) * dilation * PW : RIM - (ky - 1) * dilation * PW + PX, :]
                for ky in range(3)
            ],
            axis=1,
        )
        for kx in range(3):
            out[:, kx * width : (kx + 1) * width] = lax.dot_general(
                grad, load_input(kx), TN, preferred_element_type=F32
            ).astype(BF16)

        def input_grad(i):
            tiles = [
                self.moved[kx, rows_at(RIM + i * MT - (ky - 1) * dilation * PW, MT, PW), :]
                for ky in range(3)
                for kx in range(3)
            ]
            weights = [
                kernel[ky * LANES : (ky + 1) * LANES, kx * width : (kx + 1) * width]
                for ky in range(3)
                for kx in range(3)
            ]
            store(
                rows_at(i * MT, MT, MT),
                jnp.dot(
                    jnp.concatenate(tiles, axis=1),
                    jnp.concatenate(weights, axis=0),
                    preferred_element_type=F32,
                ),
            )

        for i in range(PX // MT):
            input_grad(i)


def forward_kernel(half, place_at, stack0, *refs):
    own, other, refs = refs[:half], refs[half : 2 * half], refs[2 * half :]
    kernels_out, carry_out, (stack_out, top_out, pre_out) = refs[:4], refs[4], refs[5:8]
    kernels, refs = refs[8:12], refs[12:]
    stack, top, pre, biases, order, taps, copied = refs[:7]
    fill_order(order)
    unpack_weights(
        EARLY, 0, place_at, (own, other), None, kernels, biases, carry_out, order, refs[7:]
    )
    copies = start_copies(kernels, kernels_out, copied)
    work = Work(taps, None, None)

    def send(source, target):
        copies.append(pltpu.make_async_copy(source, target, copied.at[len(copies)]))
        copies[-1].start()

    def first(rows, at):
        tile = stack0[rows, :].astype(F32)

        def keep(kx, value):
            stack[kx, rows, :LANES] = value

        work.spread(keep, tile, 1)

    work.strips(first)
    send(stack.at[:, :, :LANES], stack_out.at[:, :, :LANES])
    for index, kernel in enumerate(kernels):
        width = LAYERS[index]["blocks"] * LANES
        work.multiply(lambda kx, rows, width=width: stack[kx, rows, :width], kernel)

        place = slice((index + 1) * LANES, (index + 2) * LANES)

        def finish(rows, at, index=index, place=place):
            value = work.collect(at, 1) + biases[index : index + 1, :]
            pre[index, rows, :] = value

            def keep(kx, value):
                if index == 3:
                    top[kx, rows, :] = value
                else:
                    stack[kx, rows, place] = value

            work.spread(keep, leaky(value), 1)

        work.strips(finish)
        send(pre.at[index], pre_out.at[index])
        if index == 3:
            send(top, top_out)
        else:
            send(stack.at[:, :, place], stack_out.at[:, :, place])
    for copy in copies:
        copy.wait()


def forward(place_at, parts, stack0, count):
    vmem = pl.BlockSpec(memory_space=pltpu.VMEM)
    anywhere = pl.BlockSpec(memory_space=pltpu.HBM)
    kernels = [(LAYERS[i]["shape"], BF16) for i in EARLY]
    states = [((3, PX, 4 * LANES), BF16), ((3, PX, LANES), BF16), ((4, PX, LANES), F32)]
    outs = pl.pallas_call(
        functools.partial(forward_kernel, len(parts[0])),
        out_shape=[
            jax.ShapeDtypeStruct(*a) for a in (*kernels, ((count - CUT, LANES), BF16), *states)
        ],
        in_specs=[pl.BlockSpec(memory_space=pltpu.SMEM)] + [vmem] * (1 + 2 * len(parts[0])),
        out_specs=[anywhere] * 4 + [vmem] + [anywhere] * 3,
        scratch_shapes=[
            *[pltpu.VMEM(*a) for a in (*kernels, *states)],
            pltpu.VMEM((16, LANES), F32),
            ORDER,
            pltpu.VMEM((3, PX + 2 * RIM, LANES), F32),
            pltpu.SemaphoreType.DMA((13,)),
            *unpack_scratch(EARLY, count),
        ],
        compiler_params=pltpu.CompilerParams(vmem_limit_bytes=60 * 2**20),
        cost_estimate=pl.CostEstimate(
            flops=25_000_000_000, bytes_accessed=20_000_000, transcendentals=0
        ),
        name="dense_forward",
    )(place_at, stack0, *parts[0], *parts[1])
    return outs[:4], *outs[4:]


def late_kernel(
    rows,
    half,
    groups,
    pixels,
    gather_at,
    pack_at,
    carried,
    stack_in,
    below_in,
    joined_in,
    *refs,
):
    counts, refs = refs[:groups], refs[groups:]
    own, other, refs = refs[:half], refs[half : 2 * half], refs[2 * half :]
    motion_out, dstack_out, bias_out, keep, send, carry_out = refs[:6]
    order, biases, dstack, stack, below, joined, copied = refs[6:13]
    refs = refs[13:]
    kernels = refs[:9]
    grads = refs[9:]
    loads = [
        pltpu.make_async_copy(source, target, copied.at[i])
        for i, (source, target) in enumerate(zip((stack_in, below_in, joined_in), (stack, below, joined)))
    ]
    for load in loads:
        load.start()
    fill_order(order)

    def first(*scratch):
        unpack_weights(
            LATE, CUT, gather_at, (own, other), carried, kernels, biases, None, order, scratch
        )

    pl.run_scoped(first, *unpack_scratch(LATE, rows))
    for load in loads:
        load.wait()

    weighting = pixels / sum(count[:1, :] for count in counts)

    def second(*scratch):
        context(
            stack, below, joined, weighting, biases, kernels, motion_out, dstack, bias_out, grads, *scratch
        )

    pl.run_scoped(second, *CONTEXT_SCRATCH)
    store = pltpu.make_async_copy(dstack, dstack_out, copied.at[3])
    store.start()

    def third(*scratch):
        pack_gradients(
            LATE, CUT, pack_at, grads, bias_out, None, (keep, send), carry_out, order, scratch
        )

    pl.run_scoped(third, *pack_scratch(LATE, rows))
    store.wait()


def context(
    stack, below, joined, weighting, biases, kernels, motion_out, dstack, bias_out, grads, *scratch
):
    kernels = dict(zip(LATE, kernels))
    grads = dict(zip(LATE, grads))
    top, ctx, pre, taps, moved, dcur, ghead, partial = scratch
    work = Work(taps, moved, partial)
    partial[...] = jnp.zeros_like(partial)
    lane = work.lane

    def wide(kx, rows):
        return jnp.concatenate([stack[kx, rows, :], top[kx, rows, :]], axis=1)

    work.multiply(
        lambda kx, rows: jnp.concatenate([stack[kx, rows, :], below[kx, rows, :]], axis=1),
        kernels[4],
    )

    def finish_top(rows, at):
        value = work.collect(at, 1) + biases[4:5, :]
        pre[0, rows, :] = value

        def keep(kx, value):
            top[kx, rows, :] = value + below[kx, rows, :]

        work.spread(keep, leaky(value), 1)

    work.strips(finish_top)
    for index in range(6, 12):
        if index == 6:
            work.multiply(wide, kernels[index])
        else:
            work.multiply(lambda kx, rows, index=index: ctx[index - 7, kx, rows, :], kernels[index])

        def finish(rows, at, index=index):
            value = work.collect(at, LAYERS[index]["dil"]) + biases[index : index + 1, :]
            pre[index - 5, rows, :] = value

            def keep(kx, value):
                ctx[index - 6, kx, rows, :] = value

            work.spread(keep, leaky(value), LAYERS[index + 1]["dil"])

        work.strips(finish)

    def head(i):
        rows = rows_at(i * MT, MT, MT)
        product = lax.dot_general(wide(1, rows), kernels[5][...], NT, preferred_element_type=F32)
        product = product + lax.dot_general(
            ctx[5, 1, rows, :], kernels[12][...], NT, preferred_element_type=F32
        )
        taps[0, rows_at(RIM + i * MT, MT, MT), :] = product

    for i in range(PX // MT):
        head(i)

    row = iota((LANES, LANES), 0)
    col = iota((LANES, LANES), 1)
    used = (col < 18) & (row % 2 == col % 2)
    fold = jnp.where(used & (row < 18), 1.0, 0.0)
    copies = jnp.where(used & (row < 2), 1.0, 0.0).astype(BF16)
    pick = jnp.where(used & (row >= 2 * FC + 4) & (row < 2 * FC + 6), 1.0, 0.0).astype(BF16)
    marked = jnp.where(row == 2 * FC + 6, 1.0, 0.0).astype(BF16)
    shared = sum(
        jnp.dot(jnp.broadcast_to(b, (8, LANES)).astype(BF16), copies, preferred_element_type=F32)
        for b in (biases[5:6, :], biases[12:13, :])
    )[:1]

    def settle(rows, at):
        total = None
        for kx in range(3):
            part = None
            for ky in range(3):
                tile = taps[0, rows_at(RIM + at + (ky - 1) * PW, STRIP, PW), :]
                tile = jnp.where(lane // 2 == ky * 3 + kx, tile, 0.0)
                part = tile if part is None else part + tile
            part = work.inside(part, kx - 1)
            total = part if total is None else total + part
        motion = (
            jnp.dot(total, fold, preferred_element_type=F32, precision=lax.Precision.HIGHEST)
            + shared
        )
        motion_out[:, rows] = motion.T[: motion_out.shape[0]]
        own = joined[rows, :]
        aim = jnp.dot(own, pick, preferred_element_type=F32)
        mask = jnp.dot(own, marked, preferred_element_type=F32)
        mismatch = motion - aim
        square = mismatch * mismatch
        other = jnp.where(
            lane % 2 == 0, pltpu.roll(square, LANES - 1, 1), pltpu.roll(square, 1, 1)
        )
        length = jnp.sqrt(square + other + EPE_EPS)
        height = (iota((STRIP, LANES), 0) + at) // PW
        interior = (
            (height >= MARGIN)
            & (height < PH - MARGIN)
            & (work.column >= MARGIN)
            & (work.column < PW - MARGIN)
            & (lane < 18)
        )
        grad = jnp.where(interior, weighting * mask * mismatch / length, 0.0)
        grad = grad.astype(BF16).astype(F32)
        work.count_bias(5, grad)
        work.spread_grad(at, grad, 1)

    work.strips(settle)
    partial[12] = partial[5]

    def choose(rows, at):
        total = None
        for kx in range(3):
            for ky in range(3):
                tile = moved[kx, rows_at(RIM + at - (ky - 1) * PW, STRIP, PW), :].astype(F32)
                tile = jnp.where(lane // 2 == ky * 3 + kx, tile, 0.0)
                total = tile if total is None else total + tile
        ghead[rows, :] = total.astype(BF16)

    work.strips(choose)
    grads[5][:, : 4 * LANES] = lax.dot_general(
        ghead[...], stack[1], TN, preferred_element_type=F32
    ).astype(BF16)
    grads[5][:, 4 * LANES :] = lax.dot_general(
        ghead[...], top[1], TN, preferred_element_type=F32
    ).astype(BF16)
    grads[12][...] = lax.dot_general(
        ghead[...], ctx[5, 1], TN, preferred_element_type=F32
    ).astype(BF16)

    def head_back(i):
        rows = rows_at(i * MT, MT, MT)
        dstack[rows, :] = jnp.dot(ghead[rows, :], kernels[5][...], preferred_element_type=F32)
        dcur[rows, :] = jnp.dot(ghead[rows, :], kernels[12][...], preferred_element_type=F32)

    for i in range(PX // MT):
        head_back(i)

    def store_current(rows, value):
        dcur[rows, :] = value

    def store_stack(rows, value):
        dstack[rows, :] += value

    for index in range(11, 6, -1):
        work.back(
            index,
            lambda rows: dcur[rows, :],
            lambda rows, index=index: pre[index - 5, rows, :],
            lambda kx, index=index: ctx[index - 7, kx],
            kernels[index],
            grads[index],
            store_current,
        )
    work.back(
        6,
        lambda rows: dcur[rows, :],
        lambda rows: pre[1, rows, :],
        lambda kx: jnp.concatenate([stack[kx], top[kx]], axis=1),
        kernels[6],
        grads[6],
        store_stack,
    )
    work.back(
        4,
        lambda rows: dstack[rows, 4 * LANES :],
        lambda rows: pre[0, rows, :],
        lambda kx: jnp.concatenate([stack[kx], top[kx]], axis=1),
        kernels[4],
        grads[4],
        store_stack,
    )
    bias_out[...] = partial[...].sum(1)


CONTEXT_SCRATCH = (
    pltpu.VMEM((3, PX, LANES), BF16),
    pltpu.VMEM((6, 3, PX, LANES), BF16),
    pltpu.VMEM((7, PX, LANES), F32),
    pltpu.VMEM((3, PX + 2 * RIM, LANES), F32),
    pltpu.VMEM((3, PX + 2 * RIM, LANES), BF16),
    pltpu.VMEM((PX, LANES), F32),
    pltpu.VMEM((PX, LANES), BF16),
    pltpu.VMEM((16, 8, LANES), F32),
)


def late(gather_at, pack_at, parts, carried, stack, below, joined, counts, pixels, end, pieces, size):
    smem = pl.BlockSpec(memory_space=pltpu.SMEM)
    vmem = pl.BlockSpec(memory_space=pltpu.VMEM)
    anywhere = pl.BlockSpec(memory_space=pltpu.HBM)
    shapes = [pltpu.VMEM(LAYERS[i]["shape"], BF16) for i in LATE]
    return pl.pallas_call(
        functools.partial(late_kernel, end - CUT, len(parts[0]), len(counts), float(pixels)),
        out_shape=[
            jax.ShapeDtypeStruct((8, PX), F32),
            jax.ShapeDtypeStruct((PX, 5 * LANES), F32),
            jax.ShapeDtypeStruct((16, LANES), F32),
            jax.ShapeDtypeStruct((pieces, size, LANES), BF16),
            jax.ShapeDtypeStruct((pieces, size, LANES), BF16),
            jax.ShapeDtypeStruct((end // 2 - CUT, LANES), BF16),
        ],
        in_specs=[smem] * 2 + [vmem] + [anywhere] * 3 + [vmem] * (len(counts) + 2 * len(parts[0])),
        out_specs=[vmem, anywhere, vmem, vmem, vmem, vmem],
        scratch_shapes=[
            ORDER,
            pltpu.VMEM((16, LANES), F32),
            pltpu.VMEM((PX, 5 * LANES), F32),
            pltpu.VMEM(stack.shape, BF16),
            pltpu.VMEM(below.shape, BF16),
            pltpu.VMEM(joined.shape, BF16),
            pltpu.SemaphoreType.DMA((4,)),
            *shapes,
            *shapes,
        ],
        compiler_params=pltpu.CompilerParams(vmem_limit_bytes=60 * 2**20),
        cost_estimate=pl.CostEstimate(
            flops=80_000_000_000, bytes_accessed=20_000_000, transcendentals=0
        ),
        name="context",
    )(gather_at, pack_at, carried, stack, below, joined, *counts, *parts[0], *parts[1])


def correlate_back(joined, cost, grads, second, dsecond, collected, out):
    load_second(joined, second)
    dsecond[...] = jnp.zeros_like(dsecond)
    lane = iota((ROWS4, LANES), 1)
    narrow = iota((PW, LANES), 1)

    def body(i):
        rows = rows_at(i * ROWS4, ROWS4, ROWS4)
        own = joined[rows, :]
        first = jnp.where(lane < FC, own.astype(F32), 0.0).astype(BF16)
        grad = grads[rows, :LANES]
        volume = grad * leaky_slope(cost[rows, :]) * (1.0 / FC)
        dfirst = jnp.zeros((ROWS4, LANES), F32)
        for g in range(4):
            pieces = []
            for yy in range(4):
                piece = jnp.zeros((PW, LANES), F32)
                own_rows = volume[yy * PW : (yy + 1) * PW, :]
                for t in range(3 * g, 3 * g + 3):
                    dy = t - yy
                    if dy < 0 or dy >= EXT:
                        continue
                    part = jnp.where(
                        (narrow >= EXT * dy) & (narrow < EXT * (dy + 1)), own_rows, 0.0
                    )
                    shift = (-band_shift(dy, t % 3)) % LANES
                    piece = piece + pltpu.roll(part, shift, 1)
                pieces.append(pltpu.roll(piece, 0, 1, stride=1, stride_axis=0))
            band = jnp.concatenate(pieces, axis=0).astype(BF16)
            at = rows_at((4 * i + 3 * g) * PITCH, LANES)
            dfirst = dfirst + jnp.dot(
                band, second[at, :].astype(BF16), preferred_element_type=F32
            )
            dsecond[at, :] += lax.dot_general(band, first, TN, preferred_element_type=F32)
        direct = pltpu.roll(grad, LANES - NCOST, 1)
        coarse = pltpu.roll(grad, LANES + 2 * FC - NCOST - FC, 1)
        filled = jnp.where(lane < FC, dfirst + direct, 0.0)
        filled = jnp.where((lane >= 2 * FC) & (lane < 2 * FC + 4), coarse, filled)
        collected[rows, :] = filled

    for i in range(PH // 4):
        body(i)
    for s in range((PH - 2 * MARGIN) // 4):
        pieces = []
        for yy in range(4):
            at = (MARGIN + 4 * s + yy + SR) * PITCH + 8
            pieces.append(dsecond[at : at + PW, :])
        other = pltpu.roll(jnp.concatenate(pieces, axis=0), FC, 1)
        start = (MARGIN + 4 * s) * PW
        tile = collected[start : start + ROWS4, :]
        tile = jnp.where((lane >= FC) & (lane < 2 * FC), other, tile)
        out[s] = tile.T[: out.shape[1]].astype(BF16)


def early_kernel(
    pack_at,
    stack_in,
    pre_in,
    dstack_in,
    cost_in,
    joined_in,
    bias_in,
    carried,
    k1,
    k2,
    k3,
    k4,
    picture_out,
    keep,
    send,
    order,
    stack,
    pre,
    dstack,
    cost,
    joined,
    bias_out,
    copied,
    *grads,
):
    sources = (dstack_in, pre_in, stack_in, cost_in, joined_in)
    targets = (dstack, pre, stack, cost, joined)
    loads = [
        pltpu.make_async_copy(source, target, copied.at[i])
        for i, (source, target) in enumerate(zip(sources, targets))
    ]
    for load in loads:
        load.start()
    fill_order(order)
    for load in loads[:2]:
        load.wait()

    def first(*scratch):
        dense_back(
            stack,
            pre,
            dstack,
            cost,
            joined,
            bias_in,
            (k1, k2, k3, k4),
            picture_out,
            bias_out,
            grads,
            loads[2:],
            *scratch,
        )

    pl.run_scoped(first, *DENSE_SCRATCH)

    def second(*scratch):
        pack_gradients(
            EARLY, 0, pack_at, grads, bias_out, carried, (keep, send), None, order, scratch
        )

    pl.run_scoped(second, *pack_scratch(EARLY, CUT + carried.shape[0]))


def dense_back(
    stack,
    pre,
    dstack,
    cost,
    joined,
    bias_in,
    kernels,
    picture_out,
    bias_out,
    grads,
    loads,
    moved,
    dwide,
    partial,
    second,
    dsecond,
    collected,
):
    work = Work(None, moved, partial)
    partial[...] = jnp.zeros_like(partial)
    dwide[...] = dstack[:, : 4 * LANES]

    def store_stack(rows, value):
        dwide[rows, : value.shape[1]] += value

    for index in range(3, -1, -1):
        width = LAYERS[index]["blocks"] * LANES

        def load_grad(rows, index=index):
            if index == 3:
                return dstack[rows, 4 * LANES :]
            return dwide[rows, (index + 1) * LANES : (index + 2) * LANES]

        work.back(
            index,
            load_grad,
            lambda rows, index=index: pre[index, rows, :],
            lambda kx, width=width: stack[kx, :, :width],
            kernels[index],
            grads[index],
            store_stack,
            loads if index == 3 else (),
        )
    bias_out[...] = partial[...].sum(1) + bias_in[...]
    correlate_back(joined, cost, dwide, second, dsecond, collected, picture_out)


DENSE_SCRATCH = (
    pltpu.VMEM((3, PX + 2 * RIM, LANES), BF16),
    pltpu.VMEM((PX, 4 * LANES), F32),
    pltpu.VMEM((16, 8, LANES), F32),
    pltpu.VMEM((SEC_ROWS, LANES), F32),
    pltpu.VMEM((SEC_ROWS, LANES), F32),
    pltpu.VMEM((PX, LANES), F32),
)


def backward(
    pack_at, stack, pre, dstack, cost, joined, bias_grads, carried, kernels, blocks, channels, pieces, size
):
    vmem = pl.BlockSpec(memory_space=pltpu.VMEM)
    large = (stack, pre, dstack, cost, joined)
    return pl.pallas_call(
        early_kernel,
        out_shape=[
            jax.ShapeDtypeStruct((blocks, channels, LANES), BF16),
            jax.ShapeDtypeStruct((pieces, size, LANES), BF16),
            jax.ShapeDtypeStruct((pieces, size, LANES), BF16),
        ],
        in_specs=[pl.BlockSpec(memory_space=pltpu.SMEM)]
        + [pl.BlockSpec(memory_space=pltpu.HBM)] * 5
        + [vmem] * 6,
        scratch_shapes=[
            ORDER,
            *[pltpu.VMEM(a.shape, a.dtype) for a in large],
            pltpu.VMEM((16, LANES), F32),
            pltpu.SemaphoreType.DMA((5,)),
            *[pltpu.VMEM(LAYERS[i]["shape"], BF16) for i in EARLY],
        ],
        compiler_params=pltpu.CompilerParams(vmem_limit_bytes=60 * 2**20),
        cost_estimate=pl.CostEstimate(
            flops=40_000_000_000, bytes_accessed=20_000_000, transcendentals=0
        ),
        name="dense_backward",
    )(pack_at, *large, bias_grads, carried, *kernels)


def update(weights, momentum, average, gradient):
    gradient = gradient + DECAY_RATE * weights
    renewed = MOMENTUM_RATE * momentum + gradient
    stepped = weights - LEARN_RATE * (gradient + MOMENTUM_RATE * renewed)
    return (stepped, renewed, AVERAGE_DECAY * average + (1.0 - AVERAGE_DECAY) * stepped)


def swapped(value, axis, step):
    count = lax.axis_size(axis)
    return lax.ppermute(value, axis, [(i, i ^ step) for i in range(count)])


def added(one, two):
    return (one.astype(F32) + two.astype(F32)).astype(BF16)


def core_sum(keep, send, groups, devices):
    got = swapped(send, "grp", 1)
    pieces = keep.shape[0] // 2
    if groups == 2:
        return [added(keep, got)]
    return [added(keep[pieces:], got[pieces:]), added(keep[:pieces], got[:pieces])]


def x_sum(value, groups, devices):
    half = devices // 2
    step = groups // 4
    if not step:
        value = value[0]
        return [value[j] for j in range(half)]
    away, value = value
    got = swapped(away, "grp", 2 * step)
    while step > 1:
        value = added(value, got)
        step //= 2
        pieces = value.shape[0] // 2
        got = swapped(value[pieces:], "grp", 2 * step)
        value = value[:pieces]
    return [added(value[j], got[j]) for j in range(half)]


def dev_sum(pieces):
    total = pieces[0].astype(F32)
    for j in range(1, len(pieces)):
        total = total + swapped(pieces[j], "dev", j).astype(F32)
    return total


def shared_parts(value, groups):
    x_size = groups // 2
    x = lax.axis_index("grp") // 2
    held = [0]
    parts = [value]
    step = 1
    while step < x_size:
        parts = parts + [swapped(p, "grp", 2 * step) for p in parts]
        held = held + [j ^ step for j in held]
        step *= 2

    def ordered(parts):
        out = []
        for i in range(x_size):
            piece = parts[0]
            for j, part in zip(held[1:], parts[1:]):
                piece = jnp.where((x ^ j) == i, part, piece)
            out.append(piece)
        return jnp.concatenate(out)

    return ordered(parts), ordered([swapped(p, "grp", 1) for p in parts])


def shards(features, coarse_flow, target, valid_mask, weights, momentum, average):
    groups = lax.axis_size("grp")
    devices = lax.axis_size("dev")
    own_rows = features.shape[2]
    width = features.shape[3]
    breadth = width // devices
    height = own_rows * devices
    assert breadth + 2 * MARGIN == PW and height + 2 * MARGIN == PH
    core = lax.axis_index("grp") % 2
    me = lax.axis_index("dev")
    half = devices // 2
    early = me < half
    rows = weights.shape[0] // LANES
    x_size = groups // 2
    size = -(-(rows // 2) // (16 * x_size)) * 16 * x_size
    table = weights.reshape(rows, LANES)
    own = lax.dynamic_slice(table, (core * (rows - size), 0), (size, LANES)).astype(BF16)

    received = windows(features, coarse_flow, target, valid_mask, devices)
    received = lax.all_to_all(received, "dev", split_axis=0, concat_axis=0, tiled=True)

    across = swapped(own, "dev", half)
    both = jnp.stack([core, 1 - core])[:, None] * (rows - size)
    steps = [half >> i for i in range(1, half.bit_length())]
    held = [0]
    for step in steps:
        held = held + [j ^ step for j in held]
    place = (jnp.array(held, jnp.int32) ^ (me % half))[None] * rows + both
    x = lax.axis_index("grp") // 2
    part_x = (jnp.arange(x_size, dtype=jnp.int32) ^ x) * (size // x_size)
    part_dev = (jnp.arange(half, dtype=jnp.int32) ^ (me % half)) * rows
    pack_at = (part_x[:, None] + part_dev[None]).reshape(1, -1) + both
    places = (place, place + half * rows, pack_at, pack_at + half * rows)
    across, received, *places = lax.optimization_barrier((across, received, *places))
    part, last = {0: jnp.where(early, own, across)}, {0: jnp.where(early, across, own)}
    other, other_last = {}, {}

    def grow(pieces, step):
        for j in list(pieces):
            if j ^ step not in pieces:
                pieces[j ^ step] = swapped(pieces[j], "dev", step)

    def swap_cores(pieces, others):
        for j in pieces:
            if j not in others:
                others[j] = swapped(pieces[j], "grp", 1)

    first_y = swapped(part[0], "dev", 1)
    swap_cores(part, other)
    for step in steps[:-1]:
        grow(part, step)
    counted = jnp.full((8, LANES), jnp.sum(received[:, CHANNELS - 1].astype(F32)))
    counts = [counted] + [swapped(counted, "grp", j) for j in range(1, groups)]
    keys = list(part)
    *tied, received, last[0] = lax.optimization_barrier(
        (*counts, *part.values(), received, last[0])
    )
    counts, part = tied[:groups], dict(zip(keys, tied[groups:]))
    swap_cores(part, other)
    swap_cores(last, other_last)
    part[1] = first_y
    grow(part, 1)
    for step in steps[:-1]:
        grow(last, step)
    per = 4 // own_rows
    blocks = devices // per
    received = received.reshape(blocks, per, CHANNELS, own_rows * PW)
    received = jnp.swapaxes(received, 1, 2).reshape(blocks, CHANNELS, LANES)
    stack0, cost, joined = correlate(received)
    keys, keys_last = list(part), list(last)
    *tied, stack0 = lax.optimization_barrier((*part.values(), *last.values(), stack0))
    part = dict(zip(keys, tied))
    last = dict(zip(keys_last, tied[len(keys) :]))
    swap_cores(part, other)
    grow(last, 1)
    parts = ([part[j] for j in held], [other[j] for j in held])
    kernels, carried, stack, below, pre = forward(places[0], parts, stack0, half * rows)
    keys_last = list(last)
    *tied, stack = lax.optimization_barrier((*last.values(), stack))
    last = dict(zip(keys_last, tied))
    swap_cores(last, other_last)
    parts = ([last[j] for j in held], [other_last[j] for j in held])
    pack_at, pack_late_at = places[2:]
    pieces = (half * x_size, size // x_size)
    motion, dstack, bias_grads, keep, send, carried = late(
        places[1],
        pack_late_at,
        parts,
        carried,
        stack,
        below,
        joined,
        counts,
        groups * height * width,
        devices * rows,
        *pieces,
    )
    flow = motion[:2].reshape(1, 2, PH, PW)[
        :, :, MARGIN : MARGIN + height, MARGIN : MARGIN + breadth
    ]
    late_sum = core_sum(keep, send, groups, devices)
    late_sum, dstack = lax.optimization_barrier((late_sum, dstack))
    late_sum = x_sum(late_sum, groups, devices)
    tiles, keep, send = backward(
        pack_at,
        stack,
        pre,
        dstack,
        cost,
        joined,
        bias_grads,
        carried,
        kernels,
        blocks,
        CHANNELS,
        *pieces,
    )
    late_sum, keep, send = lax.optimization_barrier((late_sum, keep, send))
    late_sum = dev_sum(late_sum)
    early_sum = core_sum(keep, send, groups, devices)
    tiles = tiles.reshape(blocks, CHANNELS, per, own_rows * PW)
    tiles = jnp.swapaxes(tiles, 1, 2).reshape(devices, CHANNELS, own_rows * PW)
    returned = lax.all_to_all(tiles, "dev", split_axis=0, concat_axis=0, tiled=True)
    early_sum = x_sum(early_sum, groups, devices)
    early_sum, late_sum, returned = lax.optimization_barrier((early_sum, late_sum, returned))
    early_sum = dev_sum(early_sum)
    total = jnp.where(early, early_sum, late_sum)
    passed = jnp.where(early, late_sum, early_sum).astype(BF16)
    total = (total + swapped(passed, "dev", half).astype(F32)).astype(BF16)
    total, rest = shared_parts(total, groups)
    low = jnp.where(core == 0, total, rest)
    high = jnp.where(core == 0, rest, total)
    total_grad = jnp.concatenate([low[: rows - size], high]).astype(F32).reshape(-1)

    returned = returned.reshape(devices, CHANNELS, own_rows, PW).astype(F32)
    wide = jnp.transpose(returned, (1, 2, 0, 3))
    centre = wide[..., MARGIN : MARGIN + breadth]
    left = wide[:, :, 1:, :MARGIN]
    right = wide[:, :, :-1, MARGIN + breadth :]
    none = ((0, 0), (0, 0))
    centre = centre + jnp.pad(left, (*none, (0, 1), (breadth - MARGIN, 0)))
    centre = centre + jnp.pad(right, (*none, (1, 0), (0, breadth - MARGIN)))
    row_grad = centre.reshape(1, CHANNELS, own_rows, width)
    feature_grad = row_grad[:, : 2 * FC]
    coarse_grad = row_grad[:, 2 * FC : 2 * FC + 4]

    new_weights, new_momentum, new_average = update(weights, momentum, average, total_grad)
    return (
        flow,
        feature_grad,
        coarse_grad,
        new_weights,
        new_momentum,
        new_average,
        new_weights.astype(BF16),
    )


def solution(mesh):
    in_specs = (
        P("grp", None, "dev", None),
        P("grp", None, "dev", None),
        P("grp", None, "dev", None),
        P("grp", "dev", None),
        P("dev"),
        P("dev"),
        P("dev"),
    )
    out_specs = (
        P("grp", None, None, "dev"),
        P("grp", None, "dev", None),
        P("grp", None, "dev", None),
        P("dev"),
        P("dev"),
        P("dev"),
        P("dev"),
    )
    return jax.shard_map(shards, mesh=mesh, in_specs=in_specs, out_specs=out_specs, check_vma=False)
```

```python
import functools

import jax
import jax.numpy as jnp
from jax import lax
from jax.experimental import pallas as pl
from jax.experimental.pallas import tpu as pltpu
from jax.sharding import PartitionSpec as P

FC = 32
SR = 4
EXT = 2 * SR + 1
NCOST = EXT * EXT
NS0 = NCOST + FC + 4
DENSE = (128, 128, 96, 64, 32)
CONTEXT = (128, 128, 128, 96, 64, 32, 2)
DILATIONS = (1, 2, 4, 8, 16, 1, 1)
MARGIN = 8

SLOPE = 0.1
EPE_EPS = 0.01
MOMENTUM_RATE = 0.5
AVERAGE_DECAY = 0.5
LEARN_RATE = 0.001
DECAY_RATE = 0.0001

LANES = 128
CHANNELS = 72
PH = 48
PW = 32
PX = PH * PW
RIM = 16 * PW
STRIP = 128
MT = 768
PITCH = 40
F32 = jnp.float32
BF16 = jnp.bfloat16
NT = (((1,), (1,)), ((), ()))
TN = (((0,), (0,)), ((), ()))


def layer_table():
    places = [(NS0, 0, 0), (128, 1, 0), (128, 2, 0), (96, 3, 0), (64, 4, 0), (32, 4, 64)]
    layers = []
    offset = 0

    def add(pieces, outgoing, dilation, shift):
        nonlocal offset
        incoming = sum(n for n, _, _ in pieces)
        row = 9 * incoming
        segments = []
        at = 0
        for n, block, lane in pieces:
            first, over = 9 * at // LANES, 9 * at % LANES
            slot = -(-(9 * lane - over) // LANES)
            back = 9 * lane - over - LANES * slot
            chunks = -(-(over + 9 * n) // LANES)
            segments.append(
                dict(n=n, block=block, lane=lane, first=first, slot=slot, back=back, chunks=chunks)
            )
            at += n
        blocks = 1 + max(b for _, b, _ in pieces)
        layers.append(
            dict(
                out=outgoing,
                row=row,
                chunks=-(-row // LANES),
                start=offset,
                dil=dilation,
                shift=shift,
                segments=segments,
                blocks=blocks,
                bias=offset + row * outgoing,
                shape=(LANES, blocks * LANES) if outgoing == 2 else (3 * LANES, 3 * blocks * LANES),
            )
        )
        offset += row * outgoing + outgoing

    for i, outgoing in enumerate(DENSE):
        add(places[i::-1], outgoing, 1, 64 if i == 4 else 0)
    add(places[::-1], 2, 1, 0)
    add(places[::-1], CONTEXT[0], DILATIONS[0], 0)
    for i in range(1, 7):
        add([(CONTEXT[i - 1], 0, 0)], CONTEXT[i], DILATIONS[i], 0)
    return layers, offset


LAYERS, COUNT = layer_table()
EARLY = (0, 1, 2, 3)
LATE = (4, 5, 6, 7, 8, 9, 10, 11, 12)
CUT = LAYERS[4]["start"] // LANES // 16 * 16


def sort_groups(indices):
    order = [(segment["back"], i, s) for i in indices for s, segment in enumerate(LAYERS[i]["segments"])]
    order.sort(key=lambda t: -t[0])
    at = 0
    groups = {}
    classes = []
    for back, i, s in order:
        if not classes or classes[-1][0] != back:
            classes.append([back, at, at])
        groups[i, s] = at
        at += -(-LAYERS[i]["out"] // 16) * 16
        classes[-1][2] = at
    return groups, classes, at


def iota(shape, dim):
    return lax.broadcasted_iota(jnp.int32, shape, dim)


def rows_at(start, size, step=8):
    if isinstance(start, int):
        return pl.ds(start, size)
    return pl.ds(pl.multiple_of(start, step), size)


def sigmoid(v):
    return 0.5 * jnp.tanh(0.5 * v) + 0.5


def leaky(v):
    return SLOPE * v + (1.0 - SLOPE) * v * sigmoid(v)


def leaky_slope(v):
    s = sigmoid(v)
    return SLOPE + (1.0 - SLOPE) * (s + v * s * (1.0 - s))


def loop(count, body):
    def step(i, carry):
        body(i)
        return carry

    lax.fori_loop(0, count, step, 0)


def fill_order(order):
    order[:LANES, :] = jnp.zeros((LANES, 9 * LANES), BF16)
    order[10 * LANES :, :] = jnp.zeros((LANES, 9 * LANES), BF16)
    for k in range(9):
        for m in range(9):
            row = iota((LANES, LANES), 0) + m * LANES
            col = iota((LANES, LANES), 1)
            order[(m + 1) * LANES : (m + 2) * LANES, k * LANES : (k + 1) * LANES] = jnp.where(
                row == 9 * col + k, 1.0, 0.0
            ).astype(BF16)


ORDER = pltpu.VMEM((11 * LANES, 9 * LANES), BF16)


def within(n, lane):
    spot = iota((1, LANES), 1)
    return jnp.where((spot >= lane) & (spot < lane + n), 1.0, 0.0).astype(BF16)


def pitch_of(chunks):
    return -(-chunks // 8) * 8


def unpack_scratch(indices, count):
    _, _, group_rows = sort_groups(indices)
    return (
        pltpu.VMEM((count + 64, LANES), F32),
        pltpu.VMEM((48 * LANES, LANES), F32),
        pltpu.VMEM((group_rows, 10 * LANES), BF16),
        pltpu.VMEM((group_rows, 9 * LANES), BF16),
        pltpu.VMEM((LANES, 5 * LANES), F32),
    )


def unpack_weights(indices, base, place_at, parts, carried, outs, bias_out, carry_out, order, scratch):
    whole, slabs, aligned, result, heads = scratch
    count = whole.shape[0] - 64
    groups, classes, _ = sort_groups(indices)
    if base:
        whole[: carried.shape[0], :] = carried[...].astype(F32)
    for at_part, pieces in enumerate(parts):
        for j, piece in enumerate(pieces):
            size = piece.shape[0]
            to = place_at[at_part, j] - base

            def widen(i, piece=piece, to=to):
                whole[pl.ds(to + i * 16, 16), :] = piece[rows_at(i * 16, 16, 16), :].astype(F32)

            lax.fori_loop(0, size // 16, lambda i, c: (widen(i), c)[1], 0, unroll=8)
    whole[count:, :] = jnp.zeros((64, LANES), F32)
    if not base:
        carry_out[...] = whole[CUT:count, :].astype(BF16)
    bias_out[...] = jnp.zeros_like(bias_out)

    for at_out, index in enumerate(indices):
        layer = LAYERS[index]
        outgoing = layer["out"]
        kept = -(-outgoing // 16) * 16
        start = layer["start"] - base * LANES
        spot = iota((kept, LANES), 1)
        pitch = pitch_of(layer["chunks"] + 1)
        still = layer["row"] % LANES == 0
        if not still:
            unroll = min(32, outgoing)

            def take(i, unroll=unroll, row=layer["row"], start=start, pitch=pitch):
                for u in range(unroll):
                    o = i * unroll + u
                    first = start + o * row
                    turn = (LANES - (first & (LANES - 1))) & (LANES - 1)
                    for v in range(pitch // 8):
                        tile = whole[pl.ds((first >> 7) + 8 * v, 8), :]
                        slabs[rows_at(o * pitch + 8 * v, 8), :] = pltpu.roll(tile, turn, 1)

            for i in range(outgoing // unroll):
                take(i)
            off = (start + iota((kept, LANES), 0) * layer["row"]) & (LANES - 1)
        chunks = {}
        for t in range(layer["chunks"]):
            if still:
                row, fixed = divmod(start, LANES)
                step = layer["row"] // LANES
                here = whole[pl.ds(row + t, kept, stride=step), :]
                after = whole[pl.ds(row + t + 1, kept, stride=step), :]
                chunk = jnp.where(spot >= fixed, here, after)
                chunk = pltpu.roll(chunk, (LANES - fixed) % LANES, 1)
            else:
                here = slabs[pl.ds(t, kept, stride=pitch), :]
                after = slabs[pl.ds(t + 1, kept, stride=pitch), :]
                chunk = jnp.where(spot < LANES - off, here, after)
            chunk = chunk.astype(BF16)
            for s, segment in enumerate(layer["segments"]):
                to = t - segment["first"]
                if 0 <= to < segment["chunks"]:
                    to += segment["slot"]
                    at = groups[index, s]
                    aligned[at : at + kept, to * LANES : (to + 1) * LANES] = chunk
        for s, segment in enumerate(layer["segments"]):
            at = groups[index, s]
            for to in range(10):
                if not segment["slot"] <= to < segment["slot"] + segment["chunks"]:
                    aligned[at : at + kept, to * LANES : (to + 1) * LANES] = jnp.zeros(
                        (kept, LANES), BF16
                    )
        shift = layer["shift"]
        first = layer["bias"] - base * LANES - shift
        row, fixed = divmod(first, LANES)
        here = pltpu.roll(whole[row : row + 1, :], (LANES - fixed) % LANES, 1)
        after = pltpu.roll(whole[row + 1 : row + 2, :], (LANES - fixed) % LANES, 1)
        line = iota((1, LANES), 1)
        value = jnp.where(line < LANES - fixed, here, after)
        bias_out[index : index + 1, :] = jnp.where(
            (line >= shift) & (line < shift + outgoing), value, 0.0
        )

    for back, low, high in classes:
        wide = 9 if back == 0 else 10
        result[low:high, :] = jnp.dot(
            aligned[low:high, : wide * LANES],
            order[LANES + back : LANES + back + wide * LANES, :],
            preferred_element_type=F32,
        ).astype(BF16)

    for at_out, index in enumerate(indices):
        layer = LAYERS[index]
        outgoing = layer["out"]
        shift = layer["shift"]
        out = outs[at_out]
        width = layer["blocks"] * LANES
        if outgoing == 2:
            heads[...] = jnp.zeros_like(heads)
        elif outgoing < LANES:
            out[...] = jnp.zeros_like(out)
        kept = -(-outgoing // 16) * 16
        for block in range(layer["blocks"]):
            for k in range(9):
                total = None
                for s, segment in enumerate(layer["segments"]):
                    if segment["block"] != block:
                        continue
                    at = groups[index, s]
                    tile = result[at : at + kept, k * LANES : (k + 1) * LANES]
                    if segment["n"] < LANES:
                        tile = tile * within(segment["n"], segment["lane"])
                    total = tile if total is None else total + tile
                if outgoing == 2:
                    heads[2 * k : 2 * k + 2, block * LANES : (block + 1) * LANES] = total.astype(
                        F32
                    )[:2]
                else:
                    ky, kx = divmod(k, 3)
                    at = kx * width + block * LANES
                    out[ky * LANES + shift : ky * LANES + shift + outgoing, at : at + LANES] = total
        if outgoing == 2:
            out[...] = heads[:, :width].astype(BF16)


def pack_scratch(indices, count):
    _, _, group_rows = sort_groups(indices)
    return (
        pltpu.VMEM((count + 64, LANES), F32),
        pltpu.VMEM((40 * LANES + 64, LANES), F32),
        pltpu.VMEM((group_rows, 9 * LANES), BF16),
        pltpu.VMEM((group_rows, 10 * LANES), F32),
        pltpu.VMEM((LANES + 16, 5 * LANES), F32),
    )


def pack_gradients(indices, base, place_at, grads, bias_in, carried, halves, carry_out, order, scratch):
    whole, slabs, gathered, result, heads = scratch
    count = whole.shape[0] - 64
    groups, classes, _ = sort_groups(indices)
    for at_in, index in enumerate(indices):
        layer = LAYERS[index]
        outgoing = layer["out"]
        shift = layer["shift"]
        grad = grads[at_in]
        width = layer["blocks"] * LANES
        if outgoing == 2:
            heads[:LANES, :width] = grad[...].astype(F32)
            heads[LANES:, :] = jnp.zeros((16, heads.shape[1]), F32)
        for s, segment in enumerate(layer["segments"]):
            at = groups[index, s]
            block = segment["block"]
            for k in range(9):
                if outgoing == 2:
                    tile = heads[2 * k : 2 * k + 16, block * LANES : (block + 1) * LANES]
                    tile = tile.astype(BF16)
                else:
                    ky, kx = divmod(k, 3)
                    column = kx * width + block * LANES
                    tile = grad[
                        ky * LANES + shift : ky * LANES + shift + outgoing, column : column + LANES
                    ]
                if segment["n"] < LANES:
                    tile = tile * within(segment["n"], segment["lane"])
                gathered[at : at + tile.shape[0], k * LANES : (k + 1) * LANES] = tile

    for back, low, high in classes:
        wide = 9 if back == 0 else 10
        result[low:high, : wide * LANES] = lax.dot_general(
            gathered[low:high, :],
            order[LANES + back : LANES + back + wide * LANES, :],
            NT,
            preferred_element_type=F32,
        )

    lane = iota((8, LANES), 1)
    sub = iota((8, LANES), 0)

    for at_in, index in enumerate(indices):
        layer = LAYERS[index]
        outgoing = layer["out"]
        start = layer["start"] - base * LANES
        still = layer["row"] % LANES == 0
        pitch = pitch_of(layer["chunks"])
        spot = iota((outgoing, LANES), 1)
        turned = []
        for t in range(layer["chunks"]):
            chunk = None
            for s, segment in enumerate(layer["segments"]):
                to = t - segment["first"]
                if 0 <= to < segment["chunks"]:
                    to += segment["slot"]
                    at = groups[index, s]
                    tile = result[at : at + outgoing, to * LANES : (to + 1) * LANES]
                    chunk = tile if chunk is None else chunk + tile
            if still:
                turned.append(pltpu.roll(chunk, start % LANES, 1))
            else:
                slabs[pl.ds(t, outgoing, stride=pitch), :] = chunk
        if still:
            row, fixed = divmod(start, LANES)
            step = layer["row"] // LANES
            for t in range(step):
                before = turned[t - 1] if t else pltpu.roll(turned[-1], 1, 0)
                value = jnp.where(spot >= fixed, turned[t], before)
                if t == 0:
                    kept = whole[row : row + 1, :]
                    top = (iota((outgoing, LANES), 0) == 0) & (spot < fixed)
                    value = jnp.where(top, kept, value)
                whole[pl.ds(row + t, outgoing, stride=step), :] = value
            last = pltpu.roll(turned[-1][outgoing - 8 :, :], 1, 0)
            end = row + step * outgoing
            pltpu.store(whole.at[end : end + 8, :], last, mask=(sub == 0) & (lane < fixed))
        else:
            unroll = min(32, outgoing)

            def put(i, start=start, row=layer["row"], pitch=pitch, unroll=unroll):
                for u in range(unroll):
                    o = i * unroll + u
                    first = start + o * row
                    off = first & (LANES - 1)
                    for v in range(pitch // 8):
                        tile = pltpu.roll(slabs[rows_at(o * pitch + 8 * v, 8), :], off, 1)
                        to = (first >> 7) + 8 * v
                        pltpu.store(whole.at[pl.ds(to, 8), :], tile, mask=lane >= off)
                        pltpu.store(whole.at[pl.ds(to + 1, 8), :], tile, mask=lane < off)

            for i in range(outgoing // unroll):
                put(i)
        line = bias_in[index : index + 1, :]
        first = layer["bias"] - base * LANES
        row, fixed = divmod(first, LANES)
        line = pltpu.roll(line, (fixed - layer["shift"]) % LANES, 1)
        line = jnp.broadcast_to(line, (8, LANES))
        pltpu.store(whole.at[row : row + 8, :], line, mask=(sub == 0) & (lane >= fixed))
        pltpu.store(whole.at[row + 1 : row + 9, :], line, mask=(sub == 0) & (lane < fixed))
    if base:
        end, off = divmod(COUNT - base * LANES, LANES)
        pltpu.store(
            whole.at[end : end + 8, :], jnp.zeros((8, LANES), F32), mask=(sub > 0) | (lane >= off)
        )
        if count > end + 8:
            whole[end + 8 : count, :] = jnp.zeros((count - end - 8, LANES), F32)
        carry_out[...] = whole[: carry_out.shape[0], :].astype(BF16)
    else:
        end, off = divmod(LAYERS[4]["start"], LANES)
        line = carried[...].astype(F32)
        keep = (iota(line.shape, 0) > end - CUT) | (
            (iota(line.shape, 0) == end - CUT) & (iota(line.shape, 1) >= off)
        )
        whole[CUT:count, :] = jnp.where(keep, line, whole[CUT:count, :])
    for half in range(2):
        size = halves[half].shape[1]
        for j in range(halves[half].shape[0]):
            begin = place_at[half, j] - base

            def narrow(i, half=half, j=j, begin=begin):
                halves[half][j, rows_at(i * 16, 16, 16), :] = whole[
                    pl.ds(begin + i * 16, 16), :
                ].astype(BF16)

            lax.fori_loop(0, size // 16, lambda i, c: (narrow(i), c)[1], 0, unroll=8)


ROWS4 = 4 * PW
SEC_ROWS = (PH + 2 * SR) * PITCH + LANES


def load_second(joined, second):
    second[...] = jnp.zeros_like(second)
    keep = iota((PW, LANES), 1) < FC
    for y in range(MARGIN, PH - MARGIN):
        row = joined[y * PW : (y + 1) * PW, :].astype(F32)
        row = jnp.where(keep, pltpu.roll(row, LANES - FC, 1), 0.0)
        at = (y + SR) * PITCH + 8
        second[at : at + PW, :] = row


def start_copies(sources, targets, semaphores):
    copies = [
        pltpu.make_async_copy(source, target, semaphores.at[i])
        for i, (source, target) in enumerate(zip(sources, targets))
    ]
    for copy in copies:
        copy.start()
    return copies


def windows_kernel(*refs):
    out = refs[4]
    features, coarse, target, mask = refs[5:9]
    for copy in start_copies(refs[:4], refs[5:9], refs[9]):
        copy.wait()
    own_rows, width = mask.shape[1:]
    devices = out.shape[0]
    breadth = width // devices
    side = jnp.zeros((CHANNELS - 1, MARGIN), F32)
    arrays = [features[0].astype(F32), coarse[0].astype(F32), target[0].astype(F32)]
    marks = mask[0].astype(F32)
    for r in range(own_rows):
        valid = marks[r : r + 1, :]
        tall = jnp.concatenate([a[:, r, :] for a in arrays] + [valid], axis=0)
        tall = jnp.concatenate([side, tall, side], axis=1)
        count = sum(valid[:, at : at + PW] for at in range(0, width, PW))
        for t in range(devices):
            tile = jnp.concatenate([tall[:, t * breadth : t * breadth + PW], count], axis=0)
            out[t, :, r * PW : (r + 1) * PW] = tile.astype(BF16)


def windows(features, coarse, target, mask, devices):
    return pl.pallas_call(
        windows_kernel,
        out_shape=jax.ShapeDtypeStruct((devices, CHANNELS, mask.shape[1] * PW), BF16),
        in_specs=[pl.BlockSpec(memory_space=pltpu.HBM)] * 4,
        scratch_shapes=[pltpu.VMEM(a.shape, a.dtype) for a in (features, coarse, target, mask)]
        + [pltpu.SemaphoreType.DMA((4,))],
        compiler_params=pltpu.CompilerParams(vmem_limit_bytes=60 * 2**20),
        name="windows",
    )(features, coarse, target, mask)


def band_shift(dy, third):
    return EXT * dy - PITCH * third - (8 - SR)


def correlate_kernel(received, stack0, cost_out, joined_out, second, cost, joined, copied):
    joined[...] = jnp.zeros_like(joined)
    blocks = received.shape[0]
    spare = jnp.zeros((LANES - received.shape[1], LANES), F32)
    for s in range(blocks):
        tile = received[s].astype(F32)
        tile = jnp.concatenate([tile, spare], axis=0).T
        joined[RIM // 2 + s * ROWS4 : RIM // 2 + (s + 1) * ROWS4, :] = tile.astype(BF16)
    copies = start_copies([joined], [joined_out], copied)
    load_second(joined, second)
    row = iota((ROWS4, ROWS4), 0)
    col = iota((ROWS4, ROWS4), 1)
    flip = jnp.where((row // PW == col // PW) & (row % PW + col % PW == PW - 1), 1.0, 0.0).astype(
        BF16
    )
    lane = iota((ROWS4, LANES), 1)
    narrow = iota((PW, LANES), 1)

    def body(i):
        own = joined[rows_at(i * ROWS4, ROWS4, ROWS4), :]
        first = jnp.where(lane < FC, own.astype(F32), 0.0).astype(BF16)
        first = jnp.dot(flip, first, preferred_element_type=F32).astype(BF16)
        bands = []
        for g in range(4):
            window = second[rows_at((4 * i + 3 * g) * PITCH, LANES), :].astype(BF16)
            bands.append(lax.dot_general(first, window, NT, preferred_element_type=F32))
        pieces = []
        for yy in range(4):
            total = jnp.zeros((PW, LANES), F32)
            turned = [
                pltpu.roll(band[yy * PW : (yy + 1) * PW, :], 0, 1, stride=1, stride_axis=0)
                for band in bands
            ]
            for dy in range(EXT):
                t = yy + dy
                shift = (band_shift(dy, t % 3) - (PW - 1)) % LANES
                band = pltpu.roll(turned[t // 3], shift, 1)
                total = jnp.where((narrow >= EXT * dy) & (narrow < EXT * (dy + 1)), band, total)
            pieces.append(total * (1.0 / FC))
        total = jnp.concatenate(pieces, axis=0)
        high = total.astype(BF16)
        low = (total - high.astype(F32)).astype(BF16)
        total = jnp.dot(flip, high, preferred_element_type=F32) + jnp.dot(
            flip, low, preferred_element_type=F32
        )
        cost[rows_at(i * ROWS4, ROWS4, ROWS4), :] = total
        wide = own.astype(F32)
        filled = jnp.where(lane < NCOST, leaky(total), pltpu.roll(wide, NCOST, 1))
        coarse = pltpu.roll(wide, NCOST + FC - 2 * FC, 1)
        filled = jnp.where(lane >= NCOST + FC, coarse, filled)
        filled = jnp.where(lane < NS0, filled, 0.0)
        stack0[rows_at(i * ROWS4, ROWS4, ROWS4), :] = filled.astype(BF16)

    for i in range(PH // 4):
        body(i)
    copies.append(pltpu.make_async_copy(cost, cost_out, copied.at[1]))
    copies[1].start()
    for copy in copies:
        copy.wait()


def correlate(received):
    vmem = pl.BlockSpec(memory_space=pltpu.VMEM)
    anywhere = pl.BlockSpec(memory_space=pltpu.HBM)
    return pl.pallas_call(
        correlate_kernel,
        out_shape=[
            jax.ShapeDtypeStruct((PX, LANES), BF16),
            jax.ShapeDtypeStruct((PX, LANES), F32),
            jax.ShapeDtypeStruct((PX, LANES), BF16),
        ],
        out_specs=[vmem, anywhere, anywhere],
        scratch_shapes=[
            pltpu.VMEM((SEC_ROWS, LANES), F32),
            pltpu.VMEM((PX, LANES), F32),
            pltpu.VMEM((PX, LANES), BF16),
            pltpu.SemaphoreType.DMA((2,)),
        ],
        compiler_params=pltpu.CompilerParams(vmem_limit_bytes=60 * 2**20),
        cost_estimate=pl.CostEstimate(
            flops=8_000_000_000, bytes_accessed=2_000_000, transcendentals=0
        ),
        name="correlate",
    )(received)


class Work:
    def __init__(self, taps, moved, partial):
        self.taps = taps
        self.moved = moved
        self.partial = partial
        self.column = iota((STRIP, LANES), 0) % PW
        self.lane = iota((STRIP, LANES), 1)
        if taps is not None:
            taps[:, :RIM, :] = jnp.zeros((3, RIM, LANES), F32)
            taps[:, RIM + PX :, :] = jnp.zeros((3, RIM, LANES), F32)
        if moved is not None:
            moved[:, :RIM, :] = jnp.zeros((3, RIM, LANES), BF16)
            moved[:, RIM + PX :, :] = jnp.zeros((3, RIM, LANES), BF16)

    def strips(self, body):
        for at in range(0, PX, STRIP):
            body(pl.ds(at, STRIP), at)

    def inside(self, tile, shift):
        if shift == 0:
            return tile
        valid = (self.column + shift >= 0) & (self.column + shift < PW)
        return jnp.where(valid, pltpu.roll(tile, (-shift) % STRIP, 0), 0.0)

    def spread(self, store, tile, dilation):
        for kx in range(3):
            store(kx, self.inside(tile, (kx - 1) * dilation).astype(BF16))

    def multiply(self, load, kernel):
        def body(i):
            rows = rows_at(i * MT, MT, MT)
            value = jnp.concatenate([load(kx, rows) for kx in range(3)], axis=1)
            product = lax.dot_general(value, kernel[...], NT, preferred_element_type=F32)
            for ky in range(3):
                self.taps[ky, rows_at(RIM + i * MT, MT, MT), :] = product[
                    :, ky * LANES : (ky + 1) * LANES
                ]

        for i in range(PX // MT):
            body(i)

    def collect(self, at, dilation):
        total = None
        for ky in range(3):
            tile = self.taps[ky, rows_at(RIM + at + (ky - 1) * dilation * PW, STRIP, PW), :]
            total = tile if total is None else total + tile
        return total

    def spread_grad(self, at, grad, dilation):
        for kx in range(3):
            self.moved[kx, rows_at(RIM + at, STRIP, STRIP), :] = self.inside(
                grad, -(kx - 1) * dilation
            ).astype(BF16)

    def count_bias(self, index, grad):
        self.partial[index] += grad.reshape(STRIP // 8, 8, LANES).sum(0)

    def back(self, index, load_grad, load_pre, load_input, kernel, out, store, waits=()):
        layer = LAYERS[index]
        dilation = layer["dil"]
        width = layer["blocks"] * LANES

        def through(rows, at):
            grad = load_grad(rows) * leaky_slope(load_pre(rows))
            grad = grad.astype(BF16).astype(F32)
            self.count_bias(index, grad)
            self.spread_grad(at, grad, dilation)

        self.strips(through)
        for load in waits:
            load.wait()
        grad = jnp.concatenate(
            [
                self.moved[1, RIM - (ky - 1) * dilation * PW : RIM - (ky - 1) * dilation * PW + PX, :]
                for ky in range(3)
            ],
            axis=1,
        )
        values = [load_input(kx) for kx in range(3)]
        if index in LATE:
            values = [jnp.concatenate(values, axis=1)]
        for i, value in enumerate(values):
            out[:, i * value.shape[1] : (i + 1) * value.shape[1]] = lax.dot_general(
                grad, value, TN, preferred_element_type=F32
            ).astype(BF16)

        def input_grad(i):
            tiles = [
                self.moved[kx, rows_at(RIM + i * MT - (ky - 1) * dilation * PW, MT, PW), :]
                for ky in range(3)
                for kx in range(3)
            ]
            weights = [
                kernel[ky * LANES : (ky + 1) * LANES, kx * width : (kx + 1) * width]
                for ky in range(3)
                for kx in range(3)
            ]
            store(
                rows_at(i * MT, MT, MT),
                jnp.dot(
                    jnp.concatenate(tiles, axis=1),
                    jnp.concatenate(weights, axis=0),
                    preferred_element_type=F32,
                ),
            )

        for i in range(PX // MT):
            input_grad(i)


def forward_kernel(half, place_at, stack0, *refs):
    own, other, refs = refs[:half], refs[half : 2 * half], refs[2 * half :]
    kernels_out, carry_out, (stack_out, top_out, pre_out) = refs[:4], refs[4], refs[5:8]
    kernels, refs = refs[8:12], refs[12:]
    stack, top, pre, biases, order, taps, copied = refs[:7]
    fill_order(order)
    unpack_weights(
        EARLY, 0, place_at, (own, other), None, kernels, biases, carry_out, order, refs[7:]
    )
    copies = start_copies(kernels, kernels_out, copied)
    work = Work(taps, None, None)

    def send(source, target):
        copies.append(pltpu.make_async_copy(source, target, copied.at[len(copies)]))
        copies[-1].start()

    def first(rows, at):
        tile = stack0[rows, :].astype(F32)

        def keep(kx, value):
            stack[kx, rows, :LANES] = value

        work.spread(keep, tile, 1)

    work.strips(first)
    send(stack.at[:, :, :LANES], stack_out.at[:, :, :LANES])
    for index, kernel in enumerate(kernels):
        width = LAYERS[index]["blocks"] * LANES
        work.multiply(lambda kx, rows, width=width: stack[kx, rows, :width], kernel)

        place = slice((index + 1) * LANES, (index + 2) * LANES)

        def finish(rows, at, index=index, place=place):
            value = work.collect(at, 1) + biases[index : index + 1, :]
            pre[index, rows, :] = value

            def keep(kx, value):
                if index == 3:
                    top[kx, rows, :] = value
                else:
                    stack[kx, rows, place] = value

            work.spread(keep, leaky(value), 1)

        work.strips(finish)
        send(pre.at[index], pre_out.at[index])
        if index == 3:
            send(top, top_out)
        else:
            send(stack.at[:, :, place], stack_out.at[:, :, place])
    for copy in copies:
        copy.wait()


def forward(place_at, parts, stack0, count):
    vmem = pl.BlockSpec(memory_space=pltpu.VMEM)
    anywhere = pl.BlockSpec(memory_space=pltpu.HBM)
    kernels = [(LAYERS[i]["shape"], BF16) for i in EARLY]
    states = [((3, PX, 4 * LANES), BF16), ((3, PX, LANES), BF16), ((4, PX, LANES), F32)]
    outs = pl.pallas_call(
        functools.partial(forward_kernel, len(parts[0])),
        out_shape=[
            jax.ShapeDtypeStruct(*a) for a in (*kernels, ((count - CUT, LANES), BF16), *states)
        ],
        in_specs=[pl.BlockSpec(memory_space=pltpu.SMEM)] + [vmem] * (1 + 2 * len(parts[0])),
        out_specs=[anywhere] * 4 + [vmem] + [anywhere] * 3,
        scratch_shapes=[
            *[pltpu.VMEM(*a) for a in (*kernels, *states)],
            pltpu.VMEM((16, LANES), F32),
            ORDER,
            pltpu.VMEM((3, PX + 2 * RIM, LANES), F32),
            pltpu.SemaphoreType.DMA((13,)),
            *unpack_scratch(EARLY, count),
        ],
        compiler_params=pltpu.CompilerParams(vmem_limit_bytes=60 * 2**20),
        cost_estimate=pl.CostEstimate(
            flops=25_000_000_000, bytes_accessed=20_000_000, transcendentals=0
        ),
        name="dense_forward",
    )(place_at, stack0, *parts[0], *parts[1])
    return outs[:4], *outs[4:]


def late_kernel(
    rows,
    half,
    groups,
    pixels,
    gather_at,
    pack_at,
    carried,
    stack_in,
    below_in,
    joined_in,
    *refs,
):
    counts, refs = refs[:groups], refs[groups:]
    own, other, refs = refs[:half], refs[half : 2 * half], refs[2 * half :]
    motion_out, dstack_out, bias_out, keep, send, carry_out = refs[:6]
    order, biases, dstack, stack, below, joined, copied = refs[6:13]
    refs = refs[13:]
    kernels = refs[:9]
    grads = refs[9:]
    loads = [
        pltpu.make_async_copy(source, target, copied.at[i])
        for i, (source, target) in enumerate(zip((stack_in, below_in, joined_in), (stack, below, joined)))
    ]
    for load in loads:
        load.start()
    fill_order(order)

    def first(*scratch):
        unpack_weights(
            LATE, CUT, gather_at, (own, other), carried, kernels, biases, None, order, scratch
        )

    pl.run_scoped(first, *unpack_scratch(LATE, rows))
    for load in loads:
        load.wait()

    weighting = pixels / sum(count[:1, :] for count in counts)

    def second(*scratch):
        context(
            stack, below, joined, weighting, biases, kernels, motion_out, dstack, bias_out, grads, *scratch
        )

    pl.run_scoped(second, *CONTEXT_SCRATCH)
    store = pltpu.make_async_copy(dstack, dstack_out, copied.at[3])
    store.start()

    def third(*scratch):
        pack_gradients(
            LATE, CUT, pack_at, grads, bias_out, None, (keep, send), carry_out, order, scratch
        )

    pl.run_scoped(third, *pack_scratch(LATE, rows))
    store.wait()


def context(
    stack, below, joined, weighting, biases, kernels, motion_out, dstack, bias_out, grads, *scratch
):
    kernels = dict(zip(LATE, kernels))
    grads = dict(zip(LATE, grads))
    top, ctx, pre, taps, moved, dcur, ghead, partial = scratch
    work = Work(taps, moved, partial)
    partial[...] = jnp.zeros_like(partial)
    lane = work.lane

    def wide(kx, rows):
        return jnp.concatenate([stack[kx, rows, :], top[kx, rows, :]], axis=1)

    work.multiply(
        lambda kx, rows: jnp.concatenate([stack[kx, rows, :], below[kx, rows, :]], axis=1),
        kernels[4],
    )

    def finish_top(rows, at):
        value = work.collect(at, 1) + biases[4:5, :]
        pre[0, rows, :] = value

        def keep(kx, value):
            top[kx, rows, :] = value + below[kx, rows, :]

        work.spread(keep, leaky(value), 1)

    work.strips(finish_top)
    for index in range(6, 12):
        if index == 6:
            work.multiply(wide, kernels[index])
        else:
            work.multiply(lambda kx, rows, index=index: ctx[index - 7, kx, rows, :], kernels[index])

        def finish(rows, at, index=index):
            value = work.collect(at, LAYERS[index]["dil"]) + biases[index : index + 1, :]
            pre[index - 5, rows, :] = value

            def keep(kx, value):
                ctx[index - 6, kx, rows, :] = value

            work.spread(keep, leaky(value), LAYERS[index + 1]["dil"])

        work.strips(finish)

    def head(i):
        rows = rows_at(i * MT, MT, MT)
        product = lax.dot_general(wide(1, rows), kernels[5][...], NT, preferred_element_type=F32)
        product = product + lax.dot_general(
            ctx[5, 1, rows, :], kernels[12][...], NT, preferred_element_type=F32
        )
        taps[0, rows_at(RIM + i * MT, MT, MT), :] = product

    for i in range(PX // MT):
        head(i)

    row = iota((LANES, LANES), 0)
    col = iota((LANES, LANES), 1)
    used = (col < 18) & (row % 2 == col % 2)
    fold = jnp.where(used & (row < 18), 1.0, 0.0)
    copies = jnp.where(used & (row < 2), 1.0, 0.0).astype(BF16)
    pick = jnp.where(used & (row >= 2 * FC + 4) & (row < 2 * FC + 6), 1.0, 0.0).astype(BF16)
    marked = jnp.where(row == 2 * FC + 6, 1.0, 0.0).astype(BF16)
    shared = sum(
        jnp.dot(jnp.broadcast_to(b, (8, LANES)).astype(BF16), copies, preferred_element_type=F32)
        for b in (biases[5:6, :], biases[12:13, :])
    )[:1]

    def settle(rows, at):
        total = None
        for kx in range(3):
            part = None
            for ky in range(3):
                tile = taps[0, rows_at(RIM + at + (ky - 1) * PW, STRIP, PW), :]
                tile = jnp.where(lane // 2 == ky * 3 + kx, tile, 0.0)
                part = tile if part is None else part + tile
            part = work.inside(part, kx - 1)
            total = part if total is None else total + part
        motion = (
            jnp.dot(total, fold, preferred_element_type=F32, precision=lax.Precision.HIGHEST)
            + shared
        )
        motion_out[:, rows] = motion.T[: motion_out.shape[0]]
        own = joined[rows, :]
        aim = jnp.dot(own, pick, preferred_element_type=F32)
        mask = jnp.dot(own, marked, preferred_element_type=F32)
        mismatch = motion - aim
        square = mismatch * mismatch
        other = jnp.where(
            lane % 2 == 0, pltpu.roll(square, LANES - 1, 1), pltpu.roll(square, 1, 1)
        )
        length = jnp.sqrt(square + other + EPE_EPS)
        height = (iota((STRIP, LANES), 0) + at) // PW
        interior = (
            (height >= MARGIN)
            & (height < PH - MARGIN)
            & (work.column >= MARGIN)
            & (work.column < PW - MARGIN)
            & (lane < 18)
        )
        grad = jnp.where(interior, weighting * mask * mismatch / length, 0.0)
        grad = grad.astype(BF16).astype(F32)
        work.count_bias(5, grad)
        work.spread_grad(at, grad, 1)

    work.strips(settle)
    partial[12] = partial[5]

    def choose(rows, at):
        total = None
        for kx in range(3):
            for ky in range(3):
                tile = moved[kx, rows_at(RIM + at - (ky - 1) * PW, STRIP, PW), :].astype(F32)
                tile = jnp.where(lane // 2 == ky * 3 + kx, tile, 0.0)
                total = tile if total is None else total + tile
        ghead[rows, :] = total.astype(BF16)

    work.strips(choose)
    grads[5][:, : 4 * LANES] = lax.dot_general(
        ghead[...], stack[1], TN, preferred_element_type=F32
    ).astype(BF16)
    grads[5][:, 4 * LANES :] = lax.dot_general(
        ghead[...], top[1], TN, preferred_element_type=F32
    ).astype(BF16)
    grads[12][...] = lax.dot_general(
        ghead[...], ctx[5, 1], TN, preferred_element_type=F32
    ).astype(BF16)

    def head_back(i):
        rows = rows_at(i * MT, MT, MT)
        dstack[rows, :] = jnp.dot(ghead[rows, :], kernels[5][...], preferred_element_type=F32)
        dcur[rows, :] = jnp.dot(ghead[rows, :], kernels[12][...], preferred_element_type=F32)

    for i in range(PX // MT):
        head_back(i)

    def store_current(rows, value):
        dcur[rows, :] = value

    def store_stack(rows, value):
        dstack[rows, :] += value

    for index in range(11, 6, -1):
        work.back(
            index,
            lambda rows: dcur[rows, :],
            lambda rows, index=index: pre[index - 5, rows, :],
            lambda kx, index=index: ctx[index - 7, kx],
            kernels[index],
            grads[index],
            store_current,
        )
    work.back(
        6,
        lambda rows: dcur[rows, :],
        lambda rows: pre[1, rows, :],
        lambda kx: jnp.concatenate([stack[kx], top[kx]], axis=1),
        kernels[6],
        grads[6],
        store_stack,
    )
    work.back(
        4,
        lambda rows: dstack[rows, 4 * LANES :],
        lambda rows: pre[0, rows, :],
        lambda kx: jnp.concatenate([stack[kx], top[kx]], axis=1),
        kernels[4],
        grads[4],
        store_stack,
    )
    bias_out[...] = partial[...].sum(1)


CONTEXT_SCRATCH = (
    pltpu.VMEM((3, PX, LANES), BF16),
    pltpu.VMEM((6, 3, PX, LANES), BF16),
    pltpu.VMEM((7, PX, LANES), F32),
    pltpu.VMEM((3, PX + 2 * RIM, LANES), F32),
    pltpu.VMEM((3, PX + 2 * RIM, LANES), BF16),
    pltpu.VMEM((PX, LANES), F32),
    pltpu.VMEM((PX, LANES), BF16),
    pltpu.VMEM((16, 8, LANES), F32),
)


def late(gather_at, pack_at, parts, carried, stack, below, joined, counts, pixels, end, pieces, size):
    smem = pl.BlockSpec(memory_space=pltpu.SMEM)
    vmem = pl.BlockSpec(memory_space=pltpu.VMEM)
    anywhere = pl.BlockSpec(memory_space=pltpu.HBM)
    shapes = [pltpu.VMEM(LAYERS[i]["shape"], BF16) for i in LATE]
    return pl.pallas_call(
        functools.partial(late_kernel, end - CUT, len(parts[0]), len(counts), float(pixels)),
        out_shape=[
            jax.ShapeDtypeStruct((8, PX), F32),
            jax.ShapeDtypeStruct((PX, 5 * LANES), F32),
            jax.ShapeDtypeStruct((16, LANES), F32),
            jax.ShapeDtypeStruct((pieces, size, LANES), BF16),
            jax.ShapeDtypeStruct((pieces, size, LANES), BF16),
            jax.ShapeDtypeStruct((end // 2 - CUT, LANES), BF16),
        ],
        in_specs=[smem] * 2 + [vmem] + [anywhere] * 3 + [vmem] * (len(counts) + 2 * len(parts[0])),
        out_specs=[vmem, anywhere, vmem, vmem, vmem, vmem],
        scratch_shapes=[
            ORDER,
            pltpu.VMEM((16, LANES), F32),
            pltpu.VMEM((PX, 5 * LANES), F32),
            pltpu.VMEM(stack.shape, BF16),
            pltpu.VMEM(below.shape, BF16),
            pltpu.VMEM(joined.shape, BF16),
            pltpu.SemaphoreType.DMA((4,)),
            *shapes,
            *shapes,
        ],
        compiler_params=pltpu.CompilerParams(vmem_limit_bytes=60 * 2**20),
        cost_estimate=pl.CostEstimate(
            flops=80_000_000_000, bytes_accessed=20_000_000, transcendentals=0
        ),
        name="context",
    )(gather_at, pack_at, carried, stack, below, joined, *counts, *parts[0], *parts[1])


def correlate_back(joined, cost, grads, second, dsecond, collected, out):
    load_second(joined, second)
    dsecond[...] = jnp.zeros_like(dsecond)
    lane = iota((ROWS4, LANES), 1)
    narrow = iota((PW, LANES), 1)

    def body(i):
        rows = rows_at(i * ROWS4, ROWS4, ROWS4)
        own = joined[rows, :]
        first = jnp.where(lane < FC, own.astype(F32), 0.0).astype(BF16)
        grad = grads[rows, :LANES]
        volume = grad * leaky_slope(cost[rows, :]) * (1.0 / FC)
        dfirst = jnp.zeros((ROWS4, LANES), F32)
        for g in range(4):
            pieces = []
            for yy in range(4):
                piece = jnp.zeros((PW, LANES), F32)
                own_rows = volume[yy * PW : (yy + 1) * PW, :]
                for t in range(3 * g, 3 * g + 3):
                    dy = t - yy
                    if dy < 0 or dy >= EXT:
                        continue
                    part = jnp.where(
                        (narrow >= EXT * dy) & (narrow < EXT * (dy + 1)), own_rows, 0.0
                    )
                    shift = (-band_shift(dy, t % 3)) % LANES
                    piece = piece + pltpu.roll(part, shift, 1)
                pieces.append(pltpu.roll(piece, 0, 1, stride=1, stride_axis=0))
            band = jnp.concatenate(pieces, axis=0).astype(BF16)
            at = rows_at((4 * i + 3 * g) * PITCH, LANES)
            dfirst = dfirst + jnp.dot(
                band, second[at, :].astype(BF16), preferred_element_type=F32
            )
            dsecond[at, :] += lax.dot_general(band, first, TN, preferred_element_type=F32)
        direct = pltpu.roll(grad, LANES - NCOST, 1)
        coarse = pltpu.roll(grad, LANES + 2 * FC - NCOST - FC, 1)
        filled = jnp.where(lane < FC, dfirst + direct, 0.0)
        filled = jnp.where((lane >= 2 * FC) & (lane < 2 * FC + 4), coarse, filled)
        collected[rows, :] = filled

    for i in range(PH // 4):
        body(i)
    for s in range((PH - 2 * MARGIN) // 4):
        pieces = []
        for yy in range(4):
            at = (MARGIN + 4 * s + yy + SR) * PITCH + 8
            pieces.append(dsecond[at : at + PW, :])
        other = pltpu.roll(jnp.concatenate(pieces, axis=0), FC, 1)
        start = (MARGIN + 4 * s) * PW
        tile = collected[start : start + ROWS4, :]
        tile = jnp.where((lane >= FC) & (lane < 2 * FC), other, tile)
        out[s] = tile.T[: out.shape[1]].astype(BF16)


def early_kernel(
    pack_at,
    stack_in,
    pre_in,
    dstack_in,
    cost_in,
    joined_in,
    bias_in,
    carried,
    k1,
    k2,
    k3,
    k4,
    picture_out,
    keep,
    send,
    order,
    stack,
    pre,
    dstack,
    cost,
    joined,
    bias_out,
    copied,
    *grads,
):
    sources = (dstack_in, pre_in, stack_in, cost_in, joined_in)
    targets = (dstack, pre, stack, cost, joined)
    loads = [
        pltpu.make_async_copy(source, target, copied.at[i])
        for i, (source, target) in enumerate(zip(sources, targets))
    ]
    for load in loads:
        load.start()
    fill_order(order)
    for load in loads[:2]:
        load.wait()

    def first(*scratch):
        dense_back(
            stack,
            pre,
            dstack,
            cost,
            joined,
            bias_in,
            (k1, k2, k3, k4),
            picture_out,
            bias_out,
            grads,
            loads[2:],
            *scratch,
        )

    pl.run_scoped(first, *DENSE_SCRATCH)

    def second(*scratch):
        pack_gradients(
            EARLY, 0, pack_at, grads, bias_out, carried, (keep, send), None, order, scratch
        )

    pl.run_scoped(second, *pack_scratch(EARLY, CUT + carried.shape[0]))


def dense_back(
    stack,
    pre,
    dstack,
    cost,
    joined,
    bias_in,
    kernels,
    picture_out,
    bias_out,
    grads,
    loads,
    moved,
    dwide,
    partial,
    second,
    dsecond,
    collected,
):
    work = Work(None, moved, partial)
    partial[...] = jnp.zeros_like(partial)
    dwide[...] = dstack[:, : 4 * LANES]

    def store_stack(rows, value):
        dwide[rows, : value.shape[1]] += value

    for index in range(3, -1, -1):
        width = LAYERS[index]["blocks"] * LANES

        def load_grad(rows, index=index):
            if index == 3:
                return dstack[rows, 4 * LANES :]
            return dwide[rows, (index + 1) * LANES : (index + 2) * LANES]

        work.back(
            index,
            load_grad,
            lambda rows, index=index: pre[index, rows, :],
            lambda kx, width=width: stack[kx, :, :width],
            kernels[index],
            grads[index],
            store_stack,
            loads if index == 3 else (),
        )
    bias_out[...] = partial[...].sum(1) + bias_in[...]
    correlate_back(joined, cost, dwide, second, dsecond, collected, picture_out)


DENSE_SCRATCH = (
    pltpu.VMEM((3, PX + 2 * RIM, LANES), BF16),
    pltpu.VMEM((PX, 4 * LANES), F32),
    pltpu.VMEM((16, 8, LANES), F32),
    pltpu.VMEM((SEC_ROWS, LANES), F32),
    pltpu.VMEM((SEC_ROWS, LANES), F32),
    pltpu.VMEM((PX, LANES), F32),
)


def backward(
    pack_at, stack, pre, dstack, cost, joined, bias_grads, carried, kernels, blocks, channels, pieces, size
):
    vmem = pl.BlockSpec(memory_space=pltpu.VMEM)
    large = (stack, pre, dstack, cost, joined)
    return pl.pallas_call(
        early_kernel,
        out_shape=[
            jax.ShapeDtypeStruct((blocks, channels, LANES), BF16),
            jax.ShapeDtypeStruct((pieces, size, LANES), BF16),
            jax.ShapeDtypeStruct((pieces, size, LANES), BF16),
        ],
        in_specs=[pl.BlockSpec(memory_space=pltpu.SMEM)]
        + [pl.BlockSpec(memory_space=pltpu.HBM)] * 5
        + [vmem] * 6,
        scratch_shapes=[
            ORDER,
            *[pltpu.VMEM(a.shape, a.dtype) for a in large],
            pltpu.VMEM((16, LANES), F32),
            pltpu.SemaphoreType.DMA((5,)),
            *[pltpu.VMEM(LAYERS[i]["shape"], BF16) for i in EARLY],
        ],
        compiler_params=pltpu.CompilerParams(vmem_limit_bytes=60 * 2**20),
        cost_estimate=pl.CostEstimate(
            flops=40_000_000_000, bytes_accessed=20_000_000, transcendentals=0
        ),
        name="dense_backward",
    )(pack_at, *large, bias_grads, carried, *kernels)


def update(weights, momentum, average, gradient):
    gradient = gradient + DECAY_RATE * weights
    renewed = MOMENTUM_RATE * momentum + gradient
    stepped = weights - LEARN_RATE * (gradient + MOMENTUM_RATE * renewed)
    return (stepped, renewed, AVERAGE_DECAY * average + (1.0 - AVERAGE_DECAY) * stepped)


def swapped(value, axis, step):
    count = lax.axis_size(axis)
    return lax.ppermute(value, axis, [(i, i ^ step) for i in range(count)])


def added(one, two):
    return (one.astype(F32) + two.astype(F32)).astype(BF16)


def core_sum(keep, send, groups, devices):
    got = swapped(send, "grp", 1)
    pieces = keep.shape[0] // 2
    if groups == 2:
        return [added(keep, got)]
    return [added(keep[pieces:], got[pieces:]), added(keep[:pieces], got[:pieces])]


def x_sum(value, groups, devices):
    half = devices // 2
    step = groups // 4
    if not step:
        value = value[0]
        return [value[j] for j in range(half)]
    away, value = value
    got = swapped(away, "grp", 2 * step)
    while step > 1:
        value = added(value, got)
        step //= 2
        pieces = value.shape[0] // 2
        got = swapped(value[pieces:], "grp", 2 * step)
        value = value[:pieces]
    return [added(value[j], got[j]) for j in range(half)]


def dev_sum(pieces):
    total = pieces[0].astype(F32)
    for j in range(1, len(pieces)):
        total = total + swapped(pieces[j], "dev", j).astype(F32)
    return total


def shared_parts(value, groups):
    x_size = groups // 2
    x = lax.axis_index("grp") // 2
    held = [0]
    parts = [value]
    step = 1
    while step < x_size:
        parts = parts + [swapped(p, "grp", 2 * step) for p in parts]
        held = held + [j ^ step for j in held]
        step *= 2

    def ordered(parts):
        out = []
        for i in range(x_size):
            piece = parts[0]
            for j, part in zip(held[1:], parts[1:]):
                piece = jnp.where((x ^ j) == i, part, piece)
            out.append(piece)
        return jnp.concatenate(out)

    return ordered(parts), ordered([swapped(p, "grp", 1) for p in parts])


def shards(features, coarse_flow, target, valid_mask, weights, momentum, average):
    groups = lax.axis_size("grp")
    devices = lax.axis_size("dev")
    own_rows = features.shape[2]
    width = features.shape[3]
    breadth = width // devices
    height = own_rows * devices
    assert breadth + 2 * MARGIN == PW and height + 2 * MARGIN == PH
    core = lax.axis_index("grp") % 2
    me = lax.axis_index("dev")
    half = devices // 2
    early = me < half
    rows = weights.shape[0] // LANES
    x_size = groups // 2
    size = -(-(rows // 2) // (16 * x_size)) * 16 * x_size
    table = weights.reshape(rows, LANES)
    own = lax.dynamic_slice(table, (core * (rows - size), 0), (size, LANES)).astype(BF16)

    received = windows(features, coarse_flow, target, valid_mask, devices)
    received = lax.all_to_all(received, "dev", split_axis=0, concat_axis=0, tiled=True)

    across = swapped(own, "dev", half)
    both = jnp.stack([core, 1 - core])[:, None] * (rows - size)
    steps = [half >> i for i in range(1, half.bit_length())]
    held = [0]
    for step in steps:
        held = held + [j ^ step for j in held]
    place = (jnp.array(held, jnp.int32) ^ (me % half))[None] * rows + both
    x = lax.axis_index("grp") // 2
    part_x = (jnp.arange(x_size, dtype=jnp.int32) ^ x) * (size // x_size)
    part_dev = (jnp.arange(half, dtype=jnp.int32) ^ (me % half)) * rows
    pack_at = (part_x[:, None] + part_dev[None]).reshape(1, -1) + both
    places = (place, place + half * rows, pack_at, pack_at + half * rows)
    across, received, *places = lax.optimization_barrier((across, received, *places))
    part, last = {0: jnp.where(early, own, across)}, {0: jnp.where(early, across, own)}
    other, other_last = {}, {}

    def grow(pieces, step):
        for j in list(pieces):
            if j ^ step not in pieces:
                pieces[j ^ step] = swapped(pieces[j], "dev", step)

    def swap_cores(pieces, others):
        for j in pieces:
            if j not in others:
                others[j] = swapped(pieces[j], "grp", 1)

    first_y = swapped(part[0], "dev", 1)
    swap_cores(part, other)
    for step in steps[:-1]:
        grow(part, step)
    counted = jnp.full((8, LANES), jnp.sum(received[:, CHANNELS - 1].astype(F32)))
    counts = [counted] + [swapped(counted, "grp", j) for j in range(1, groups)]
    keys = list(part)
    *tied, received, last[0] = lax.optimization_barrier(
        (*counts, *part.values(), received, last[0])
    )
    counts, part = tied[:groups], dict(zip(keys, tied[groups:]))
    swap_cores(part, other)
    swap_cores(last, other_last)
    part[1] = first_y
    grow(part, 1)
    for step in steps[:-1]:
        grow(last, step)
    per = 4 // own_rows
    blocks = devices // per
    received = received.reshape(blocks, per, CHANNELS, own_rows * PW)
    received = jnp.swapaxes(received, 1, 2).reshape(blocks, CHANNELS, LANES)
    stack0, cost, joined = correlate(received)
    keys, keys_last = list(part), list(last)
    *tied, stack0 = lax.optimization_barrier((*part.values(), *last.values(), stack0))
    part = dict(zip(keys, tied))
    last = dict(zip(keys_last, tied[len(keys) :]))
    swap_cores(part, other)
    grow(last, 1)
    parts = ([part[j] for j in held], [other[j] for j in held])
    kernels, carried, stack, below, pre = forward(places[0], parts, stack0, half * rows)
    keys_last = list(last)
    *tied, stack = lax.optimization_barrier((*last.values(), stack))
    last = dict(zip(keys_last, tied))
    swap_cores(last, other_last)
    parts = ([last[j] for j in held], [other_last[j] for j in held])
    pack_at, pack_late_at = places[2:]
    pieces = (half * x_size, size // x_size)
    motion, dstack, bias_grads, keep, send, carried = late(
        places[1],
        pack_late_at,
        parts,
        carried,
        stack,
        below,
        joined,
        counts,
        groups * height * width,
        devices * rows,
        *pieces,
    )
    flow = motion[:2].reshape(1, 2, PH, PW)[
        :, :, MARGIN : MARGIN + height, MARGIN : MARGIN + breadth
    ]
    late_sum = core_sum(keep, send, groups, devices)
    late_sum, dstack = lax.optimization_barrier((late_sum, dstack))
    late_sum = x_sum(late_sum, groups, devices)
    tiles, keep, send = backward(
        pack_at,
        stack,
        pre,
        dstack,
        cost,
        joined,
        bias_grads,
        carried,
        kernels,
        blocks,
        CHANNELS,
        *pieces,
    )
    late_sum, keep, send = lax.optimization_barrier((late_sum, keep, send))
    late_sum = dev_sum(late_sum)
    early_sum = core_sum(keep, send, groups, devices)
    tiles = tiles.reshape(blocks, CHANNELS, per, own_rows * PW)
    tiles = jnp.swapaxes(tiles, 1, 2).reshape(devices, CHANNELS, own_rows * PW)
    returned = lax.all_to_all(tiles, "dev", split_axis=0, concat_axis=0, tiled=True)
    early_sum = x_sum(early_sum, groups, devices)
    early_sum, late_sum, returned = lax.optimization_barrier((early_sum, late_sum, returned))
    early_sum = dev_sum(early_sum)
    total = jnp.where(early, early_sum, late_sum)
    passed = jnp.where(early, late_sum, early_sum).astype(BF16)
    total = (total + swapped(passed, "dev", half).astype(F32)).astype(BF16)
    total, rest = shared_parts(total, groups)
    low = jnp.where(core == 0, total, rest)
    high = jnp.where(core == 0, rest, total)
    total_grad = jnp.concatenate([low[: rows - size], high]).astype(F32).reshape(-1)

    returned = returned.reshape(devices, CHANNELS, own_rows, PW).astype(F32)
    wide = jnp.transpose(returned, (1, 2, 0, 3))
    centre = wide[..., MARGIN : MARGIN + breadth]
    left = wide[:, :, 1:, :MARGIN]
    right = wide[:, :, :-1, MARGIN + breadth :]
    none = ((0, 0), (0, 0))
    centre = centre + jnp.pad(left, (*none, (0, 1), (breadth - MARGIN, 0)))
    centre = centre + jnp.pad(right, (*none, (1, 0), (0, breadth - MARGIN)))
    row_grad = centre.reshape(1, CHANNELS, own_rows, width)
    feature_grad = row_grad[:, : 2 * FC]
    coarse_grad = row_grad[:, 2 * FC : 2 * FC + 4]

    new_weights, new_momentum, new_average = update(weights, momentum, average, total_grad)
    return (
        flow,
        feature_grad,
        coarse_grad,
        new_weights,
        new_momentum,
        new_average,
        new_weights.astype(BF16),
    )


def solution(mesh):
    in_specs = (
        P("grp", None, "dev", None),
        P("grp", None, "dev", None),
        P("grp", None, "dev", None),
        P("grp", "dev", None),
        P("dev"),
        P("dev"),
        P("dev"),
    )
    out_specs = (
        P("grp", None, None, "dev"),
        P("grp", None, "dev", None),
        P("grp", None, "dev", None),
        P("dev"),
        P("dev"),
        P("dev"),
        P("dev"),
    )
    return jax.shard_map(shards, mesh=mesh, in_specs=in_specs, out_specs=out_specs, check_vma=False)
```

```python
import functools

import jax
import jax.numpy as jnp
from jax import lax
from jax.experimental import pallas as pl
from jax.experimental.pallas import tpu as pltpu
from jax.sharding import PartitionSpec as P

FC = 32
SR = 4
EXT = 2 * SR + 1
NCOST = EXT * EXT
NS0 = NCOST + FC + 4
DENSE = (128, 128, 96, 64, 32)
CONTEXT = (128, 128, 128, 96, 64, 32, 2)
DILATIONS = (1, 2, 4, 8, 16, 1, 1)
MARGIN = 8

SLOPE = 0.1
EPE_EPS = 0.01
MOMENTUM_RATE = 0.5
AVERAGE_DECAY = 0.5
LEARN_RATE = 0.001
DECAY_RATE = 0.0001

LANES = 128
CHANNELS = 72
PH = 48
PW = 32
PX = PH * PW
RIM = 16 * PW
STRIP = 128
MT = 768
PITCH = 40
F32 = jnp.float32
BF16 = jnp.bfloat16
NT = (((1,), (1,)), ((), ()))
TN = (((0,), (0,)), ((), ()))


def layer_table():
    places = [(NS0, 0, 0), (128, 1, 0), (128, 2, 0), (96, 3, 0), (64, 4, 0), (32, 4, 64)]
    layers = []
    offset = 0

    def add(pieces, outgoing, dilation, shift):
        nonlocal offset
        incoming = sum(n for n, _, _ in pieces)
        row = 9 * incoming
        segments = []
        at = 0
        for n, block, lane in pieces:
            first, over = 9 * at // LANES, 9 * at % LANES
            slot = -(-(9 * lane - over) // LANES)
            back = 9 * lane - over - LANES * slot
            chunks = -(-(over + 9 * n) // LANES)
            segments.append(
                dict(n=n, block=block, lane=lane, first=first, slot=slot, back=back, chunks=chunks)
            )
            at += n
        blocks = 1 + max(b for _, b, _ in pieces)
        layers.append(
            dict(
                out=outgoing,
                row=row,
                chunks=-(-row // LANES),
                start=offset,
                dil=dilation,
                shift=shift,
                segments=segments,
                blocks=blocks,
                bias=offset + row * outgoing,
                shape=(LANES, blocks * LANES) if outgoing == 2 else (3 * LANES, 3 * blocks * LANES),
            )
        )
        offset += row * outgoing + outgoing

    for i, outgoing in enumerate(DENSE):
        add(places[i::-1], outgoing, 1, 64 if i == 4 else 0)
    add(places[::-1], 2, 1, 0)
    add(places[::-1], CONTEXT[0], DILATIONS[0], 0)
    for i in range(1, 7):
        add([(CONTEXT[i - 1], 0, 0)], CONTEXT[i], DILATIONS[i], 0)
    return layers, offset


LAYERS, COUNT = layer_table()
EARLY = (0, 1, 2, 3)
LATE = (4, 5, 6, 7, 8, 9, 10, 11, 12)
CUT = LAYERS[4]["start"] // LANES // 16 * 16


def sort_groups(indices):
    order = [(segment["back"], i, s) for i in indices for s, segment in enumerate(LAYERS[i]["segments"])]
    order.sort(key=lambda t: -t[0])
    at = 0
    groups = {}
    classes = []
    for back, i, s in order:
        if not classes or classes[-1][0] != back:
            classes.append([back, at, at])
        groups[i, s] = at
        at += -(-LAYERS[i]["out"] // 16) * 16
        classes[-1][2] = at
    return groups, classes, at


def iota(shape, dim):
    return lax.broadcasted_iota(jnp.int32, shape, dim)


def rows_at(start, size, step=8):
    if isinstance(start, int):
        return pl.ds(start, size)
    return pl.ds(pl.multiple_of(start, step), size)


def sigmoid(v):
    return 0.5 * jnp.tanh(0.5 * v) + 0.5


def leaky(v):
    return SLOPE * v + (1.0 - SLOPE) * v * sigmoid(v)


def leaky_slope(v):
    s = sigmoid(v)
    return SLOPE + (1.0 - SLOPE) * (s + v * s * (1.0 - s))


def loop(count, body):
    def step(i, carry):
        body(i)
        return carry

    lax.fori_loop(0, count, step, 0)


def fill_order(order):
    order[:LANES, :] = jnp.zeros((LANES, 9 * LANES), BF16)
    order[10 * LANES :, :] = jnp.zeros((LANES, 9 * LANES), BF16)
    for k in range(9):
        for m in range(9):
            row = iota((LANES, LANES), 0) + m * LANES
            col = iota((LANES, LANES), 1)
            order[(m + 1) * LANES : (m + 2) * LANES, k * LANES : (k + 1) * LANES] = jnp.where(
                row == 9 * col + k, 1.0, 0.0
            ).astype(BF16)


ORDER = pltpu.VMEM((11 * LANES, 9 * LANES), BF16)


def within(n, lane):
    spot = iota((1, LANES), 1)
    return jnp.where((spot >= lane) & (spot < lane + n), 1.0, 0.0).astype(BF16)


def pitch_of(chunks):
    return -(-chunks // 8) * 8


def unpack_scratch(indices, count):
    _, _, group_rows = sort_groups(indices)
    return (
        pltpu.VMEM((count + 64, LANES), F32),
        pltpu.VMEM((48 * LANES, LANES), F32),
        pltpu.VMEM((group_rows, 10 * LANES), BF16),
        pltpu.VMEM((group_rows, 9 * LANES), BF16),
        pltpu.VMEM((LANES, 5 * LANES), F32),
    )


def unpack_weights(indices, base, place_at, parts, carried, outs, bias_out, carry_out, order, scratch):
    whole, slabs, aligned, result, heads = scratch
    count = whole.shape[0] - 64
    groups, classes, _ = sort_groups(indices)
    if base:
        whole[: carried.shape[0], :] = carried[...].astype(F32)
    for at_part, pieces in enumerate(parts):
        for j, piece in enumerate(pieces):
            size = piece.shape[0]
            to = place_at[at_part, j] - base

            def widen(i, piece=piece, to=to):
                whole[pl.ds(to + i * 16, 16), :] = piece[rows_at(i * 16, 16, 16), :].astype(F32)

            lax.fori_loop(0, size // 16, lambda i, c: (widen(i), c)[1], 0, unroll=8)
    whole[count:, :] = jnp.zeros((64, LANES), F32)
    if not base:
        carry_out[...] = whole[CUT:count, :].astype(BF16)
    bias_out[...] = jnp.zeros_like(bias_out)

    for at_out, index in enumerate(indices):
        layer = LAYERS[index]
        outgoing = layer["out"]
        kept = -(-outgoing // 16) * 16
        start = layer["start"] - base * LANES
        spot = iota((kept, LANES), 1)
        pitch = pitch_of(layer["chunks"] + 1)
        still = layer["row"] % LANES == 0
        if not still:
            unroll = min(32, outgoing)

            def take(i, unroll=unroll, row=layer["row"], start=start, pitch=pitch):
                for u in range(unroll):
                    o = i * unroll + u
                    first = start + o * row
                    turn = (LANES - (first & (LANES - 1))) & (LANES - 1)
                    for v in range(pitch // 8):
                        tile = whole[pl.ds((first >> 7) + 8 * v, 8), :]
                        slabs[rows_at(o * pitch + 8 * v, 8), :] = pltpu.roll(tile, turn, 1)

            for i in range(outgoing // unroll):
                take(i)
            off = (start + iota((kept, LANES), 0) * layer["row"]) & (LANES - 1)
        chunks = {}
        for t in range(layer["chunks"]):
            if still:
                row, fixed = divmod(start, LANES)
                step = layer["row"] // LANES
                here = whole[pl.ds(row + t, kept, stride=step), :]
                after = whole[pl.ds(row + t + 1, kept, stride=step), :]
                chunk = jnp.where(spot >= fixed, here, after)
                chunk = pltpu.roll(chunk, (LANES - fixed) % LANES, 1)
            else:
                here = slabs[pl.ds(t, kept, stride=pitch), :]
                after = slabs[pl.ds(t + 1, kept, stride=pitch), :]
                chunk = jnp.where(spot < LANES - off, here, after)
            chunk = chunk.astype(BF16)
            for s, segment in enumerate(layer["segments"]):
                to = t - segment["first"]
                if 0 <= to < segment["chunks"]:
                    to += segment["slot"]
                    at = groups[index, s]
                    aligned[at : at + kept, to * LANES : (to + 1) * LANES] = chunk
        for s, segment in enumerate(layer["segments"]):
            at = groups[index, s]
            for to in range(10):
                if not segment["slot"] <= to < segment["slot"] + segment["chunks"]:
                    aligned[at : at + kept, to * LANES : (to + 1) * LANES] = jnp.zeros(
                        (kept, LANES), BF16
                    )
        shift = layer["shift"]
        first = layer["bias"] - base * LANES - shift
        row, fixed = divmod(first, LANES)
        here = pltpu.roll(whole[row : row + 1, :], (LANES - fixed) % LANES, 1)
        after = pltpu.roll(whole[row + 1 : row + 2, :], (LANES - fixed) % LANES, 1)
        line = iota((1, LANES), 1)
        value = jnp.where(line < LANES - fixed, here, after)
        bias_out[index : index + 1, :] = jnp.where(
            (line >= shift) & (line < shift + outgoing), value, 0.0
        )

    for back, low, high in classes:
        wide = 9 if back == 0 else 10
        result[low:high, :] = jnp.dot(
            aligned[low:high, : wide * LANES],
            order[LANES + back : LANES + back + wide * LANES, :],
            preferred_element_type=F32,
        ).astype(BF16)

    for at_out, index in enumerate(indices):
        layer = LAYERS[index]
        outgoing = layer["out"]
        shift = layer["shift"]
        out = outs[at_out]
        width = layer["blocks"] * LANES
        if outgoing == 2:
            heads[...] = jnp.zeros_like(heads)
        elif outgoing < LANES:
            out[...] = jnp.zeros_like(out)
        kept = -(-outgoing // 16) * 16
        for block in range(layer["blocks"]):
            for k in range(9):
                total = None
                for s, segment in enumerate(layer["segments"]):
                    if segment["block"] != block:
                        continue
                    at = groups[index, s]
                    tile = result[at : at + kept, k * LANES : (k + 1) * LANES]
                    if segment["n"] < LANES:
                        tile = tile * within(segment["n"], segment["lane"])
                    total = tile if total is None else total + tile
                if outgoing == 2:
                    heads[2 * k : 2 * k + 2, block * LANES : (block + 1) * LANES] = total.astype(
                        F32
                    )[:2]
                else:
                    ky, kx = divmod(k, 3)
                    at = kx * width + block * LANES
                    out[ky * LANES + shift : ky * LANES + shift + outgoing, at : at + LANES] = total
        if outgoing == 2:
            out[...] = heads[:, :width].astype(BF16)


def pack_scratch(indices, count):
    _, _, group_rows = sort_groups(indices)
    return (
        pltpu.VMEM((count + 64, LANES), F32),
        pltpu.VMEM((40 * LANES + 64, LANES), F32),
        pltpu.VMEM((group_rows, 9 * LANES), BF16),
        pltpu.VMEM((group_rows, 10 * LANES), F32),
        pltpu.VMEM((LANES + 16, 5 * LANES), F32),
    )


def pack_gradients(indices, base, place_at, grads, bias_in, carried, halves, carry_out, order, scratch):
    whole, slabs, gathered, result, heads = scratch
    count = whole.shape[0] - 64
    groups, classes, _ = sort_groups(indices)
    for at_in, index in enumerate(indices):
        layer = LAYERS[index]
        outgoing = layer["out"]
        shift = layer["shift"]
        grad = grads[at_in]
        width = layer["blocks"] * LANES
        if outgoing == 2:
            heads[:LANES, :width] = grad[...].astype(F32)
            heads[LANES:, :] = jnp.zeros((16, heads.shape[1]), F32)
        for s, segment in enumerate(layer["segments"]):
            at = groups[index, s]
            block = segment["block"]
            for k in range(9):
                if outgoing == 2:
                    tile = heads[2 * k : 2 * k + 16, block * LANES : (block + 1) * LANES]
                    tile = tile.astype(BF16)
                else:
                    ky, kx = divmod(k, 3)
                    column = kx * width + block * LANES
                    tile = grad[
                        ky * LANES + shift : ky * LANES + shift + outgoing, column : column + LANES
                    ]
                if segment["n"] < LANES:
                    tile = tile * within(segment["n"], segment["lane"])
                gathered[at : at + tile.shape[0], k * LANES : (k + 1) * LANES] = tile

    for back, low, high in classes:
        wide = 9 if back == 0 else 10
        result[low:high, : wide * LANES] = lax.dot_general(
            gathered[low:high, :],
            order[LANES + back : LANES + back + wide * LANES, :],
            NT,
            preferred_element_type=F32,
        )

    lane = iota((8, LANES), 1)
    sub = iota((8, LANES), 0)

    for at_in, index in enumerate(indices):
        layer = LAYERS[index]
        outgoing = layer["out"]
        start = layer["start"] - base * LANES
        still = layer["row"] % LANES == 0
        pitch = pitch_of(layer["chunks"])
        spot = iota((outgoing, LANES), 1)
        turned = []
        for t in range(layer["chunks"]):
            chunk = None
            for s, segment in enumerate(layer["segments"]):
                to = t - segment["first"]
                if 0 <= to < segment["chunks"]:
                    to += segment["slot"]
                    at = groups[index, s]
                    tile = result[at : at + outgoing, to * LANES : (to + 1) * LANES]
                    chunk = tile if chunk is None else chunk + tile
            if still:
                turned.append(pltpu.roll(chunk, start % LANES, 1))
            else:
                slabs[pl.ds(t, outgoing, stride=pitch), :] = chunk
        if still:
            row, fixed = divmod(start, LANES)
            step = layer["row"] // LANES
            for t in range(step):
                before = turned[t - 1] if t else pltpu.roll(turned[-1], 1, 0)
                value = jnp.where(spot >= fixed, turned[t], before)
                if t == 0:
                    kept = whole[row : row + 1, :]
                    top = (iota((outgoing, LANES), 0) == 0) & (spot < fixed)
                    value = jnp.where(top, kept, value)
                whole[pl.ds(row + t, outgoing, stride=step), :] = value
            last = pltpu.roll(turned[-1][outgoing - 8 :, :], 1, 0)
            end = row + step * outgoing
            pltpu.store(whole.at[end : end + 8, :], last, mask=(sub == 0) & (lane < fixed))
        else:
            unroll = min(32, outgoing)

            def put(i, start=start, row=layer["row"], pitch=pitch, unroll=unroll):
                for u in range(unroll):
                    o = i * unroll + u
                    first = start + o * row
                    off = first & (LANES - 1)
                    for v in range(pitch // 8):
                        tile = pltpu.roll(slabs[rows_at(o * pitch + 8 * v, 8), :], off, 1)
                        to = (first >> 7) + 8 * v
                        pltpu.store(whole.at[pl.ds(to, 8), :], tile, mask=lane >= off)
                        pltpu.store(whole.at[pl.ds(to + 1, 8), :], tile, mask=lane < off)

            for i in range(outgoing // unroll):
                put(i)
        line = bias_in[index : index + 1, :]
        first = layer["bias"] - base * LANES
        row, fixed = divmod(first, LANES)
        line = pltpu.roll(line, (fixed - layer["shift"]) % LANES, 1)
        line = jnp.broadcast_to(line, (8, LANES))
        pltpu.store(whole.at[row : row + 8, :], line, mask=(sub == 0) & (lane >= fixed))
        pltpu.store(whole.at[row + 1 : row + 9, :], line, mask=(sub == 0) & (lane < fixed))
    if base:
        end, off = divmod(COUNT - base * LANES, LANES)
        pltpu.store(
            whole.at[end : end + 8, :], jnp.zeros((8, LANES), F32), mask=(sub > 0) | (lane >= off)
        )
        if count > end + 8:
            whole[end + 8 : count, :] = jnp.zeros((count - end - 8, LANES), F32)
        carry_out[...] = whole[: carry_out.shape[0], :].astype(BF16)
    else:
        end, off = divmod(LAYERS[4]["start"], LANES)
        line = carried[...].astype(F32)
        keep = (iota(line.shape, 0) > end - CUT) | (
            (iota(line.shape, 0) == end - CUT) & (iota(line.shape, 1) >= off)
        )
        whole[CUT:count, :] = jnp.where(keep, line, whole[CUT:count, :])
    for half in range(2):
        size = halves[half].shape[1]
        for j in range(halves[half].shape[0]):
            begin = place_at[half, j] - base

            def narrow(i, half=half, j=j, begin=begin):
                halves[half][j, rows_at(i * 16, 16, 16), :] = whole[
                    pl.ds(begin + i * 16, 16), :
                ].astype(BF16)

            lax.fori_loop(0, size // 16, lambda i, c: (narrow(i), c)[1], 0, unroll=8)


ROWS4 = 4 * PW
SEC_ROWS = (PH + 2 * SR) * PITCH + LANES


def load_second(joined, second):
    second[...] = jnp.zeros_like(second)
    keep = iota((PW, LANES), 1) < FC
    for y in range(MARGIN, PH - MARGIN):
        row = joined[y * PW : (y + 1) * PW, :].astype(F32)
        row = jnp.where(keep, pltpu.roll(row, LANES - FC, 1), 0.0)
        at = (y + SR) * PITCH + 8
        second[at : at + PW, :] = row


def start_copies(sources, targets, semaphores):
    copies = [
        pltpu.make_async_copy(source, target, semaphores.at[i])
        for i, (source, target) in enumerate(zip(sources, targets))
    ]
    for copy in copies:
        copy.start()
    return copies


def windows_kernel(*refs):
    out = refs[4]
    features, coarse, target, mask = refs[5:9]
    for copy in start_copies(refs[:4], refs[5:9], refs[9]):
        copy.wait()
    own_rows, width = mask.shape[1:]
    devices = out.shape[0]
    breadth = width // devices
    side = jnp.zeros((CHANNELS - 1, MARGIN), F32)
    arrays = [features[0].astype(F32), coarse[0].astype(F32), target[0].astype(F32)]
    marks = mask[0].astype(F32)
    for r in range(own_rows):
        valid = marks[r : r + 1, :]
        tall = jnp.concatenate([a[:, r, :] for a in arrays] + [valid], axis=0)
        tall = jnp.concatenate([side, tall, side], axis=1)
        count = sum(valid[:, at : at + PW] for at in range(0, width, PW))
        for t in range(devices):
            tile = jnp.concatenate([tall[:, t * breadth : t * breadth + PW], count], axis=0)
            out[t, :, r * PW : (r + 1) * PW] = tile.astype(BF16)


def windows(features, coarse, target, mask, devices):
    return pl.pallas_call(
        windows_kernel,
        out_shape=jax.ShapeDtypeStruct((devices, CHANNELS, mask.shape[1] * PW), BF16),
        in_specs=[pl.BlockSpec(memory_space=pltpu.HBM)] * 4,
        scratch_shapes=[pltpu.VMEM(a.shape, a.dtype) for a in (features, coarse, target, mask)]
        + [pltpu.SemaphoreType.DMA((4,))],
        compiler_params=pltpu.CompilerParams(vmem_limit_bytes=60 * 2**20),
        name="windows",
    )(features, coarse, target, mask)


def band_shift(dy, third):
    return EXT * dy - PITCH * third - (8 - SR)


def correlate_kernel(received, stack0, cost_out, joined_out, second, cost, joined, copied):
    joined[...] = jnp.zeros_like(joined)
    blocks = received.shape[0]
    spare = jnp.zeros((LANES - received.shape[1], LANES), F32)
    for s in range(blocks):
        tile = received[s].astype(F32)
        tile = jnp.concatenate([tile, spare], axis=0).T
        joined[RIM // 2 + s * ROWS4 : RIM // 2 + (s + 1) * ROWS4, :] = tile.astype(BF16)
    copies = start_copies([joined], [joined_out], copied)
    load_second(joined, second)
    row = iota((ROWS4, ROWS4), 0)
    col = iota((ROWS4, ROWS4), 1)
    flip = jnp.where((row // PW == col // PW) & (row % PW + col % PW == PW - 1), 1.0, 0.0).astype(
        BF16
    )
    lane = iota((ROWS4, LANES), 1)
    narrow = iota((PW, LANES), 1)

    def body(i):
        own = joined[rows_at(i * ROWS4, ROWS4, ROWS4), :]
        first = jnp.where(lane < FC, own.astype(F32), 0.0).astype(BF16)
        first = jnp.dot(flip, first, preferred_element_type=F32).astype(BF16)
        bands = []
        for g in range(4):
            window = second[rows_at((4 * i + 3 * g) * PITCH, LANES), :].astype(BF16)
            bands.append(lax.dot_general(first, window, NT, preferred_element_type=F32))
        pieces = []
        for yy in range(4):
            total = jnp.zeros((PW, LANES), F32)
            turned = [
                pltpu.roll(band[yy * PW : (yy + 1) * PW, :], 0, 1, stride=1, stride_axis=0)
                for band in bands
            ]
            for dy in range(EXT):
                t = yy + dy
                shift = (band_shift(dy, t % 3) - (PW - 1)) % LANES
                band = pltpu.roll(turned[t // 3], shift, 1)
                total = jnp.where((narrow >= EXT * dy) & (narrow < EXT * (dy + 1)), band, total)
            pieces.append(total * (1.0 / FC))
        total = jnp.concatenate(pieces, axis=0)
        high = total.astype(BF16)
        low = (total - high.astype(F32)).astype(BF16)
        total = jnp.dot(flip, high, preferred_element_type=F32) + jnp.dot(
            flip, low, preferred_element_type=F32
        )
        cost[rows_at(i * ROWS4, ROWS4, ROWS4), :] = total
        wide = own.astype(F32)
        filled = jnp.where(lane < NCOST, leaky(total), pltpu.roll(wide, NCOST, 1))
        coarse = pltpu.roll(wide, NCOST + FC - 2 * FC, 1)
        filled = jnp.where(lane >= NCOST + FC, coarse, filled)
        filled = jnp.where(lane < NS0, filled, 0.0)
        stack0[rows_at(i * ROWS4, ROWS4, ROWS4), :] = filled.astype(BF16)

    for i in range(PH // 4):
        body(i)
    copies.append(pltpu.make_async_copy(cost, cost_out, copied.at[1]))
    copies[1].start()
    for copy in copies:
        copy.wait()


def correlate(received):
    vmem = pl.BlockSpec(memory_space=pltpu.VMEM)
    anywhere = pl.BlockSpec(memory_space=pltpu.HBM)
    return pl.pallas_call(
        correlate_kernel,
        out_shape=[
            jax.ShapeDtypeStruct((PX, LANES), BF16),
            jax.ShapeDtypeStruct((PX, LANES), F32),
            jax.ShapeDtypeStruct((PX, LANES), BF16),
        ],
        out_specs=[vmem, anywhere, anywhere],
        scratch_shapes=[
            pltpu.VMEM((SEC_ROWS, LANES), F32),
            pltpu.VMEM((PX, LANES), F32),
            pltpu.VMEM((PX, LANES), BF16),
            pltpu.SemaphoreType.DMA((2,)),
        ],
        compiler_params=pltpu.CompilerParams(vmem_limit_bytes=60 * 2**20),
        cost_estimate=pl.CostEstimate(
            flops=8_000_000_000, bytes_accessed=2_000_000, transcendentals=0
        ),
        name="correlate",
    )(received)


class Work:
    def __init__(self, taps, moved, partial):
        self.taps = taps
        self.moved = moved
        self.partial = partial
        self.column = iota((STRIP, LANES), 0) % PW
        self.lane = iota((STRIP, LANES), 1)
        if taps is not None:
            taps[:, :RIM, :] = jnp.zeros((3, RIM, LANES), F32)
            taps[:, RIM + PX :, :] = jnp.zeros((3, RIM, LANES), F32)
        if moved is not None:
            moved[:, :RIM, :] = jnp.zeros((3, RIM, LANES), BF16)
            moved[:, RIM + PX :, :] = jnp.zeros((3, RIM, LANES), BF16)

    def strips(self, body):
        for at in range(0, PX, STRIP):
            body(pl.ds(at, STRIP), at)

    def inside(self, tile, shift):
        if shift == 0:
            return tile
        valid = (self.column + shift >= 0) & (self.column + shift < PW)
        return jnp.where(valid, pltpu.roll(tile, (-shift) % STRIP, 0), 0.0)

    def spread(self, store, tile, dilation):
        for kx in range(3):
            store(kx, self.inside(tile, (kx - 1) * dilation).astype(BF16))

    def multiply(self, load, kernel):
        def body(i):
            rows = rows_at(i * MT, MT, MT)
            value = jnp.concatenate([load(kx, rows) for kx in range(3)], axis=1)
            product = lax.dot_general(value, kernel[...], NT, preferred_element_type=F32)
            for ky in range(3):
                self.taps[ky, rows_at(RIM + i * MT, MT, MT), :] = product[
                    :, ky * LANES : (ky + 1) * LANES
                ]

        for i in range(PX // MT):
            body(i)

    def collect(self, at, dilation):
        total = None
        for ky in range(3):
            tile = self.taps[ky, rows_at(RIM + at + (ky - 1) * dilation * PW, STRIP, PW), :]
            total = tile if total is None else total + tile
        return total

    def spread_grad(self, at, grad, dilation):
        for kx in range(3):
            self.moved[kx, rows_at(RIM + at, STRIP, STRIP), :] = self.inside(
                grad, -(kx - 1) * dilation
            ).astype(BF16)

    def count_bias(self, index, grad):
        self.partial[index] += grad.reshape(STRIP // 8, 8, LANES).sum(0)

    def back(self, index, load_grad, load_pre, load_input, kernel, out, store, waits=()):
        layer = LAYERS[index]
        dilation = layer["dil"]
        width = layer["blocks"] * LANES

        def through(rows, at):
            grad = load_grad(rows) * leaky_slope(load_pre(rows))
            grad = grad.astype(BF16).astype(F32)
            self.count_bias(index, grad)
            self.spread_grad(at, grad, dilation)

        self.strips(through)
        for load in waits:
            load.wait()
        grad = jnp.concatenate(
            [
                self.moved[1, RIM - (ky - 1) * dilation * PW : RIM - (ky - 1) * dilation * PW + PX, :]
                for ky in range(3)
            ],
            axis=1,
        )
        values = [load_input(kx) for kx in range(3)]
        if index in LATE:
            values = [jnp.concatenate(values, axis=1)]
        for i, value in enumerate(values):
            out[:, i * value.shape[1] : (i + 1) * value.shape[1]] = lax.dot_general(
                grad, value, TN, preferred_element_type=F32
            ).astype(BF16)

        def input_grad(i):
            tiles = [
                self.moved[kx, rows_at(RIM + i * MT - (ky - 1) * dilation * PW, MT, PW), :]
                for ky in range(3)
                for kx in range(3)
            ]
            weights = [
                kernel[ky * LANES : (ky + 1) * LANES, kx * width : (kx + 1) * width]
                for ky in range(3)
                for kx in range(3)
            ]
            store(
                rows_at(i * MT, MT, MT),
                jnp.dot(
                    jnp.concatenate(tiles, axis=1),
                    jnp.concatenate(weights, axis=0),
                    preferred_element_type=F32,
                ),
            )

        for i in range(PX // MT):
            input_grad(i)


def forward_kernel(half, place_at, stack0, *refs):
    own, other, refs = refs[:half], refs[half : 2 * half], refs[2 * half :]
    kernels_out, carry_out, (stack_out, top_out, pre_out) = refs[:4], refs[4], refs[5:8]
    kernels, refs = refs[8:12], refs[12:]
    stack, top, pre, biases, order, taps, copied = refs[:7]
    held = refs[12 : 12 + 2 * half]
    arrivals = start_copies((*own, *other), held, refs[-1])
    fill_order(order)
    for arrival in arrivals:
        arrival.wait()
    parts = (held[:half], held[half:])
    unpack_weights(
        EARLY, 0, place_at, parts, None, kernels, biases, carry_out, order, refs[7:12]
    )
    copies = start_copies(kernels, kernels_out, copied)
    work = Work(taps, None, None)

    def send(source, target):
        copies.append(pltpu.make_async_copy(source, target, copied.at[len(copies)]))
        copies[-1].start()

    def first(rows, at):
        tile = stack0[rows, :].astype(F32)

        def keep(kx, value):
            stack[kx, rows, :LANES] = value

        work.spread(keep, tile, 1)

    work.strips(first)
    send(stack.at[:, :, :LANES], stack_out.at[:, :, :LANES])
    for index, kernel in enumerate(kernels):
        width = LAYERS[index]["blocks"] * LANES
        work.multiply(lambda kx, rows, width=width: stack[kx, rows, :width], kernel)

        place = slice((index + 1) * LANES, (index + 2) * LANES)

        def finish(rows, at, index=index, place=place):
            value = work.collect(at, 1) + biases[index : index + 1, :]
            pre[index, rows, :] = value

            def keep(kx, value):
                if index == 3:
                    top[kx, rows, :] = value
                else:
                    stack[kx, rows, place] = value

            work.spread(keep, leaky(value), 1)

        work.strips(finish)
        send(pre.at[index], pre_out.at[index])
        if index == 3:
            send(top, top_out)
        else:
            send(stack.at[:, :, place], stack_out.at[:, :, place])
    for copy in copies:
        copy.wait()


def forward(place_at, parts, stack0, count):
    vmem = pl.BlockSpec(memory_space=pltpu.VMEM)
    anywhere = pl.BlockSpec(memory_space=pltpu.HBM)
    kernels = [(LAYERS[i]["shape"], BF16) for i in EARLY]
    states = [((3, PX, 4 * LANES), BF16), ((3, PX, LANES), BF16), ((4, PX, LANES), F32)]
    outs = pl.pallas_call(
        functools.partial(forward_kernel, len(parts[0])),
        out_shape=[
            jax.ShapeDtypeStruct(*a) for a in (*kernels, ((count - CUT, LANES), BF16), *states)
        ],
        in_specs=[pl.BlockSpec(memory_space=pltpu.SMEM), vmem] + [anywhere] * (2 * len(parts[0])),
        out_specs=[anywhere] * 4 + [vmem] + [anywhere] * 3,
        scratch_shapes=[
            *[pltpu.VMEM(*a) for a in (*kernels, *states)],
            pltpu.VMEM((16, LANES), F32),
            ORDER,
            pltpu.VMEM((3, PX + 2 * RIM, LANES), F32),
            pltpu.SemaphoreType.DMA((13,)),
            *unpack_scratch(EARLY, count),
            *[pltpu.VMEM(p.shape, BF16) for p in (*parts[0], *parts[1])],
            pltpu.SemaphoreType.DMA((2 * len(parts[0]),)),
        ],
        compiler_params=pltpu.CompilerParams(vmem_limit_bytes=60 * 2**20),
        cost_estimate=pl.CostEstimate(
            flops=25_000_000_000, bytes_accessed=20_000_000, transcendentals=0
        ),
        name="dense_forward",
    )(place_at, stack0, *parts[0], *parts[1])
    return outs[:4], *outs[4:]


def late_kernel(
    rows,
    half,
    groups,
    pixels,
    gather_at,
    pack_at,
    carried,
    stack_in,
    below_in,
    joined_in,
    *refs,
):
    counts, refs = refs[:groups], refs[groups:]
    own, other, refs = refs[:half], refs[half : 2 * half], refs[2 * half :]
    motion_out, dstack_out, bias_out, keep, send, carry_out = refs[:6]
    order, biases, dstack, stack, below, joined, copied = refs[6:13]
    refs = refs[13:]
    kernels = refs[:9]
    grads = refs[9:18]
    held = refs[18 : 18 + 2 * half]
    arrivals = start_copies((*own, *other), held, refs[-1])
    loads = [
        pltpu.make_async_copy(source, target, copied.at[i])
        for i, (source, target) in enumerate(zip((stack_in, below_in, joined_in), (stack, below, joined)))
    ]
    for load in loads:
        load.start()
    fill_order(order)
    for arrival in arrivals:
        arrival.wait()

    def first(*scratch):
        unpack_weights(
            LATE, CUT, gather_at, (held[:half], held[half:]), carried, kernels, biases, None, order, scratch
        )

    pl.run_scoped(first, *unpack_scratch(LATE, rows))
    for load in loads:
        load.wait()

    weighting = pixels / sum(count[:1, :] for count in counts)

    def second(*scratch):
        context(
            stack, below, joined, weighting, biases, kernels, motion_out, dstack, bias_out, grads, *scratch
        )

    pl.run_scoped(second, *CONTEXT_SCRATCH)
    store = pltpu.make_async_copy(dstack, dstack_out, copied.at[3])
    store.start()

    def third(*scratch):
        pack_gradients(
            LATE, CUT, pack_at, grads, bias_out, None, (keep, send), carry_out, order, scratch
        )

    pl.run_scoped(third, *pack_scratch(LATE, rows))
    store.wait()


def context(
    stack, below, joined, weighting, biases, kernels, motion_out, dstack, bias_out, grads, *scratch
):
    kernels = dict(zip(LATE, kernels))
    grads = dict(zip(LATE, grads))
    top, ctx, pre, taps, moved, dcur, ghead, partial = scratch
    work = Work(taps, moved, partial)
    partial[...] = jnp.zeros_like(partial)
    lane = work.lane

    def wide(kx, rows):
        return jnp.concatenate([stack[kx, rows, :], top[kx, rows, :]], axis=1)

    work.multiply(
        lambda kx, rows: jnp.concatenate([stack[kx, rows, :], below[kx, rows, :]], axis=1),
        kernels[4],
    )

    def finish_top(rows, at):
        value = work.collect(at, 1) + biases[4:5, :]
        pre[0, rows, :] = value

        def keep(kx, value):
            top[kx, rows, :] = value + below[kx, rows, :]

        work.spread(keep, leaky(value), 1)

    work.strips(finish_top)
    for index in range(6, 12):
        if index == 6:
            work.multiply(wide, kernels[index])
        else:
            work.multiply(lambda kx, rows, index=index: ctx[index - 7, kx, rows, :], kernels[index])

        def finish(rows, at, index=index):
            value = work.collect(at, LAYERS[index]["dil"]) + biases[index : index + 1, :]
            pre[index - 5, rows, :] = value

            def keep(kx, value):
                ctx[index - 6, kx, rows, :] = value

            work.spread(keep, leaky(value), LAYERS[index + 1]["dil"])

        work.strips(finish)

    def head(i):
        rows = rows_at(i * MT, MT, MT)
        product = lax.dot_general(wide(1, rows), kernels[5][...], NT, preferred_element_type=F32)
        product = product + lax.dot_general(
            ctx[5, 1, rows, :], kernels[12][...], NT, preferred_element_type=F32
        )
        taps[0, rows_at(RIM + i * MT, MT, MT), :] = product

    for i in range(PX // MT):
        head(i)

    row = iota((LANES, LANES), 0)
    col = iota((LANES, LANES), 1)
    used = (col < 18) & (row % 2 == col % 2)
    fold = jnp.where(used & (row < 18), 1.0, 0.0)
    copies = jnp.where(used & (row < 2), 1.0, 0.0).astype(BF16)
    pick = jnp.where(used & (row >= 2 * FC + 4) & (row < 2 * FC + 6), 1.0, 0.0).astype(BF16)
    marked = jnp.where(row == 2 * FC + 6, 1.0, 0.0).astype(BF16)
    shared = sum(
        jnp.dot(jnp.broadcast_to(b, (8, LANES)).astype(BF16), copies, preferred_element_type=F32)
        for b in (biases[5:6, :], biases[12:13, :])
    )[:1]

    def settle(rows, at):
        total = None
        for kx in range(3):
            part = None
            for ky in range(3):
                tile = taps[0, rows_at(RIM + at + (ky - 1) * PW, STRIP, PW), :]
                tile = jnp.where(lane // 2 == ky * 3 + kx, tile, 0.0)
                part = tile if part is None else part + tile
            part = work.inside(part, kx - 1)
            total = part if total is None else total + part
        motion = (
            jnp.dot(total, fold, preferred_element_type=F32, precision=lax.Precision.HIGHEST)
            + shared
        )
        motion_out[:, rows] = motion.T[: motion_out.shape[0]]
        own = joined[rows, :]
        aim = jnp.dot(own, pick, preferred_element_type=F32)
        mask = jnp.dot(own, marked, preferred_element_type=F32)
        mismatch = motion - aim
        square = mismatch * mismatch
        other = jnp.where(
            lane % 2 == 0, pltpu.roll(square, LANES - 1, 1), pltpu.roll(square, 1, 1)
        )
        length = jnp.sqrt(square + other + EPE_EPS)
        height = (iota((STRIP, LANES), 0) + at) // PW
        interior = (
            (height >= MARGIN)
            & (height < PH - MARGIN)
            & (work.column >= MARGIN)
            & (work.column < PW - MARGIN)
            & (lane < 18)
        )
        grad = jnp.where(interior, weighting * mask * mismatch / length, 0.0)
        grad = grad.astype(BF16).astype(F32)
        work.count_bias(5, grad)
        work.spread_grad(at, grad, 1)

    work.strips(settle)
    partial[12] = partial[5]

    def choose(rows, at):
        total = None
        for kx in range(3):
            for ky in range(3):
                tile = moved[kx, rows_at(RIM + at - (ky - 1) * PW, STRIP, PW), :].astype(F32)
                tile = jnp.where(lane // 2 == ky * 3 + kx, tile, 0.0)
                total = tile if total is None else total + tile
        ghead[rows, :] = total.astype(BF16)

    work.strips(choose)
    grads[5][:, : 4 * LANES] = lax.dot_general(
        ghead[...], stack[1], TN, preferred_element_type=F32
    ).astype(BF16)
    grads[5][:, 4 * LANES :] = lax.dot_general(
        ghead[...], top[1], TN, preferred_element_type=F32
    ).astype(BF16)
    grads[12][...] = lax.dot_general(
        ghead[...], ctx[5, 1], TN, preferred_element_type=F32
    ).astype(BF16)

    def head_back(i):
        rows = rows_at(i * MT, MT, MT)
        dstack[rows, :] = jnp.dot(ghead[rows, :], kernels[5][...], preferred_element_type=F32)
        dcur[rows, :] = jnp.dot(ghead[rows, :], kernels[12][...], preferred_element_type=F32)

    for i in range(PX // MT):
        head_back(i)

    def store_current(rows, value):
        dcur[rows, :] = value

    def store_stack(rows, value):
        dstack[rows, :] += value

    for index in range(11, 6, -1):
        work.back(
            index,
            lambda rows: dcur[rows, :],
            lambda rows, index=index: pre[index - 5, rows, :],
            lambda kx, index=index: ctx[index - 7, kx],
            kernels[index],
            grads[index],
            store_current,
        )
    work.back(
        6,
        lambda rows: dcur[rows, :],
        lambda rows: pre[1, rows, :],
        lambda kx: jnp.concatenate([stack[kx], top[kx]], axis=1),
        kernels[6],
        grads[6],
        store_stack,
    )
    work.back(
        4,
        lambda rows: dstack[rows, 4 * LANES :],
        lambda rows: pre[0, rows, :],
        lambda kx: jnp.concatenate([stack[kx], top[kx]], axis=1),
        kernels[4],
        grads[4],
        store_stack,
    )
    bias_out[...] = partial[...].sum(1)


CONTEXT_SCRATCH = (
    pltpu.VMEM((3, PX, LANES), BF16),
    pltpu.VMEM((6, 3, PX, LANES), BF16),
    pltpu.VMEM((7, PX, LANES), F32),
    pltpu.VMEM((3, PX + 2 * RIM, LANES), F32),
    pltpu.VMEM((3, PX + 2 * RIM, LANES), BF16),
    pltpu.VMEM((PX, LANES), F32),
    pltpu.VMEM((PX, LANES), BF16),
    pltpu.VMEM((16, 8, LANES), F32),
)


def late(gather_at, pack_at, parts, carried, stack, below, joined, counts, pixels, end, pieces, size):
    smem = pl.BlockSpec(memory_space=pltpu.SMEM)
    vmem = pl.BlockSpec(memory_space=pltpu.VMEM)
    anywhere = pl.BlockSpec(memory_space=pltpu.HBM)
    shapes = [pltpu.VMEM(LAYERS[i]["shape"], BF16) for i in LATE]
    return pl.pallas_call(
        functools.partial(late_kernel, end - CUT, len(parts[0]), len(counts), float(pixels)),
        out_shape=[
            jax.ShapeDtypeStruct((8, PX), F32),
            jax.ShapeDtypeStruct((PX, 5 * LANES), F32),
            jax.ShapeDtypeStruct((16, LANES), F32),
            jax.ShapeDtypeStruct((pieces, size, LANES), BF16),
            jax.ShapeDtypeStruct((pieces, size, LANES), BF16),
            jax.ShapeDtypeStruct((end // 2 - CUT, LANES), BF16),
        ],
        in_specs=[smem] * 2 + [vmem] + [anywhere] * 3 + [vmem] * len(counts) + [anywhere] * (2 * len(parts[0])),
        out_specs=[vmem, anywhere, vmem, vmem, vmem, vmem],
        scratch_shapes=[
            ORDER,
            pltpu.VMEM((16, LANES), F32),
            pltpu.VMEM((PX, 5 * LANES), F32),
            pltpu.VMEM(stack.shape, BF16),
            pltpu.VMEM(below.shape, BF16),
            pltpu.VMEM(joined.shape, BF16),
            pltpu.SemaphoreType.DMA((4,)),
            *shapes,
            *shapes,
            *[pltpu.VMEM(p.shape, BF16) for p in (*parts[0], *parts[1])],
            pltpu.SemaphoreType.DMA((2 * len(parts[0]),)),
        ],
        compiler_params=pltpu.CompilerParams(vmem_limit_bytes=60 * 2**20),
        cost_estimate=pl.CostEstimate(
            flops=80_000_000_000, bytes_accessed=20_000_000, transcendentals=0
        ),
        name="context",
    )(gather_at, pack_at, carried, stack, below, joined, *counts, *parts[0], *parts[1])


def correlate_back(joined, cost, grads, second, dsecond, collected, out):
    load_second(joined, second)
    dsecond[...] = jnp.zeros_like(dsecond)
    lane = iota((ROWS4, LANES), 1)
    narrow = iota((PW, LANES), 1)

    def body(i):
        rows = rows_at(i * ROWS4, ROWS4, ROWS4)
        own = joined[rows, :]
        first = jnp.where(lane < FC, own.astype(F32), 0.0).astype(BF16)
        grad = grads[rows, :LANES]
        volume = grad * leaky_slope(cost[rows, :]) * (1.0 / FC)
        dfirst = jnp.zeros((ROWS4, LANES), F32)
        for g in range(4):
            pieces = []
            for yy in range(4):
                piece = jnp.zeros((PW, LANES), F32)
                own_rows = volume[yy * PW : (yy + 1) * PW, :]
                for t in range(3 * g, 3 * g + 3):
                    dy = t - yy
                    if dy < 0 or dy >= EXT:
                        continue
                    part = jnp.where(
                        (narrow >= EXT * dy) & (narrow < EXT * (dy + 1)), own_rows, 0.0
                    )
                    shift = (-band_shift(dy, t % 3)) % LANES
                    piece = piece + pltpu.roll(part, shift, 1)
                pieces.append(pltpu.roll(piece, 0, 1, stride=1, stride_axis=0))
            band = jnp.concatenate(pieces, axis=0).astype(BF16)
            at = rows_at((4 * i + 3 * g) * PITCH, LANES)
            dfirst = dfirst + jnp.dot(
                band, second[at, :].astype(BF16), preferred_element_type=F32
            )
            dsecond[at, :] += lax.dot_general(band, first, TN, preferred_element_type=F32)
        direct = pltpu.roll(grad, LANES - NCOST, 1)
        coarse = pltpu.roll(grad, LANES + 2 * FC - NCOST - FC, 1)
        filled = jnp.where(lane < FC, dfirst + direct, 0.0)
        filled = jnp.where((lane >= 2 * FC) & (lane < 2 * FC + 4), coarse, filled)
        collected[rows, :] = filled

    for i in range(PH // 4):
        body(i)
    for s in range((PH - 2 * MARGIN) // 4):
        pieces = []
        for yy in range(4):
            at = (MARGIN + 4 * s + yy + SR) * PITCH + 8
            pieces.append(dsecond[at : at + PW, :])
        other = pltpu.roll(jnp.concatenate(pieces, axis=0), FC, 1)
        start = (MARGIN + 4 * s) * PW
        tile = collected[start : start + ROWS4, :]
        tile = jnp.where((lane >= FC) & (lane < 2 * FC), other, tile)
        out[s] = tile.T[: out.shape[1]].astype(BF16)


def early_kernel(
    pack_at,
    stack_in,
    pre_in,
    dstack_in,
    cost_in,
    joined_in,
    bias_in,
    carried,
    k1,
    k2,
    k3,
    k4,
    picture_out,
    keep,
    send,
    order,
    stack,
    pre,
    dstack,
    cost,
    joined,
    bias_out,
    copied,
    *grads,
):
    sources = (dstack_in, pre_in, stack_in, cost_in, joined_in)
    targets = (dstack, pre, stack, cost, joined)
    loads = [
        pltpu.make_async_copy(source, target, copied.at[i])
        for i, (source, target) in enumerate(zip(sources, targets))
    ]
    for load in loads:
        load.start()
    fill_order(order)
    for load in loads[:2]:
        load.wait()

    def first(*scratch):
        dense_back(
            stack,
            pre,
            dstack,
            cost,
            joined,
            bias_in,
            (k1, k2, k3, k4),
            picture_out,
            bias_out,
            grads,
            loads[2:],
            *scratch,
        )

    pl.run_scoped(first, *DENSE_SCRATCH)

    def second(*scratch):
        pack_gradients(
            EARLY, 0, pack_at, grads, bias_out, carried, (keep, send), None, order, scratch
        )

    pl.run_scoped(second, *pack_scratch(EARLY, CUT + carried.shape[0]))


def dense_back(
    stack,
    pre,
    dstack,
    cost,
    joined,
    bias_in,
    kernels,
    picture_out,
    bias_out,
    grads,
    loads,
    moved,
    dwide,
    partial,
    second,
    dsecond,
    collected,
):
    work = Work(None, moved, partial)
    partial[...] = jnp.zeros_like(partial)
    dwide[...] = dstack[:, : 4 * LANES]

    def store_stack(rows, value):
        dwide[rows, : value.shape[1]] += value

    for index in range(3, -1, -1):
        width = LAYERS[index]["blocks"] * LANES

        def load_grad(rows, index=index):
            if index == 3:
                return dstack[rows, 4 * LANES :]
            return dwide[rows, (index + 1) * LANES : (index + 2) * LANES]

        work.back(
            index,
            load_grad,
            lambda rows, index=index: pre[index, rows, :],
            lambda kx, width=width: stack[kx, :, :width],
            kernels[index],
            grads[index],
            store_stack,
            loads if index == 3 else (),
        )
    bias_out[...] = partial[...].sum(1) + bias_in[...]
    correlate_back(joined, cost, dwide, second, dsecond, collected, picture_out)


DENSE_SCRATCH = (
    pltpu.VMEM((3, PX + 2 * RIM, LANES), BF16),
    pltpu.VMEM((PX, 4 * LANES), F32),
    pltpu.VMEM((16, 8, LANES), F32),
    pltpu.VMEM((SEC_ROWS, LANES), F32),
    pltpu.VMEM((SEC_ROWS, LANES), F32),
    pltpu.VMEM((PX, LANES), F32),
)


def backward(
    pack_at, stack, pre, dstack, cost, joined, bias_grads, carried, kernels, blocks, channels, pieces, size
):
    vmem = pl.BlockSpec(memory_space=pltpu.VMEM)
    large = (stack, pre, dstack, cost, joined)
    return pl.pallas_call(
        early_kernel,
        out_shape=[
            jax.ShapeDtypeStruct((blocks, channels, LANES), BF16),
            jax.ShapeDtypeStruct((pieces, size, LANES), BF16),
            jax.ShapeDtypeStruct((pieces, size, LANES), BF16),
        ],
        in_specs=[pl.BlockSpec(memory_space=pltpu.SMEM)]
        + [pl.BlockSpec(memory_space=pltpu.HBM)] * 5
        + [vmem] * 6,
        scratch_shapes=[
            ORDER,
            *[pltpu.VMEM(a.shape, a.dtype) for a in large],
            pltpu.VMEM((16, LANES), F32),
            pltpu.SemaphoreType.DMA((5,)),
            *[pltpu.VMEM(LAYERS[i]["shape"], BF16) for i in EARLY],
        ],
        compiler_params=pltpu.CompilerParams(vmem_limit_bytes=60 * 2**20),
        cost_estimate=pl.CostEstimate(
            flops=40_000_000_000, bytes_accessed=20_000_000, transcendentals=0
        ),
        name="dense_backward",
    )(pack_at, *large, bias_grads, carried, *kernels)


def update(weights, momentum, average, gradient):
    gradient = gradient + DECAY_RATE * weights
    renewed = MOMENTUM_RATE * momentum + gradient
    stepped = weights - LEARN_RATE * (gradient + MOMENTUM_RATE * renewed)
    return (stepped, renewed, AVERAGE_DECAY * average + (1.0 - AVERAGE_DECAY) * stepped)


def swapped(value, axis, step):
    count = lax.axis_size(axis)
    return lax.ppermute(value, axis, [(i, i ^ step) for i in range(count)])


def added(one, two):
    return (one.astype(F32) + two.astype(F32)).astype(BF16)


def core_sum(keep, send, groups, devices):
    got = swapped(send, "grp", 1)
    pieces = keep.shape[0] // 2
    if groups == 2:
        return [added(keep, got)]
    return [added(keep[pieces:], got[pieces:]), added(keep[:pieces], got[:pieces])]


def x_sum(value, groups, devices):
    half = devices // 2
    step = groups // 4
    if not step:
        value = value[0]
        return [value[j] for j in range(half)]
    away, value = value
    got = swapped(away, "grp", 2 * step)
    while step > 1:
        value = added(value, got)
        step //= 2
        pieces = value.shape[0] // 2
        got = swapped(value[pieces:], "grp", 2 * step)
        value = value[:pieces]
    return [added(value[j], got[j]) for j in range(half)]


def dev_sum(pieces):
    total = pieces[0].astype(F32)
    for j in range(1, len(pieces)):
        total = total + swapped(pieces[j], "dev", j).astype(F32)
    return total


def shared_parts(value, groups):
    x_size = groups // 2
    x = lax.axis_index("grp") // 2
    held = [0]
    parts = [value]
    step = 1
    while step < x_size:
        parts = parts + [swapped(p, "grp", 2 * step) for p in parts]
        held = held + [j ^ step for j in held]
        step *= 2

    def ordered(parts):
        out = []
        for i in range(x_size):
            piece = parts[0]
            for j, part in zip(held[1:], parts[1:]):
                piece = jnp.where((x ^ j) == i, part, piece)
            out.append(piece)
        return jnp.concatenate(out)

    return ordered(parts), ordered([swapped(p, "grp", 1) for p in parts])


def shards(features, coarse_flow, target, valid_mask, weights, momentum, average):
    groups = lax.axis_size("grp")
    devices = lax.axis_size("dev")
    own_rows = features.shape[2]
    width = features.shape[3]
    breadth = width // devices
    height = own_rows * devices
    assert breadth + 2 * MARGIN == PW and height + 2 * MARGIN == PH
    core = lax.axis_index("grp") % 2
    me = lax.axis_index("dev")
    half = devices // 2
    early = me < half
    rows = weights.shape[0] // LANES
    x_size = groups // 2
    size = -(-(rows // 2) // (16 * x_size)) * 16 * x_size
    table = weights.reshape(rows, LANES)
    own = lax.dynamic_slice(table, (core * (rows - size), 0), (size, LANES)).astype(BF16)

    received = windows(features, coarse_flow, target, valid_mask, devices)
    received = lax.all_to_all(received, "dev", split_axis=0, concat_axis=0, tiled=True)

    across = swapped(own, "dev", half)
    both = jnp.stack([core, 1 - core])[:, None] * (rows - size)
    steps = [half >> i for i in range(1, half.bit_length())]
    held = [0]
    for step in steps:
        held = held + [j ^ step for j in held]
    place = (jnp.array(held, jnp.int32) ^ (me % half))[None] * rows + both
    x = lax.axis_index("grp") // 2
    part_x = (jnp.arange(x_size, dtype=jnp.int32) ^ x) * (size // x_size)
    part_dev = (jnp.arange(half, dtype=jnp.int32) ^ (me % half)) * rows
    pack_at = (part_x[:, None] + part_dev[None]).reshape(1, -1) + both
    places = (place, place + half * rows, pack_at, pack_at + half * rows)
    across, received, *places = lax.optimization_barrier((across, received, *places))
    part, last = {0: jnp.where(early, own, across)}, {0: jnp.where(early, across, own)}
    other, other_last = {}, {}

    def grow(pieces, step):
        for j in list(pieces):
            if j ^ step not in pieces:
                pieces[j ^ step] = swapped(pieces[j], "dev", step)

    def swap_cores(pieces, others):
        for j in pieces:
            if j not in others:
                others[j] = swapped(pieces[j], "grp", 1)

    first_y = swapped(part[0], "dev", 1)
    swap_cores(part, other)
    for step in steps[:-1]:
        grow(part, step)
    counted = jnp.full((8, LANES), jnp.sum(received[:, CHANNELS - 1].astype(F32)))
    counts = [counted] + [swapped(counted, "grp", j) for j in range(1, groups)]
    keys = list(part)
    *tied, received, last[0] = lax.optimization_barrier(
        (*counts, *part.values(), received, last[0])
    )
    counts, part = tied[:groups], dict(zip(keys, tied[groups:]))
    swap_cores(part, other)
    swap_cores(last, other_last)
    part[1] = first_y
    grow(part, 1)
    for step in steps[:-1]:
        grow(last, step)
    per = 4 // own_rows
    blocks = devices // per
    received = received.reshape(blocks, per, CHANNELS, own_rows * PW)
    received = jnp.swapaxes(received, 1, 2).reshape(blocks, CHANNELS, LANES)
    stack0, cost, joined = correlate(received)
    keys, keys_last = list(part), list(last)
    *tied, stack0 = lax.optimization_barrier((*part.values(), *last.values(), stack0))
    part = dict(zip(keys, tied))
    last = dict(zip(keys_last, tied[len(keys) :]))
    swap_cores(part, other)
    grow(last, 1)
    parts = ([part[j] for j in held], [other[j] for j in held])
    kernels, carried, stack, below, pre = forward(places[0], parts, stack0, half * rows)
    keys_last = list(last)
    *tied, stack = lax.optimization_barrier((*last.values(), stack))
    last = dict(zip(keys_last, tied))
    swap_cores(last, other_last)
    parts = ([last[j] for j in held], [other_last[j] for j in held])
    pack_at, pack_late_at = places[2:]
    pieces = (half * x_size, size // x_size)
    motion, dstack, bias_grads, keep, send, carried = late(
        places[1],
        pack_late_at,
        parts,
        carried,
        stack,
        below,
        joined,
        counts,
        groups * height * width,
        devices * rows,
        *pieces,
    )
    flow = motion[:2].reshape(1, 2, PH, PW)[
        :, :, MARGIN : MARGIN + height, MARGIN : MARGIN + breadth
    ]
    late_sum = core_sum(keep, send, groups, devices)
    late_sum, dstack = lax.optimization_barrier((late_sum, dstack))
    late_sum = x_sum(late_sum, groups, devices)
    tiles, keep, send = backward(
        pack_at,
        stack,
        pre,
        dstack,
        cost,
        joined,
        bias_grads,
        carried,
        kernels,
        blocks,
        CHANNELS,
        *pieces,
    )
    late_sum, keep, send = lax.optimization_barrier((late_sum, keep, send))
    late_sum = dev_sum(late_sum)
    early_sum = core_sum(keep, send, groups, devices)
    tiles = tiles.reshape(blocks, CHANNELS, per, own_rows * PW)
    tiles = jnp.swapaxes(tiles, 1, 2).reshape(devices, CHANNELS, own_rows * PW)
    returned = lax.all_to_all(tiles, "dev", split_axis=0, concat_axis=0, tiled=True)
    early_sum = x_sum(early_sum, groups, devices)
    early_sum, late_sum, returned = lax.optimization_barrier((early_sum, late_sum, returned))
    early_sum = dev_sum(early_sum)
    total = jnp.where(early, early_sum, late_sum)
    passed = jnp.where(early, late_sum, early_sum).astype(BF16)
    total = (total + swapped(passed, "dev", half).astype(F32)).astype(BF16)
    total, rest = shared_parts(total, groups)
    low = jnp.where(core == 0, total, rest)
    high = jnp.where(core == 0, rest, total)
    total_grad = jnp.concatenate([low[: rows - size], high]).astype(F32).reshape(-1)

    returned = returned.reshape(devices, CHANNELS, own_rows, PW).astype(F32)
    wide = jnp.transpose(returned, (1, 2, 0, 3))
    centre = wide[..., MARGIN : MARGIN + breadth]
    left = wide[:, :, 1:, :MARGIN]
    right = wide[:, :, :-1, MARGIN + breadth :]
    none = ((0, 0), (0, 0))
    centre = centre + jnp.pad(left, (*none, (0, 1), (breadth - MARGIN, 0)))
    centre = centre + jnp.pad(right, (*none, (1, 0), (0, breadth - MARGIN)))
    row_grad = centre.reshape(1, CHANNELS, own_rows, width)
    feature_grad = row_grad[:, : 2 * FC]
    coarse_grad = row_grad[:, 2 * FC : 2 * FC + 4]

    new_weights, new_momentum, new_average = update(weights, momentum, average, total_grad)
    return (
        flow,
        feature_grad,
        coarse_grad,
        new_weights,
        new_momentum,
        new_average,
        new_weights.astype(BF16),
    )


def solution(mesh):
    in_specs = (
        P("grp", None, "dev", None),
        P("grp", None, "dev", None),
        P("grp", None, "dev", None),
        P("grp", "dev", None),
        P("dev"),
        P("dev"),
        P("dev"),
    )
    out_specs = (
        P("grp", None, None, "dev"),
        P("grp", None, "dev", None),
        P("grp", None, "dev", None),
        P("dev"),
        P("dev"),
        P("dev"),
        P("dev"),
    )
    return jax.shard_map(shards, mesh=mesh, in_specs=in_specs, out_specs=out_specs, check_vma=False)
```
